32 devices in a mesh: dp: 8 (over z, y), row: 2 (over x), col: 2 (over core).
Axes of the slice: x: 2, y: 2, z: 4, core: 2. Of those that a mesh axis runs over, the one named last changes fastest.
Arguments:
- tokens: bfloat16 [4096, 2048], P('dp', ('row', 'col')), may hold values from -6 to 6
- norm_first: float32 [2048], P(('row', 'col')), may hold values from 0.5 to 1.5
- mixer_in: bfloat16 [2048, 6144], P('row', 'col'), may hold values from -0.125 to 0.125
- query_weight: bfloat16 [2048, 1024], P('row', 'col'), may hold values from -0.125 to 0.125
- bc_weight: bfloat16 [2048, 512], P('row'), may hold values from -0.125 to 0.125
- step_weight: bfloat16 [2048, 48], P('row'), may hold values from -0.125 to 0.125
- kv_weight: bfloat16 [2048, 2, 256], P('row', 'col'), may hold values from -0.125 to 0.125
- conv_inner: float32 [4, 3072], P(None, ('col', 'row')), may hold values from -3 to 3
- conv_shared: float32 [4, 512], replicated, may hold values from -3 to 3
- log_rate: float32 [48], P(('col', 'row')), may hold values from -1 to 2.5
- step_bias: float32 [48], P(('col', 'row')), may hold values from -4 to -1
- skip_gain: float32 [48], P(('col', 'row')), may hold values from 0.5 to 1.5
- group_gain: float32 [3072], P(('col', 'row')), may hold values from 0.5 to 1.5
- out_weight: bfloat16 [4096, 2048], P('col', 'row'), may hold values from -1 to 1
- norm_second: float32 [2048], P(('row', 'col')), may hold values from 0.5 to 1.5
- gate_weight: bfloat16 [2048, 4096], P('row', 'col'), may hold values from -0.125 to 0.125
- up_weight: bfloat16 [2048, 4096], P('row', 'col'), may hold values from -0.125 to 0.125
- down_weight: bfloat16 [4096, 2048], P('col', 'row'), may hold values from -0.09375 to 0.09375
- cotangent: bfloat16 [4096, 2048], P('dp', ('row', 'col')), may hold values from -6 to 6
Outputs:
- layer_out: bfloat16 [4096, 2048], P('dp', ('row', 'col'))
- tokens_grad: float32 [4096, 2048], P('dp', ('row', 'col'))
- norm_first_grad: float32 [2048], P(('row', 'col', 'dp'))
- mixer_in_grad: float32 [2048, 6144], P(('row', 'dp'), 'col')
- query_weight_grad: float32 [2048, 1024], P(('row', 'dp'), 'col')
- bc_weight_grad: float32 [2048, 512], P(('row', 'dp'))
- step_weight_grad: float32 [2048, 48], P(('row', 'dp'))
- kv_weight_grad: float32 [2048, 2, 256], P(('row', 'dp'), 'col')
- conv_inner_grad: float32 [4, 3072], P(None, ('col', 'row', 'dp'))
- conv_shared_grad: float32 [4, 512], P(None, 'dp')
- log_rate_grad: float32 [48], P(('col', 'row'))
- step_bias_grad: float32 [48], P(('col', 'row'))
- skip_gain_grad: float32 [48], P(('col', 'row'))
- group_gain_grad: float32 [3072], P(('col', 'row', 'dp'))
- out_weight_grad: float32 [4096, 2048], P(('col', 'dp'), 'row')
- norm_second_grad: float32 [2048], P(('row', 'col', 'dp'))
- gate_weight_grad: float32 [2048, 4096], P(('row', 'dp'), 'col')
- up_weight_grad: float32 [2048, 4096], P(('row', 'dp'), 'col')
- down_weight_grad: float32 [4096, 2048], P(('col', 'dp'), 'row')
The draws below stay inside these ranges and needn't reach their ends.
All inputs are finite; a program needn't handle non-finite values.
Results may differ from the reference program's by a relative error of at most 0.023.
Values may be sent and summed in bfloat16 or wider, within the bound.
No kernel may reach another device: no remote copies, remote signals or barrier semaphores. Data moves between devices by JAX's collectives and lax.ppermute only.
A program may use at most 256 MiB of HBM per device.

```python
import math
import jax
import jax.numpy as jnp
from jax import lax

D = 2048
FF = 4096
HM = 48
PM = 64
NS = 256
HA = 8
KV = 2
HD = 128
KW = 4
SCAN_BLOCK = 256
SEQ = 512
MIX = 4096
TOKENS = 4096
N_DP = 8


def draw_out_weight(key, part):
    key = jax.random.fold_in(key, 11)
    baseline = jax.random.normal(key, (MIX, D), jnp.float32) / jnp.sqrt(jnp.float32(MIX))
    group_width = HM // HA * PM + HD
    position = jnp.arange(MIX) % group_width
    boost_factor = jnp.where(position >= HM // HA * PM, 10.0, 1.0)
    scaled = jnp.clip(baseline * boost_factor[:, None], -1.0, 1.0)
    return scaled.astype(jnp.bfloat16)


def block_levels(key, shape, split, low, largest):
    loudness, own = 1.0, jax.random.fold_in(key, 6)
    for dim, shards_of in split:
        steps = jnp.exp(jax.random.uniform(jax.random.fold_in(own, dim), (shards_of,), jnp.float32, low / len(split), largest / len(split)))
        loudness = loudness * jnp.repeat(steps, shape[dim] // shards_of).reshape([-1 if axis == dim else 1 for axis in range(len(shape))])
    return loudness


def noise(key, shape, width, reach, pieces=(), held_as=jnp.bfloat16):
    level = block_levels(key, shape, pieces, -0.22, 0.18) if pieces else 1.0
    drawn = jax.random.normal(key, shape, jnp.float32) * width * level
    return jnp.minimum(jnp.maximum(drawn, -reach), reach).astype(held_as)


def setup_inputs(seed: int = 0) -> dict:
    streams_of = jax.random.split(jax.random.key(seed), 20)
    tokens = noise(streams_of[0], (TOKENS, D), 1.0, 6.0, ((0, 8), (1, 4)))
    norm_first = jnp.clip(1.0 + 0.1 * jax.random.normal(streams_of[1], (D,), jnp.float32), 0.5, 1.5)
    mixer_in = noise(streams_of[2], (D, 2 * HM * PM), D ** -0.5, 0.125, ((0, 2), (1, 2)))
    query_weight = noise(streams_of[3], (D, HA * HD), D ** -0.5, 0.125, ((0, 2), (1, 2)))
    bc_weight = noise(streams_of[4], (D, 2 * NS), D ** -0.5, 0.125, ((0, 2),))
    step_weight = noise(streams_of[5], (D, HM), D ** -0.5, 0.125, ((0, 2),))
    kv_weight = noise(streams_of[6], (D, KV, 2 * HD), D ** -0.5, 0.125, ((0, 2), (1, 2)))
    conv_inner = noise(streams_of[7], (KW, HM * PM), 0.5, 3.0, ((1, 4),), jnp.float32)
    conv_shared = noise(streams_of[8], (KW, 2 * NS), 0.5, 3.0, (), jnp.float32)
    log_rate = jnp.clip(-1.0 + 3.5 * jax.random.uniform(streams_of[9], (HM,), jnp.float32) ** block_levels(streams_of[9], (HM,), ((0, 4),), -0.2, 0.2), -1.0, 2.5)
    step_bias = jnp.clip(-4.0 + 3.0 * jax.random.uniform(streams_of[10], (HM,), jnp.float32) ** block_levels(streams_of[10], (HM,), ((0, 4),), -0.2, 0.2), -4.0, -1.0)
    skip_gain = jnp.clip(0.5 + 1.0 * jax.random.uniform(streams_of[11], (HM,), jnp.float32) ** block_levels(streams_of[11], (HM,), ((0, 4),), -0.2, 0.2), 0.5, 1.5)
    group_gain = jnp.clip(1.0 + 0.1 * jax.random.normal(streams_of[12], (HM * PM,), jnp.float32), 0.5, 1.5)
    out_weight = draw_out_weight(jax.random.fold_in(streams_of[19], 71), 0)
    norm_second = jnp.clip(1.0 + 0.1 * jax.random.normal(streams_of[14], (D,), jnp.float32), 0.5, 1.5)
    gate_weight = noise(streams_of[15], (D, FF), D ** -0.5, 0.125, ((0, 2), (1, 2)))
    up_weight = noise(streams_of[16], (D, FF), D ** -0.5, 0.125, ((0, 2), (1, 2)))
    down_weight = noise(streams_of[17], (FF, D), FF ** -0.5, 0.09375, ((0, 2), (1, 2)))
    cotangent = noise(streams_of[18], (TOKENS, D), 1.0, 6.0, ((0, 8), (1, 4)))
    return dict(tokens=tokens, norm_first=norm_first, mixer_in=mixer_in, query_weight=query_weight, bc_weight=bc_weight, step_weight=step_weight, kv_weight=kv_weight, conv_inner=conv_inner, conv_shared=conv_shared, log_rate=log_rate, step_bias=step_bias, skip_gain=skip_gain, group_gain=group_gain, out_weight=out_weight, norm_second=norm_second, gate_weight=gate_weight, up_weight=up_weight, down_weight=down_weight, cotangent=cotangent)


@jax.custom_vjp
def low(v):
    return lax.optimization_barrier(v.astype(jnp.bfloat16)).astype(jnp.float32)

@jax.custom_vjp
def low_back(v):
    return v

def low_keep(v):
    return (low(v), None)

def low_pass(kept, grad):
    return (grad,)

def back_keep(v):
    return (v, None)

def back_low(kept, grad):
    return (low(grad),)
low.defvjp(low_keep, low_pass)
low_back.defvjp(back_keep, back_low)
norm_epsilon = 1e-05
rope_base = 10000.0
highest = lax.Precision.HIGHEST

def product(left_side, right_side):
    return jnp.dot(left_side, right_side, precision=highest, preferred_element_type=jnp.float32)

def causal_conv(signal, tap_weights):
    tap_count = tap_weights.shape[0]
    length = signal.shape[0]
    padded = jnp.pad(signal, ((tap_count - 1, 0), (0, 0)))
    running_sum = jnp.zeros_like(signal)
    for offset in range(tap_count):
        running_sum = running_sum + tap_weights[offset] * padded[offset:offset + length]
    return running_sum

def rotate(rotated_in):
    length = rotated_in.shape[0]
    half_width = rotated_in.shape[2] // 2
    inverse = rope_base ** (-jnp.arange(half_width, dtype=jnp.float32) * 2.0 / rotated_in.shape[2])
    angles = jnp.arange(length, dtype=jnp.float32)[:, None] * inverse[None, :]
    cosine = jnp.cos(angles)[:, None, :]
    sine_part = jnp.sin(angles)[:, None, :]
    front_part = rotated_in[..., :half_width]
    back_part = rotated_in[..., half_width:]
    return jnp.concatenate([front_part * cosine - back_part * sine_part, back_part * cosine + front_part * sine_part], axis=-1)

def mixer_core(mix_sum, query_sum, shared_sum, step_raw, pair_sum, conv_inner, conv_shared, log_rate, step_bias, skip_gain, quantize):
    length = mix_sum.shape[0]
    head_count = log_rate.shape[0]
    state_dim = shared_sum.shape[1] // 2
    head_width = mix_sum.shape[1] // (2 * head_count)
    head_pairs = mix_sum.reshape(length, head_count, 2, head_width)
    gate_part = head_pairs[:, :, 0, :]
    inner_seq = jax.nn.silu(causal_conv(head_pairs[:, :, 1, :].reshape(length, head_count * head_width), conv_inner))
    inner_seq = inner_seq.reshape(length, head_count, head_width)
    shared = jax.nn.silu(causal_conv(shared_sum, conv_shared))
    bmatrix = shared[:, :state_dim]
    cmatrix = shared[:, state_dim:]
    step_size = jax.nn.softplus(step_raw + step_bias)
    log_decay = -jnp.exp(log_rate) * step_size
    block_count = length // SCAN_BLOCK
    lower_mask = jnp.tril(jnp.ones((SCAN_BLOCK, SCAN_BLOCK), jnp.float32))[:, :, None]

    def state_block(carry_state, block_inputs):
        inner_block, basis_block, read_block, step_block, decay_block = block_inputs
        running = jnp.cumsum(decay_block, axis=0)
        gram_block = jnp.dot(read_block, basis_block.T, precision=highest)
        spread = jnp.exp(jnp.minimum(running[:, None, :] - running[None, :, :], 0.0)) * lower_mask
        mixing = gram_block[:, :, None] * spread * step_block[None, :, :]
        within = jnp.einsum('tsh,shp->thp', mixing, inner_block, precision=highest)
        carried = jnp.einsum('hpn,tn->thp', carry_state, read_block, precision=highest) * jnp.exp(running)[:, :, None]
        tail_weight = jnp.exp(running[-1][None, :] - running) * step_block
        fresh_state = jnp.einsum('sh,shp,sn->hpn', tail_weight, inner_block, basis_block, precision=highest)
        return (jnp.exp(running[-1])[:, None, None] * carry_state + fresh_state, within + carried)
    block_inputs = (inner_seq.reshape(block_count, SCAN_BLOCK, head_count, head_width), bmatrix.reshape(block_count, SCAN_BLOCK, state_dim), cmatrix.reshape(block_count, SCAN_BLOCK, state_dim), step_size.reshape(block_count, SCAN_BLOCK, head_count), log_decay.reshape(block_count, SCAN_BLOCK, head_count))
    initial = jnp.zeros((head_count, head_width, state_dim), jnp.float32)
    final_state, outputs = lax.scan(jax.checkpoint(state_block), initial, block_inputs)
    ssm_out = outputs.reshape(length, head_count, head_width) + skip_gain[None, :, None] * inner_seq
    gated_out = (ssm_out * jax.nn.silu(gate_part)).reshape(length, head_count * head_width)
    query_heads = query_sum.shape[1] // HD
    pair_heads = pair_sum.shape[1]
    queries = quantize(rotate(query_sum.reshape(length, query_heads, HD)))
    key_heads = quantize(rotate(pair_sum[:, :, :HD]))
    value_heads = quantize(pair_sum[:, :, HD:])
    key_heads = jnp.repeat(key_heads, query_heads // pair_heads, axis=1)
    value_heads = jnp.repeat(value_heads, query_heads // pair_heads, axis=1)
    block_rows = min(512, length)
    score_scale = 1.0 / math.sqrt(HD)
    positions = jnp.arange(length, dtype=jnp.int32)

    def attend(first_row):
        query_block = lax.dynamic_slice_in_dim(queries, first_row, block_rows, 0)
        scores = jnp.einsum('qhd,khd->hqk', query_block, key_heads, precision=highest) * score_scale
        query_rows = first_row + jnp.arange(block_rows, dtype=jnp.int32)
        visible = positions[None, :] <= query_rows[:, None]
        scores = jnp.where(visible[None, :, :], scores, -1e+30)
        exponent = jnp.exp(scores - lax.optimization_barrier(jnp.max(scores, axis=2, keepdims=True)))
        softmax_weights = quantize(exponent / lax.optimization_barrier(jnp.sum(exponent, axis=2, keepdims=True)))
        return jnp.einsum('hqk,khd->qhd', softmax_weights, value_heads, precision=highest)
    starts = jnp.arange(length // block_rows, dtype=jnp.int32) * block_rows
    attended = lax.map(jax.checkpoint(attend), starts).reshape(length, query_heads * HD)
    return (gated_out, attended)

def rms_scale(values_in):
    return lax.rsqrt(lax.optimization_barrier(jnp.mean(values_in * values_in, axis=-1, keepdims=True)) + norm_epsilon)

def layer(sequence, params):
    norm_first, mixer_in, query_weight, bc_weight, step_weight, kv_weight, conv_inner, conv_shared, log_rate, step_bias, skip_gain, group_gain, out_weight, norm_second, gate_weight, up_weight, down_weight = params
    length = sequence.shape[0]
    first_in = low(sequence * rms_scale(sequence) * norm_first)
    mix_sum = low_back(product(first_in, mixer_in))
    query_sum = low_back(product(first_in, query_weight))
    shared_sum = low_back(product(first_in, bc_weight))
    step_sum = low_back(product(first_in, step_weight))
    pair_sum = low_back(jnp.einsum('td,dkc->tkc', first_in, kv_weight, precision=highest))
    gated_out, attended = mixer_core(mix_sum, query_sum, shared_sum, step_sum, pair_sum, conv_inner, conv_shared, log_rate, step_bias, skip_gain, low)
    normed = gated_out * rms_scale(gated_out) * group_gain
    mixed_vec = jnp.concatenate([normed.reshape(length, HA, -1), attended.reshape(length, HA, HD)], axis=2)
    mixed_vec = low(mixed_vec.reshape(length, MIX))
    second = sequence + low_back(product(mixed_vec, out_weight))
    second_in = low(second * rms_scale(second) * norm_second)
    gate_sum = low_back(product(second_in, gate_weight))
    up_sum = low_back(product(second_in, up_weight))
    hidden = low(jax.nn.silu(gate_sum) * up_sum)
    return second + low_back(product(hidden, down_weight))

def reference(tokens, norm_first, mixer_in, query_weight, bc_weight, step_weight, kv_weight, conv_inner, conv_shared, log_rate, step_bias, skip_gain, group_gain, out_weight, norm_second, gate_weight, up_weight, down_weight, cotangent):
    params = tuple((item.astype(jnp.float32) for item in (norm_first, mixer_in, query_weight, bc_weight, step_weight, kv_weight, conv_inner, conv_shared, log_rate, step_bias, skip_gain, group_gain, out_weight, norm_second, gate_weight, up_weight, down_weight)))

    def forward(inputs, weights):

        def one_sequence(sequence):
            return layer(sequence, weights)
        stacked = inputs.reshape(N_DP, SEQ, D)
        return lax.map(jax.checkpoint(one_sequence), stacked).reshape(TOKENS, D)
    output, pullback = jax.vjp(forward, tokens.astype(jnp.float32), params)
    input_grad, grads = pullback(cotangent.astype(jnp.float32))
    return (output.astype(jnp.bfloat16), input_grad, grads[0], grads[1], grads[2], grads[3], grads[4], grads[5], grads[6], grads[7], grads[8], grads[9], grads[10], grads[11], grads[12], grads[13], grads[14], grads[15], grads[16])
```

```python
from functools import partial
import math

import jax
import jax.numpy as jnp
from jax import lax
from jax.experimental import pallas as pl
from jax.experimental.pallas import tpu as pltpu
from jax.sharding import PartitionSpec as P

D = 2048
HM = 48
PM = 64
NS = 256
HD = 128
LANES = 128
CHUNK = 128

norm_epsilon = 1e-05
rope_base = 10000.0
highest = lax.Precision.HIGHEST
f32 = jnp.float32
bf16 = jnp.bfloat16
VMEM_LIMIT = 56 * 1024 * 1024


def product(left_side, right_side):
    return jnp.dot(left_side, right_side, preferred_element_type=f32)


def product_back(left_side, right_side):
    return lax.dot_general(
        left_side, right_side, (((1,), (1,)), ((), ())), preferred_element_type=f32
    )


def outer_sum(left_side, right_side):
    return lax.dot_general(
        left_side, right_side, (((0,), (0,)), ((), ())), preferred_element_type=f32
    )


def swap(values_in, axis):
    return lax.ppermute(values_in, axis, [(0, 1), (1, 0)])


def in_order(own, other, place, axis):
    return jnp.concatenate(
        [jnp.where(place == 0, own, other), jnp.where(place == 0, other, own)], axis=axis
    )


def part_of(values_in, place, axis):
    size = values_in.shape[axis] // 2
    return lax.dynamic_slice_in_dim(values_in, place * size, size, axis)


def rows_total(values_in):
    values_in = values_in + swap(values_in, "col")
    return values_in + swap(values_in, "row")


def dp_bits():
    bits, bit = [], 1
    while bit < lax.axis_size("dp"):
        bits.append(bit)
        bit *= 2
    return bits


def swap_dp(values_in, bit):
    return lax.ppermute(values_in, "dp", [(i, i ^ bit) for i in range(lax.axis_size("dp"))])


def scatter_dp(grads, last_first=False):
    bits = dp_bits()
    count = lax.axis_size("dp")
    me = lax.axis_index("dp")
    rest = (grads.shape[0] // count,) + grads.shape[1:]
    parts = grads.reshape((2,) * len(bits) + rest)
    left = bits[::-1]
    order = bits[1:] + bits[:1] if last_first else bits
    for bit in order:
        axis = left.index(bit)
        mine = (me // bit) % 2
        send = lax.dynamic_index_in_dim(parts, 1 - mine, axis, keepdims=False)
        keep = lax.dynamic_index_in_dim(parts, mine, axis, keepdims=False)
        parts = keep.astype(f32) + swap_dp(send, bit).astype(f32)
        left.pop(axis)
        if left:
            parts = parts.astype(bf16)
    return parts


def sigmoid(values_in):
    return 1.0 / (1.0 + jnp.exp(-values_in))


def softplus(values_in):
    return jnp.maximum(values_in, 0.0) + jnp.log1p(jnp.exp(-jnp.abs(values_in)))


def low_lanes():
    return lax.broadcasted_iota(jnp.int32, (1, LANES), 1) < PM


def pair_columns(values_in, pair):
    return jnp.where(
        low_lanes(), values_in[:, 2 * pair : 2 * pair + 1], values_in[:, 2 * pair + 1 : 2 * pair + 2]
    )


def shift_down(values_in, count):
    if count == 0:
        return values_in
    rows = lax.broadcasted_iota(jnp.int32, values_in.shape, 0)
    return jnp.where(rows >= count, pltpu.roll(values_in, count, 0), 0.0)


def shift_up(values_in, count):
    if count == 0:
        return values_in
    length = values_in.shape[0]
    rows = lax.broadcasted_iota(jnp.int32, values_in.shape, 0)
    return jnp.where(rows < length - count, pltpu.roll(values_in, length - count, 0), 0.0)


def conv(values_in, taps):
    count = taps.shape[0]
    total = values_in * taps[count - 1 : count, :]
    for tap in range(count - 1):
        total = total + taps[tap : tap + 1, :] * shift_down(values_in, count - 1 - tap)
    return total


def conv_back(grad, values_in, taps):
    count = taps.shape[0]
    total = grad * taps[count - 1 : count, :]
    for tap in range(count - 1):
        total = total + taps[tap : tap + 1, :] * shift_up(grad, count - 1 - tap)
    tap_grads = [
        jnp.sum(grad * shift_down(values_in, count - 1 - tap), axis=0, keepdims=True)
        for tap in range(count)
    ]
    return total, tap_grads


def stacked_pair(values_in):
    low = low_lanes()
    return jnp.concatenate(
        [jnp.where(low, values_in, 0.0), jnp.where(low, 0.0, values_in)], axis=0
    ).astype(bf16)


def lower_mask():
    rows = lax.broadcasted_iota(jnp.int32, (CHUNK, CHUNK), 0)
    columns = lax.broadcasted_iota(jnp.int32, (CHUNK, CHUNK), 1)
    return (rows >= columns).astype(f32)


def mixer_forward_kernel(
    own_ref,
    other_ref,
    factor_ref,
    shared_ref,
    step_ref,
    conv_inner_ref,
    conv_shared_ref,
    head_ref,
    skip_ref,
    gain_ref,
    gained_ref,
    square_ref,
    mix_ref,
    ssm_ref,
    states_ref,
    inner_buf,
    gate_buf,
    maps_buf,
    step_buf,
    decay_buf,
    weighted_buf,
    state_buf,
):
    pairs = gained_ref.shape[1] // LANES
    length = own_ref.shape[0]
    low = low_lanes()
    factor = factor_ref[...]
    for pair in range(pairs):
        first = slice(2 * pair * LANES, (2 * pair + 1) * LANES)
        second = slice((2 * pair + 1) * LANES, (2 * pair + 2) * LANES)
        own = slice(pair * LANES, (pair + 1) * LANES)
        head_a = (own_ref[:, first] + other_ref[:, first].astype(f32)) * factor
        head_b = (own_ref[:, second] + other_ref[:, second].astype(f32)) * factor
        mix_ref[:, first] = head_a
        mix_ref[:, second] = head_b
        taken = jnp.where(low, pltpu.roll(head_a, PM, 1), head_b)
        gate_buf[:, own] = jnp.where(low, head_a, pltpu.roll(head_b, PM, 1))
        taken = conv(taken, conv_inner_ref[:, own])
        inner_buf[:, own] = taken * sigmoid(taken)
    for block in range(shared_ref.shape[1] // LANES):
        own = slice(block * LANES, (block + 1) * LANES)
        taken = conv(shared_ref[:, own], conv_shared_ref[:, own])
        maps_buf[:, own] = (taken * sigmoid(taken)).astype(bf16)
    steps = softplus(step_ref[...] + head_ref[1:2, :])
    step_buf[...] = steps
    decay_buf[...] = -jnp.exp(head_ref[0:1, :]) * steps
    state_buf[...] = jnp.zeros_like(state_buf)
    mask = lower_mask()

    def chunk(index, carry):
        rows = pl.ds(pl.multiple_of(index * CHUNK, CHUNK), CHUNK)
        running = jnp.dot(mask, decay_buf[rows, :], precision=highest, preferred_element_type=f32)
        running_t = running.T
        step = step_buf[rows, :]
        step_t = step.T
        last = running[CHUNK - 1 : CHUNK, :]
        grown = jnp.exp(running)
        tail = jnp.exp(last - running) * step
        grown_last = jnp.exp(last)
        basis = maps_buf[rows, 0:NS]
        read = maps_buf[rows, NS : 2 * NS]
        gram = product_back(read, basis)
        state_low = state_buf[...].astype(bf16)
        states_ref[pl.ds(pl.multiple_of(index * NS, NS), NS), :] = state_low
        carried = product(read, state_low)
        square = jnp.zeros((CHUNK, 1), f32)
        for pair in range(pairs):
            own = slice(pair * LANES, (pair + 1) * LANES)
            inner = inner_buf[rows, own]
            mixing = []
            for head in (2 * pair, 2 * pair + 1):
                spread = jnp.exp(
                    jnp.minimum(running[:, head : head + 1] - running_t[head : head + 1, :], 0.0)
                )
                mixing.append(
                    (gram * spread * mask * step_t[head : head + 1, :]).astype(bf16)
                )
            ssm = product(jnp.concatenate(mixing, axis=1), stacked_pair(inner))
            ssm = ssm + pair_columns(grown, pair) * carried[:, own] + skip_ref[:, own] * inner
            ssm_ref[rows, own] = ssm
            weighted_buf[:, own] = (pair_columns(tail, pair) * inner).astype(bf16)
            gate = gate_buf[rows, own]
            gated = ssm * gate * sigmoid(gate)
            square = square + jnp.sum(gated * gated, axis=1, keepdims=True)
            gained_ref[rows, own] = (gated * gain_ref[:, own]).astype(bf16)
        square_ref[rows, :] = square
        fresh = outer_sum(basis, weighted_buf[...])
        for pair in range(pairs):
            own = slice(pair * LANES, (pair + 1) * LANES)
            state_buf[:, own] = (
                pair_columns(grown_last, pair) * state_buf[:, own] + fresh[:, own]
            )
        return carry

    lax.fori_loop(0, length // CHUNK, chunk, 0)


def mixer_backward_kernel(
    mix_ref,
    ssm_ref,
    states_ref,
    shared_ref,
    step_ref,
    conv_inner_ref,
    conv_shared_ref,
    head_ref,
    skip_ref,
    gain_ref,
    lanes_ref,
    grad_ref,
    group_factor_ref,
    group_scale_ref,
    factor_ref,
    mix_grad_ref,
    shared_grad_ref,
    step_grad_ref,
    inner_taps_ref,
    shared_taps_ref,
    head_grad_ref,
    wide_grad_ref,
    total_ref,
    taken_buf,
    inner_buf,
    maps_buf,
    step_buf,
    decay_buf,
    weighted_buf,
    grown_buf,
    inner_grad_buf,
    maps_grad_buf,
    sums_buf,
    state_grad_buf,
):
    pairs = ssm_ref.shape[1] // LANES
    length = ssm_ref.shape[0]
    group_pairs = pairs // (grad_ref.shape[1] // (pairs * LANES // 2 + HD))
    low = low_lanes()
    for pair in range(pairs):
        first = slice(2 * pair * LANES, (2 * pair + 1) * LANES)
        second = slice((2 * pair + 1) * LANES, (2 * pair + 2) * LANES)
        own = slice(pair * LANES, (pair + 1) * LANES)
        taken = jnp.where(low, pltpu.roll(mix_ref[:, first], PM, 1), mix_ref[:, second])
        taken_buf[:, own] = taken
        taken = conv(taken, conv_inner_ref[:, own])
        inner_buf[:, own] = taken * sigmoid(taken)
    for block in range(shared_ref.shape[1] // LANES):
        own = slice(block * LANES, (block + 1) * LANES)
        taken = conv(shared_ref[:, own], conv_shared_ref[:, own])
        maps_buf[:, own] = (taken * sigmoid(taken)).astype(bf16)
    shifted = step_ref[...] + head_ref[1:2, :]
    steps = softplus(shifted)
    rate = -jnp.exp(head_ref[0:1, :])
    step_buf[...] = steps
    decay_buf[...] = rate * steps
    state_grad_buf[...] = jnp.zeros_like(state_grad_buf)
    head_grad_ref[...] = jnp.zeros_like(head_grad_ref)
    wide_grad_ref[...] = jnp.zeros_like(wide_grad_ref)
    mask = lower_mask()
    chunks = length // CHUNK
    lane_index = lax.broadcasted_iota(jnp.int32, (1, LANES), 1)

    def chunk(turn, carry):
        index = chunks - 1 - turn
        rows = pl.ds(pl.multiple_of(index * CHUNK, CHUNK), CHUNK)
        running = jnp.dot(mask, decay_buf[rows, :], precision=highest, preferred_element_type=f32)
        running_t = running.T
        step = step_buf[rows, :]
        step_t = step.T
        last = running[CHUNK - 1 : CHUNK, :]
        grown = jnp.exp(running)
        fading = jnp.exp(last - running)
        grown_last = jnp.exp(last)
        basis = maps_buf[rows, 0:NS]
        read = maps_buf[rows, NS : 2 * NS]
        gram = product_back(read, basis)
        state_low = states_ref[pl.ds(pl.multiple_of(index * NS, NS), NS), :]
        carried = product(read, state_low)
        state_grad_low = state_grad_buf[...].astype(bf16)
        weighted_grad = product(basis, state_grad_low)
        gram_grad = jnp.zeros((CHUNK, CHUNK), f32)
        decay_grad = jnp.zeros((CHUNK, LANES), f32)
        column_grads = []
        total = jnp.zeros((CHUNK, 1), f32)
        group_factor = group_factor_ref[rows, :]
        group_scale = group_scale_ref[rows, :]
        factor = factor_ref[rows, :]
        for pair in range(pairs):
            first = slice(2 * pair * LANES, (2 * pair + 1) * LANES)
            second = slice((2 * pair + 1) * LANES, (2 * pair + 2) * LANES)
            own = slice(pair * LANES, (pair + 1) * LANES)
            place = pair * LANES + (pair // group_pairs) * HD
            incoming = grad_ref[rows, place : place + LANES]
            head_a = mix_ref[rows, first]
            head_b = mix_ref[rows, second]
            gate = jnp.where(low, head_a, pltpu.roll(head_b, PM, 1))
            gate_sigmoid = sigmoid(gate)
            gate_act = gate * gate_sigmoid
            ssm = ssm_ref[rows, own]
            gated = ssm * gate_act
            wide_grad_ref[0:1, own] += jnp.sum(
                incoming * gated * group_factor, axis=0, keepdims=True
            )
            gated_grad = group_factor * gain_ref[:, own] * incoming - gated * group_scale
            gate_grad = gated_grad * ssm * gate_sigmoid * (1.0 + gate * (1.0 - gate_sigmoid))
            ssm_grad = gated_grad * gate_act
            inner = inner_buf[rows, own]
            wide_grad_ref[1:2, own] += jnp.sum(ssm_grad * inner, axis=0, keepdims=True)
            gate_b = pltpu.roll(gate_grad, PM, 1)
            total = total + jnp.sum(gate_grad * gate, axis=1, keepdims=True)
            mix_grad_ref[rows, first] = jnp.where(low, gate_grad * factor, 0.0).astype(bf16)
            mix_grad_ref[rows, second] = jnp.where(low, gate_b * factor, 0.0).astype(bf16)
            grad_low = ssm_grad.astype(bf16)
            mixing_grad = product_back(grad_low, stacked_pair(inner))
            spreads = []
            for side, head in enumerate((2 * pair, 2 * pair + 1)):
                spread = mask * jnp.exp(
                    jnp.minimum(running[:, head : head + 1] - running_t[head : head + 1, :], 0.0)
                )
                step_row = step_t[head : head + 1, :]
                spread_gram = gram * spread
                spreads.append(spread_gram.astype(bf16))
                own_grad = mixing_grad[:, side * CHUNK : (side + 1) * CHUNK] * step_row
                gram_grad = gram_grad + own_grad * spread
                moved = own_grad * spread_gram
                decay_grad = decay_grad + jnp.where(
                    lane_index == head, jnp.sum(moved, axis=1, keepdims=True), 0.0
                )
                column_grads.append(jnp.sum(moved, axis=0, keepdims=True))
            within = outer_sum(jnp.concatenate(spreads, axis=0), stacked_pair(ssm_grad))
            fading_grad = pair_columns(fading, pair) * weighted_grad[:, own]
            spread_grad = within + fading_grad
            step_wide = pair_columns(step, pair)
            inner_grad_buf[rows, own] = step_wide * spread_grad + skip_ref[:, own] * ssm_grad
            grown_grad = pair_columns(grown, pair) * ssm_grad
            grown_buf[:, own] = grown_grad.astype(bf16)
            weighted_buf[:, own] = (pair_columns(fading, pair) * step_wide * inner).astype(bf16)
            sums_buf[0:CHUNK, own] = (inner * spread_grad).astype(bf16)
            sums_buf[CHUNK : 2 * CHUNK, own] = (inner * fading_grad * step_wide).astype(bf16)
            sums_buf[2 * CHUNK : 3 * CHUNK, own] = (grown_grad * carried[:, own]).astype(bf16)
        head_sums = product(sums_buf[...], lanes_ref[...])
        step_part = head_sums[0:CHUNK, :]
        fading_part = head_sums[CHUNK : 2 * CHUNK, :]
        grown_part = head_sums[2 * CHUNK : 3 * CHUNK, :]
        fill = jnp.zeros((CHUNK - len(column_grads), CHUNK), f32)
        column_grad = jnp.concatenate(column_grads + [fill], axis=0).T
        decay_grad = decay_grad - column_grad + grown_part - fading_part
        state_part = jnp.zeros((1, LANES), f32)
        grown_low = grown_buf[...]
        fresh = outer_sum(read, grown_low)
        for pair in range(pairs):
            own = slice(pair * LANES, (pair + 1) * LANES)
            state_grad = state_grad_buf[:, own]
            held = jnp.sum(state_grad * state_low[:, own].astype(f32), axis=0, keepdims=True)
            for side, head in enumerate((2 * pair, 2 * pair + 1)):
                kept = jnp.where(low if side == 0 else jnp.logical_not(low), held, 0.0)
                state_part = state_part + jnp.where(
                    lane_index == head, jnp.sum(kept, axis=1, keepdims=True), 0.0
                )
            state_grad_buf[:, own] = pair_columns(grown_last, pair) * state_grad + fresh[:, own]
        last_grad = jnp.sum(fading_part, axis=0, keepdims=True) + grown_last * state_part
        decay_sum = (
            lax.dot_general(
                mask,
                decay_grad,
                (((0,), (0,)), ((), ())),
                precision=highest,
                preferred_element_type=f32,
            )
            + last_grad
        )
        raw_shift = step_ref[rows, :] + head_ref[1:2, :]
        raw_grad = (step_part + decay_sum * rate) * sigmoid(raw_shift)
        head_grad_ref[0:1, :] += jnp.sum(decay_sum * decay_buf[rows, :], axis=0, keepdims=True)
        head_grad_ref[1:2, :] += jnp.sum(raw_grad, axis=0, keepdims=True)
        step_grad_ref[rows, :] = (raw_grad * factor).astype(bf16)
        total = total + jnp.sum(raw_grad * step_ref[rows, :], axis=1, keepdims=True)
        total_ref[rows, :] = total
        gram_low = gram_grad.astype(bf16)
        maps_grad_buf[rows, 0:NS] = outer_sum(gram_low, read) + product_back(
            weighted_buf[...], state_grad_low
        )
        maps_grad_buf[rows, NS : 2 * NS] = product(gram_low, basis) + product_back(
            grown_low, state_low
        )
        return carry

    lax.fori_loop(0, chunks, chunk, 0)
    factor = factor_ref[...]
    total = total_ref[...]
    for pair in range(pairs):
        first = slice(2 * pair * LANES, (2 * pair + 1) * LANES)
        second = slice((2 * pair + 1) * LANES, (2 * pair + 2) * LANES)
        own = slice(pair * LANES, (pair + 1) * LANES)
        taken = taken_buf[:, own]
        taps = conv_inner_ref[:, own]
        before = conv(taken, taps)
        before_sigmoid = sigmoid(before)
        grad = inner_grad_buf[:, own] * before_sigmoid * (1.0 + before * (1.0 - before_sigmoid))
        grad, tap_grads = conv_back(grad, taken, taps)
        for tap, tap_grad in enumerate(tap_grads):
            inner_taps_ref[tap : tap + 1, own] = tap_grad
        total = total + jnp.sum(grad * taken, axis=1, keepdims=True)
        grad = grad * factor
        low_a = mix_grad_ref[:, first].astype(f32)
        low_b = mix_grad_ref[:, second].astype(f32)
        mix_grad_ref[:, first] = jnp.where(low, low_a, pltpu.roll(grad, PM, 1)).astype(bf16)
        mix_grad_ref[:, second] = jnp.where(low, low_b, grad).astype(bf16)
    for block in range(shared_ref.shape[1] // LANES):
        own = slice(block * LANES, (block + 1) * LANES)
        taken = shared_ref[:, own]
        taps = conv_shared_ref[:, own]
        before = conv(taken, taps)
        before_sigmoid = sigmoid(before)
        grad = maps_grad_buf[:, own] * before_sigmoid * (1.0 + before * (1.0 - before_sigmoid))
        grad, tap_grads = conv_back(grad, taken, taps)
        for tap, tap_grad in enumerate(tap_grads):
            shared_taps_ref[tap : tap + 1, own] = tap_grad
        total = total + jnp.sum(grad * taken, axis=1, keepdims=True)
        shared_grad_ref[:, own] = (grad * factor).astype(bf16)
    total_ref[...] = total


def call(kernel, outs, scratch, flops, *operands):
    moved = sum(math.prod(item.shape) * item.dtype.itemsize for item in operands)
    moved += sum(math.prod(item.shape) * item.dtype.itemsize for item in outs)
    return pl.pallas_call(
        kernel,
        out_shape=outs,
        in_specs=[pl.BlockSpec(memory_space=pltpu.VMEM)] * len(operands),
        out_specs=[pl.BlockSpec(memory_space=pltpu.VMEM)] * len(outs),
        scratch_shapes=scratch,
        compiler_params=pltpu.CompilerParams(vmem_limit_bytes=VMEM_LIMIT),
        cost_estimate=pl.CostEstimate(flops=flops, bytes_accessed=moved, transcendentals=0),
    )(*operands)


def shape(dims, dtype=f32):
    return jax.ShapeDtypeStruct(dims, dtype)


def mixer_forward(own, other, factor, shared, step, taps, shared_taps, heads, skip, gain):
    length, width = own.shape
    channels = width // 2
    chunks = length // CHUNK
    return call(
        mixer_forward_kernel,
        [
            shape((length, channels), bf16),
            shape((length, 1)),
            shape((length, width)),
            shape((length, channels)),
            shape((chunks * NS, channels), bf16),
        ],
        [
            pltpu.VMEM((length, channels), f32),
            pltpu.VMEM((length, channels), f32),
            pltpu.VMEM((length, 2 * NS), bf16),
            pltpu.VMEM((length, LANES), f32),
            pltpu.VMEM((length, LANES), f32),
            pltpu.VMEM((CHUNK, channels), bf16),
            pltpu.VMEM((NS, channels), f32),
        ],
        8 * 10**9,
        own, other, factor, shared, step, taps, shared_taps, heads, skip, gain,
    )


def mixer_backward(
    mix, ssm, states, shared, step, taps, shared_taps, heads, skip, gain, lanes, grad,
    group_factor, group_scale, factor,
):
    length, width = mix.shape
    channels = width // 2
    return call(
        mixer_backward_kernel,
        [
            shape((length, width), bf16),
            shape((length, 2 * NS), bf16),
            shape((length, LANES), bf16),
            shape((taps.shape[0], channels)),
            shape((taps.shape[0], 2 * NS)),
            shape((8, LANES)),
            shape((8, channels)),
            shape((length, 1)),
        ],
        [
            pltpu.VMEM((length, channels), f32),
            pltpu.VMEM((length, channels), f32),
            pltpu.VMEM((length, 2 * NS), bf16),
            pltpu.VMEM((length, LANES), f32),
            pltpu.VMEM((length, LANES), f32),
            pltpu.VMEM((CHUNK, channels), bf16),
            pltpu.VMEM((CHUNK, channels), bf16),
            pltpu.VMEM((length, channels), f32),
            pltpu.VMEM((length, 2 * NS), f32),
            pltpu.VMEM((3 * CHUNK, channels), bf16),
            pltpu.VMEM((NS, channels), f32),
        ],
        16 * 10**9,
        mix, ssm, states, shared, step, taps, shared_taps, heads, skip, gain, lanes, grad,
        group_factor, group_scale, factor,
    )


def rotated(values_in, cosine, sine):
    return values_in * cosine + pltpu.roll(values_in, HD // 2, 1) * sine


def rotated_back(grad, cosine, sine):
    return grad * cosine + pltpu.roll(grad * sine, HD // 2, 1)


def attention_forward_kernel(query_ref, pair_ref, cosine_ref, sine_ref, out_ref):
    length = query_ref.shape[0]
    scale = 1.0 / math.sqrt(HD)
    block = min(256, length)
    keys = rotated(pair_ref[:, :HD], cosine_ref[...], sine_ref[...]).astype(bf16)
    vals = pair_ref[:, HD:].astype(bf16)
    for head in range(query_ref.shape[1] // HD):
        lanes = slice(head * HD, (head + 1) * HD)
        queries = rotated(query_ref[:, lanes], cosine_ref[...], sine_ref[...]).astype(bf16)
        for start in range(0, length, block):
            end = start + block
            scores = product_back(queries[start:end], keys[:end]) * scale
            rows = start + lax.broadcasted_iota(jnp.int32, (block, end), 0)
            columns = lax.broadcasted_iota(jnp.int32, (block, end), 1)
            scores = jnp.where(columns <= rows, scores, -1e30)
            exponent = jnp.exp(scores - jnp.max(scores, axis=1, keepdims=True))
            probs = exponent * (1.0 / jnp.sum(exponent, axis=1, keepdims=True))
            out_ref[start:end, lanes] = product(probs.astype(bf16), vals[:end]).astype(bf16)


def attention_backward_kernel(
    query_ref, pair_ref, cosine_ref, sine_ref, grad_ref, factor_ref,
    query_grad_ref, pair_grad_ref, total_ref, key_buf, val_buf,
):
    length = query_ref.shape[0]
    scale = 1.0 / math.sqrt(HD)
    block = min(256, length)
    cosine, sine = cosine_ref[...], sine_ref[...]
    keys = rotated(pair_ref[:, :HD], cosine, sine).astype(bf16)
    vals = pair_ref[:, HD:].astype(bf16)
    heads = query_ref.shape[1] // HD
    group = grad_ref.shape[1] // heads
    key_buf[...] = jnp.zeros_like(key_buf)
    val_buf[...] = jnp.zeros_like(val_buf)
    for head in range(heads):
        lanes = slice(head * HD, (head + 1) * HD)
        queries = rotated(query_ref[:, lanes], cosine, sine).astype(bf16)
        incoming = grad_ref[:, (head + 1) * group - HD : (head + 1) * group].astype(bf16)
        for start in range(0, length, block):
            end = start + block
            scores = product_back(queries[start:end], keys[:end]) * scale
            rows = start + lax.broadcasted_iota(jnp.int32, (block, end), 0)
            columns = lax.broadcasted_iota(jnp.int32, (block, end), 1)
            scores = jnp.where(columns <= rows, scores, -1e30)
            exponent = jnp.exp(scores - jnp.max(scores, axis=1, keepdims=True))
            probs = exponent * (1.0 / jnp.sum(exponent, axis=1, keepdims=True))
            grad_low = incoming[start:end]
            val_buf[:end, :] += outer_sum(probs.astype(bf16), grad_low)
            probs_grad = product_back(grad_low, vals[:end])
            inner = jnp.sum(probs * probs_grad, axis=1, keepdims=True)
            scores_grad = (probs * (probs_grad - inner) * scale).astype(bf16)
            query_grad = rotated_back(
                product(scores_grad, keys[:end]), cosine[start:end], sine[start:end]
            )
            key_buf[:end, :] += outer_sum(scores_grad, queries[start:end])
            taken = query_ref[start:end, lanes]
            part = jnp.sum(query_grad * taken, axis=1, keepdims=True)
            if head == 0:
                total_ref[start:end, :] = part
            else:
                total_ref[start:end, :] += part
            query_grad_ref[start:end, lanes] = (query_grad * factor_ref[start:end, :]).astype(bf16)
    key_grad = rotated_back(key_buf[...], cosine, sine)
    val_grad = val_buf[...]
    total_ref[...] += jnp.sum(
        key_grad * pair_ref[:, :HD] + val_grad * pair_ref[:, HD:], axis=1, keepdims=True
    )
    pair_grad_ref[:, :HD] = (key_grad * factor_ref[...]).astype(bf16)
    pair_grad_ref[:, HD:] = (val_grad * factor_ref[...]).astype(bf16)


def attention_forward(query, pair, cosine, sine):
    return call(
        attention_forward_kernel, [shape(query.shape, bf16)], [], 4 * 10**9,
        query, pair, cosine, sine,
    )[0]


def attention_backward(query, pair, cosine, sine, grad, factor):
    length = query.shape[0]
    return call(
        attention_backward_kernel,
        [shape(query.shape, bf16), shape(pair.shape, bf16), shape((length, 1))],
        [pltpu.VMEM((length, HD), f32), pltpu.VMEM((length, HD), f32)],
        8 * 10**9,
        query, pair, cosine, sine, grad, factor,
    )


def rope_tables(length):
    half = HD // 2
    inverse = rope_base ** (-jnp.arange(half, dtype=f32) * 2.0 / HD)
    angles = jnp.arange(length, dtype=f32)[:, None] * inverse[None, :]
    cosine, sine = jnp.cos(angles), jnp.sin(angles)
    return jnp.concatenate([cosine, cosine], axis=1), jnp.concatenate([-sine, sine], axis=1)


def to_lanes(values_in):
    return jnp.pad(values_in, ((0, 0), (0, LANES - values_in.shape[1])))


def local(
    tokens,
    norm_first,
    mixer_in,
    query_weight,
    bc_weight,
    step_weight,
    kv_weight,
    conv_inner,
    conv_shared,
    log_rate,
    step_bias,
    skip_gain,
    group_gain,
    out_weight,
    norm_second,
    gate_weight,
    up_weight,
    down_weight,
    cotangent,
):
    length = tokens.shape[0]
    row = lax.axis_index("row")
    col = lax.axis_index("col")
    quarter = col * 2 + row
    head_count = log_rate.shape[0]
    channels = group_gain.shape[0]
    kv_flat = kv_weight.reshape(kv_weight.shape[0], -1)
    residual = tokens.astype(f32)

    first_own = (residual * norm_first).astype(bf16)
    first_half = in_order(first_own, swap(first_own, "col"), col, 1)
    first_factor = lax.rsqrt(rows_total(jnp.sum(residual * residual, axis=1)) / D + norm_epsilon)
    first_column = first_factor[:, None]

    query_own = product(first_half, part_of(query_weight, row, 1))
    query_out = product(first_half, part_of(query_weight, 1 - row, 1)).astype(bf16)
    pair_own = product(first_half, kv_flat)
    shared_own = product(first_half, bc_weight)
    step_own = product(first_half, step_weight)
    early = swap(
        jnp.concatenate(
            [query_out, pair_own.astype(bf16), shared_own.astype(bf16), to_lanes(step_own).astype(bf16)],
            axis=1,
        ),
        "row",
    )
    query_width = query_own.shape[1]
    pair_width = pair_own.shape[1]
    shared_width = shared_own.shape[1]
    mix_out = product(first_half, part_of(mixer_in, 1 - row, 1)).astype(bf16)
    mix_other = swap(mix_out, "row")
    mix_own = product(first_half, part_of(mixer_in, row, 1))
    query_sum = (query_own + early[:, :query_width].astype(f32)) * first_column
    place = query_width
    pair_sum = (pair_own + early[:, place : place + pair_width].astype(f32)) * first_column
    place += pair_width
    shared_sum = (shared_own + early[:, place : place + shared_width].astype(f32)) * first_column
    place += shared_width
    step_sum = (
        step_own + early[:, place : place + step_own.shape[1]].astype(f32)
    ) * first_column
    step_sum = to_lanes(lax.dynamic_slice_in_dim(step_sum, quarter * head_count, head_count, 1))

    cot_half = in_order(cotangent, swap(cotangent, "col"), col, 1)
    hidden_back = product_back(cot_half, part_of(down_weight, 1 - row, 0)).astype(bf16)
    hidden_back = swap(hidden_back, "row")
    hidden_back_own = product_back(cot_half, part_of(down_weight, row, 0))

    cosine, sine = rope_tables(length)
    attended = attention_forward(query_sum, pair_sum, cosine, sine)
    heads = to_lanes(jnp.stack([log_rate, step_bias] + [jnp.zeros_like(log_rate)] * 6))
    skip_wide = jnp.repeat(skip_gain, PM)[None, :]
    gain_wide = group_gain[None, :]
    gained, square, mix_sum, ssm, states = mixer_forward(
        mix_own, mix_other, first_column, shared_sum, step_sum, conv_inner, conv_shared,
        heads, skip_wide, gain_wide,
    )
    group_factor = lax.rsqrt(rows_total(square[:, 0]) / (HM * PM) + norm_epsilon)
    groups = attended.shape[1] // HD
    normed = (gained.astype(f32) * group_factor[:, None]).astype(bf16)
    mixed = jnp.concatenate(
        [normed.reshape(length, groups, -1), attended.reshape(length, groups, HD)], axis=2
    ).reshape(length, -1)
    mixed_half = in_order(mixed, swap(mixed, "row"), row, 1)

    out_partial = product(mixed_half, out_weight)
    second = (
        residual
        + part_of(out_partial, col, 1)
        + swap(part_of(out_partial, 1 - col, 1).astype(bf16), "col").astype(f32)
    )
    second_own = (second * norm_second).astype(bf16)
    second_half = in_order(second_own, swap(second_own, "col"), col, 1)
    second_factor = lax.rsqrt(rows_total(jnp.sum(second * second, axis=1)) / D + norm_epsilon)
    second_column = second_factor[:, None]
    gate_other = swap(product(second_half, part_of(gate_weight, 1 - row, 1)).astype(bf16), "row")
    up_other = swap(product(second_half, part_of(up_weight, 1 - row, 1)).astype(bf16), "row")
    gate_sum = (
        product(second_half, part_of(gate_weight, row, 1)) + gate_other.astype(f32)
    ) * second_column
    up_sum = (
        product(second_half, part_of(up_weight, row, 1)) + up_other.astype(f32)
    ) * second_column
    gate_sigmoid = jax.nn.sigmoid(gate_sum)
    gate_act = gate_sum * gate_sigmoid
    hidden_grad = hidden_back_own + hidden_back.astype(f32)
    gate_grad = hidden_grad * up_sum * gate_sigmoid * (1.0 + gate_sum * (1.0 - gate_sigmoid))
    up_grad = hidden_grad * gate_act
    second_total = rows_total(jnp.sum(gate_grad * gate_sum + up_grad * up_sum, axis=1))
    gate_low = (gate_grad * second_column).astype(bf16)
    up_low = (up_grad * second_column).astype(bf16)
    gate_half = in_order(gate_low, swap(gate_low, "row"), row, 1)
    up_half = in_order(up_low, swap(up_low, "row"), row, 1)
    second_in_partial = product_back(gate_half, gate_weight) + product_back(up_half, up_weight)
    second_in_grad = part_of(second_in_partial, col, 1) + swap(
        part_of(second_in_partial, 1 - col, 1).astype(bf16), "col"
    ).astype(f32)
    cot_own = cotangent.astype(f32)
    second_grad = (
        cot_own
        + norm_second * second_in_grad
        - second * (second_factor**2 * second_total / D)[:, None]
    )
    norm_second_grad = jnp.sum(second_in_grad * second, axis=0)

    branch_own = second_grad.astype(bf16)
    branch_half = in_order(branch_own, swap(branch_own, "col"), col, 1)
    mixed_back = swap(
        product_back(branch_half, part_of(out_weight, 1 - row, 0)).astype(bf16), "row"
    )
    mixed_grad = product_back(branch_half, part_of(out_weight, row, 0)) + mixed_back.astype(f32)

    hidden = (gate_act * up_sum).astype(bf16)
    hidden_half = in_order(hidden, swap(hidden, "row"), row, 1)
    layer_partial = product(hidden_half, down_weight)
    layer_out = (
        second
        + part_of(layer_partial, col, 1)
        + swap(part_of(layer_partial, 1 - col, 1).astype(bf16), "col").astype(f32)
    ).astype(bf16)

    gate_weight_grad = scatter_dp(outer_sum(second_half, gate_half).astype(bf16))
    up_weight_grad = scatter_dp(outer_sum(second_half, up_half).astype(bf16))
    down_weight_grad = scatter_dp(outer_sum(hidden_half, cot_half).astype(bf16))
    out_weight_grad = scatter_dp(outer_sum(mixed_half, branch_half).astype(bf16), True)

    normed_grad = mixed_grad.reshape(length, groups, -1)[:, :, : channels // groups]
    group_total = rows_total(
        jnp.sum(
            normed_grad * gained.astype(f32).reshape(length, groups, -1), axis=(1, 2)
        )
    )
    group_scale = group_factor**3 * group_total / (HM * PM)
    lanes = (
        jnp.arange(channels)[:, None] // PM == jnp.arange(LANES)[None, :]
    ).astype(bf16)
    query_grad, pair_grad, attention_total = attention_backward(
        query_sum, pair_sum, cosine, sine, mixed_grad, first_column
    )
    (
        mix_grad,
        shared_grad,
        step_grad,
        conv_inner_grad,
        conv_shared_part,
        head_grads,
        wide_grads,
        mixer_total,
    ) = mixer_backward(
        mix_sum, ssm, states, shared_sum, step_sum, conv_inner, conv_shared, heads, skip_wide,
        gain_wide, lanes, mixed_grad, group_factor[:, None], group_scale[:, None], first_column,
    )
    first_total = rows_total((attention_total + mixer_total)[:, 0])

    mix_half = in_order(mix_grad, swap(mix_grad, "row"), row, 1)
    query_half = in_order(query_grad, swap(query_grad, "row"), row, 1)
    shared_sums = shared_grad.astype(f32) + swap(shared_grad, "col").astype(f32)
    shared_low = shared_sums.astype(bf16)
    late = jnp.concatenate([shared_low, pair_grad], axis=1)
    late = (late.astype(f32) + swap(late, "row").astype(f32)).astype(bf16)
    shared_low, pair_low = late[:, :shared_width], late[:, shared_width:]
    step_two = in_order(
        step_grad[:, :head_count], swap(step_grad, "row")[:, :head_count], row, 1
    )
    step_all = in_order(step_two, swap(step_two, "col"), col, 1)

    first_in_partial = (
        product_back(mix_half, mixer_in)
        + product_back(query_half, query_weight)
        + product_back(pair_low, kv_flat)
        + 0.5 * (product_back(shared_low, bc_weight) + product_back(step_all, step_weight))
    )
    first_in_grad = part_of(first_in_partial, col, 1) + swap(
        part_of(first_in_partial, 1 - col, 1).astype(bf16), "col"
    ).astype(f32)
    input_grad = (
        second_grad
        + norm_first * first_in_grad
        - residual * (first_factor**2 * first_total / D)[:, None]
    )
    norm_first_grad = jnp.sum(first_in_grad * residual, axis=0)

    mixer_in_grad = scatter_dp(outer_sum(first_half, mix_half).astype(bf16))
    rest = jnp.concatenate(
        [query_half, pair_low, part_of(shared_low, col, 1), to_lanes(step_all)], axis=1
    )
    rest_grad = scatter_dp(outer_sum(first_half, rest).astype(bf16))
    place = query_half.shape[1]
    query_weight_grad = rest_grad[:, :place]
    kv_weight_grad = rest_grad[:, place : place + pair_width].reshape((-1,) + kv_weight.shape[1:])
    place += pair_width
    bc_own = rest_grad[:, place : place + shared_width // 2]
    bc_weight_grad = in_order(bc_own, swap(bc_own, "col"), col, 1)
    place += shared_width // 2
    step_weight_grad = rest_grad[:, place : place + step_weight.shape[1]]

    conv_shared_sum = conv_shared_part + swap(conv_shared_part, "col")
    conv_shared_sum = conv_shared_sum + swap(conv_shared_sum, "row")
    skip_grad = wide_grads[1].reshape(head_count, PM).sum(axis=1)
    pieces = [
        norm_first_grad,
        norm_second_grad,
        conv_inner_grad.reshape(-1),
        conv_shared_sum.reshape(-1),
        wide_grads[0],
        jnp.pad(head_grads[0, :head_count], (0, LANES - head_count)),
        jnp.pad(head_grads[1, :head_count], (0, LANES - head_count)),
        jnp.pad(skip_grad, (0, LANES - head_count)),
    ]
    small = jnp.concatenate(pieces).reshape(-1, LANES)
    for bit in dp_bits():
        small = small + swap_dp(small, bit)
    small = small.reshape(-1)
    sums, place = [], 0
    for piece in pieces:
        sums.append(small[place : place + piece.shape[0]])
        place += piece.shape[0]
    me, count = lax.axis_index("dp"), lax.axis_size("dp")

    def own_block(values_in, axis):
        size = values_in.shape[axis] // count
        return lax.dynamic_slice_in_dim(values_in, me * size, size, axis)

    return (
        layer_out,
        input_grad,
        own_block(sums[0], 0),
        mixer_in_grad,
        query_weight_grad,
        bc_weight_grad,
        step_weight_grad,
        kv_weight_grad,
        own_block(sums[2].reshape(conv_inner.shape), 1),
        own_block(sums[3].reshape(conv_shared.shape), 1),
        sums[5][:head_count],
        sums[6][:head_count],
        sums[7][:head_count],
        own_block(sums[4], 0),
        out_weight_grad,
        own_block(sums[1], 0),
        gate_weight_grad,
        up_weight_grad,
        down_weight_grad,
    )


def solution(mesh):
    in_specs = (
        P("dp", ("row", "col")),
        P(("row", "col")),
        P("row", "col"),
        P("row", "col"),
        P("row", None),
        P("row", None),
        P("row", "col", None),
        P(None, ("col", "row")),
        P(),
        P(("col", "row")),
        P(("col", "row")),
        P(("col", "row")),
        P(("col", "row")),
        P("col", "row"),
        P(("row", "col")),
        P("row", "col"),
        P("row", "col"),
        P("col", "row"),
        P("dp", ("row", "col")),
    )
    out_specs = (
        P("dp", ("row", "col")),
        P("dp", ("row", "col")),
        P(("row", "col", "dp")),
        P(("row", "dp"), "col"),
        P(("row", "dp"), "col"),
        P(("row", "dp"), None),
        P(("row", "dp"), None),
        P(("row", "dp"), "col", None),
        P(None, ("col", "row", "dp")),
        P(None, "dp"),
        P(("col", "row")),
        P(("col", "row")),
        P(("col", "row")),
        P(("col", "row", "dp")),
        P(("col", "dp"), "row"),
        P(("row", "col", "dp")),
        P(("row", "dp"), "col"),
        P(("row", "dp"), "col"),
        P(("col", "dp"), "row"),
    )
    return jax.shard_map(local, mesh=mesh, in_specs=in_specs, out_specs=out_specs, check_vma=False)
```

```python
from functools import partial
import math

import jax
import jax.numpy as jnp
from jax import lax
from jax.experimental import pallas as pl
from jax.experimental.pallas import tpu as pltpu
from jax.sharding import PartitionSpec as P

D = 2048
HM = 48
PM = 64
NS = 256
HD = 128
MIX = 4096
LANES = 128
CHUNK = 128

norm_epsilon = 1e-05
rope_base = 10000.0
highest = lax.Precision.HIGHEST
f32 = jnp.float32
bf16 = jnp.bfloat16
VMEM_LIMIT = 56 * 1024 * 1024


def product(left_side, right_side):
    return jnp.dot(left_side, right_side, preferred_element_type=f32)


def product_back(left_side, right_side):
    return lax.dot_general(
        left_side, right_side, (((1,), (1,)), ((), ())), preferred_element_type=f32
    )


def outer_sum(left_side, right_side):
    return lax.dot_general(
        left_side, right_side, (((0,), (0,)), ((), ())), preferred_element_type=f32
    )


def swap(values_in, axis):
    return lax.ppermute(values_in, axis, [(0, 1), (1, 0)])


def in_order(own, other, place, axis):
    return jnp.concatenate(
        [jnp.where(place == 0, own, other), jnp.where(place == 0, other, own)], axis=axis
    )


def part_of(values_in, place, axis):
    size = values_in.shape[axis] // 2
    return lax.dynamic_slice_in_dim(values_in, place * size, size, axis)


def rows_total(values_in):
    values_in = values_in + swap(values_in, "col")
    return values_in + swap(values_in, "row")


def sum_cols(values_in, col):
    sent = swap(part_of(values_in, 1 - col, 1).astype(bf16), "col")
    return part_of(values_in, col, 1) + sent.astype(f32)


def near_blocks(values_in, near):
    size = MIX // 2 // lax.axis_size("dp")
    places = range(0, values_in.shape[1], 2 * size)
    return jnp.concatenate(
        [
            jnp.where(
                near == 0,
                values_in[:, place : place + size],
                values_in[:, place + size : place + 2 * size],
            )
            for place in places
        ],
        axis=1,
    )


def dp_bits():
    bits, bit = [], 1
    while bit < lax.axis_size("dp"):
        bits.append(bit)
        bit *= 2
    return bits


def swap_dp(values_in, bit):
    return lax.ppermute(values_in, "dp", [(i, i ^ bit) for i in range(lax.axis_size("dp"))])


def tie(*values_in):
    return lax.optimization_barrier(values_in)


class Spine:
    def __init__(self, token):
        self.token = token

    def wait(self, *values_in):
        tied = tie(self.token, *values_in)
        self.token = tied[0]
        return tied[1] if len(tied) == 2 else tied[1:]


class Scatter:
    def __init__(self, spine, grads, pairs, dtype=bf16):
        self.spine, self.dtype = spine, dtype
        self.bits = dp_bits()[1:]
        blocks = lax.axis_size("dp") // 2 * (2 if pairs else 1)
        rest = (blocks // 2 ** len(self.bits), grads.shape[0] // blocks) + grads.shape[1:]
        self.left = self.bits[::-1]
        self.parts = grads.reshape((2,) * len(self.bits) + rest)
        self.send()

    def send(self):
        bit = self.bits[len(self.bits) - len(self.left)]
        axis = self.left.index(bit)
        mine = (lax.axis_index("dp") // bit) % 2
        send = lax.dynamic_index_in_dim(self.parts, 1 - mine, axis, keepdims=False)
        self.parts = lax.dynamic_index_in_dim(self.parts, mine, axis, keepdims=False)
        self.arrived = swap_dp(send, bit)
        self.left.pop(axis)

    def add(self):
        arrived = self.spine.wait(self.arrived)
        total = self.parts.astype(f32) + arrived.astype(f32)
        self.parts = total.astype(bf16 if self.left else self.dtype)
        if self.left:
            self.send()

    def finish(self):
        while self.left:
            self.add()
        self.add()
        return self.parts


def place_kernel(count, owners, where_ref, *refs):
    pieces, out_ref = refs[:count], refs[count]
    rows = pieces[0].shape[0]
    for turn in range(count):
        start = pl.multiple_of((where_ref[0] ^ owners[turn]) * rows, rows)
        out_ref[pl.ds(start, rows), :] = pieces[turn][...]


def place_pieces(pieces, owners):
    count = len(pieces)
    rows, columns = pieces[0].shape
    return pl.pallas_call(
        partial(place_kernel, count, owners),
        out_shape=jax.ShapeDtypeStruct((count * rows, columns), pieces[0].dtype),
        in_specs=[pl.BlockSpec(memory_space=pltpu.SMEM)]
        + [pl.BlockSpec(memory_space=pltpu.VMEM)] * count,
        out_specs=pl.BlockSpec(memory_space=pltpu.VMEM),
        compiler_params=pltpu.CompilerParams(vmem_limit_bytes=VMEM_LIMIT),
        cost_estimate=pl.CostEstimate(
            flops=0, bytes_accessed=4 * count * rows * columns, transcendentals=0
        ),
    )(lax.axis_index("dp").astype(jnp.int32)[None], *pieces)


class Spread:
    def __init__(self, mine):
        self.pieces, self.owners = [mine], [0]
        self.bits = [dp_bits()[::-1]]
        self.first = 0

    def wait(self, spine):
        arrived = spine.wait(*self.pieces[self.first :])
        self.pieces[self.first :] = arrived if isinstance(arrived, (tuple, list)) else [arrived]

    def level(self):
        start, self.first = self.first, len(self.pieces)
        sends = [
            (-bit, turn) for turn in range(start, self.first) for bit in self.bits[turn]
        ]
        for bit, turn in sorted(sends):
            self.pieces.append(swap_dp(self.pieces[turn], -bit))
            self.owners.append(self.owners[turn] ^ -bit)
            self.bits.append([lower for lower in self.bits[turn] if lower < -bit])

    def finish(self, spine):
        self.wait(spine)
        while len(self.pieces) < lax.axis_size("dp"):
            self.level()
            self.wait(spine)
        return place_pieces(self.pieces, self.owners)


def sigmoid(values_in):
    return 1.0 / (1.0 + jnp.exp(-values_in))


def softplus(values_in):
    return jnp.maximum(values_in, 0.0) + jnp.log1p(jnp.exp(-jnp.abs(values_in)))


def low_lanes():
    return lax.broadcasted_iota(jnp.int32, (1, LANES), 1) < PM


def pair_columns(values_in, pair):
    return jnp.where(
        low_lanes(), values_in[:, 2 * pair : 2 * pair + 1], values_in[:, 2 * pair + 1 : 2 * pair + 2]
    )


def shift_down(values_in, count):
    if count == 0:
        return values_in
    rows = lax.broadcasted_iota(jnp.int32, values_in.shape, 0)
    return jnp.where(rows >= count, pltpu.roll(values_in, count, 0), 0.0)


def shift_up(values_in, count):
    if count == 0:
        return values_in
    length = values_in.shape[0]
    rows = lax.broadcasted_iota(jnp.int32, values_in.shape, 0)
    return jnp.where(rows < length - count, pltpu.roll(values_in, length - count, 0), 0.0)


def conv(values_in, taps):
    count = taps.shape[0]
    total = values_in * taps[count - 1 : count, :]
    for tap in range(count - 1):
        total = total + taps[tap : tap + 1, :] * shift_down(values_in, count - 1 - tap)
    return total


def conv_back(grad, values_in, taps):
    count = taps.shape[0]
    total = grad * taps[count - 1 : count, :]
    for tap in range(count - 1):
        total = total + taps[tap : tap + 1, :] * shift_up(grad, count - 1 - tap)
    tap_grads = [
        jnp.sum(grad * shift_down(values_in, count - 1 - tap), axis=0, keepdims=True)
        for tap in range(count)
    ]
    return total, tap_grads


def stacked_pair(values_in):
    low = low_lanes()
    return jnp.concatenate(
        [jnp.where(low, values_in, 0.0), jnp.where(low, 0.0, values_in)], axis=0
    ).astype(bf16)


def lower_mask():
    rows = lax.broadcasted_iota(jnp.int32, (CHUNK, CHUNK), 0)
    columns = lax.broadcasted_iota(jnp.int32, (CHUNK, CHUNK), 1)
    return (rows >= columns).astype(f32)


def mixer_forward_kernel(
    own_ref,
    other_ref,
    factor_ref,
    shared_ref,
    step_ref,
    conv_inner_ref,
    conv_shared_ref,
    head_ref,
    skip_ref,
    gain_ref,
    attended_ref,
    mixed_ref,
    square_ref,
    mix_ref,
    ssm_ref,
    states_ref,
    inner_buf,
    gate_buf,
    maps_buf,
    step_buf,
    decay_buf,
    weighted_buf,
    state_buf,
):
    pairs = ssm_ref.shape[1] // LANES
    length = own_ref.shape[0]
    groups = attended_ref.shape[1] // HD
    group_pairs = pairs // groups
    low = low_lanes()
    factor = factor_ref[...]
    for group in range(groups):
        place = ((group + 1) * group_pairs + group) * LANES
        mixed_ref[:, place : place + HD] = attended_ref[:, group * HD : (group + 1) * HD]
    for pair in range(pairs):
        first = slice(2 * pair * LANES, (2 * pair + 1) * LANES)
        second = slice((2 * pair + 1) * LANES, (2 * pair + 2) * LANES)
        own = slice(pair * LANES, (pair + 1) * LANES)
        head_a = (own_ref[:, first] + other_ref[:, first].astype(f32)) * factor
        head_b = (own_ref[:, second] + other_ref[:, second].astype(f32)) * factor
        mix_ref[:, first] = head_a
        mix_ref[:, second] = head_b
        taken = jnp.where(low, pltpu.roll(head_a, PM, 1), head_b)
        gate_buf[:, own] = jnp.where(low, head_a, pltpu.roll(head_b, PM, 1))
        taken = conv(taken, conv_inner_ref[:, own])
        inner_buf[:, own] = taken * sigmoid(taken)
    for block in range(shared_ref.shape[1] // LANES):
        own = slice(block * LANES, (block + 1) * LANES)
        taken = conv(shared_ref[:, own], conv_shared_ref[:, own])
        maps_buf[:, own] = (taken * sigmoid(taken)).astype(bf16)
    steps = softplus(step_ref[...] + head_ref[1:2, :])
    step_buf[...] = steps
    decay_buf[...] = -jnp.exp(head_ref[0:1, :]) * steps
    state_buf[...] = jnp.zeros_like(state_buf)
    mask = lower_mask()

    def chunk(index, carry):
        rows = pl.ds(pl.multiple_of(index * CHUNK, CHUNK), CHUNK)
        running = jnp.dot(mask, decay_buf[rows, :], precision=highest, preferred_element_type=f32)
        running_t = running.T
        step = step_buf[rows, :]
        step_t = step.T
        last = running[CHUNK - 1 : CHUNK, :]
        grown = jnp.exp(running)
        tail = jnp.exp(last - running) * step
        grown_last = jnp.exp(last)
        basis = maps_buf[rows, 0:NS]
        read = maps_buf[rows, NS : 2 * NS]
        gram = product_back(read, basis)
        state_low = state_buf[...].astype(bf16)
        states_ref[pl.ds(pl.multiple_of(index * NS, NS), NS), :] = state_low
        carried = product(read, state_low)
        square = jnp.zeros((CHUNK, 1), f32)
        for pair in range(pairs):
            own = slice(pair * LANES, (pair + 1) * LANES)
            inner = inner_buf[rows, own]
            mixing = []
            for head in (2 * pair, 2 * pair + 1):
                spread = jnp.exp(
                    jnp.minimum(running[:, head : head + 1] - running_t[head : head + 1, :], 0.0)
                )
                mixing.append(
                    (gram * spread * mask * step_t[head : head + 1, :]).astype(bf16)
                )
            ssm = product(jnp.concatenate(mixing, axis=1), stacked_pair(inner))
            ssm = ssm + pair_columns(grown, pair) * carried[:, own] + skip_ref[:, own] * inner
            ssm_ref[rows, own] = ssm
            weighted_buf[:, own] = (pair_columns(tail, pair) * inner).astype(bf16)
            gate = gate_buf[rows, own]
            gated = ssm * gate * sigmoid(gate)
            square = square + jnp.sum(gated * gated, axis=1, keepdims=True)
            place = pair * LANES + (pair // group_pairs) * HD
            mixed_ref[rows, place : place + LANES] = (gated * gain_ref[:, own]).astype(bf16)
        square_ref[rows, :] = square
        fresh = outer_sum(basis, weighted_buf[...])
        for pair in range(pairs):
            own = slice(pair * LANES, (pair + 1) * LANES)
            state_buf[:, own] = (
                pair_columns(grown_last, pair) * state_buf[:, own] + fresh[:, own]
            )
        return carry

    lax.fori_loop(0, length // CHUNK, chunk, 0)


def mixer_backward_kernel(
    mix_ref,
    ssm_ref,
    states_ref,
    shared_ref,
    step_ref,
    conv_inner_ref,
    conv_shared_ref,
    head_ref,
    skip_ref,
    gain_ref,
    lanes_ref,
    grad_ref,
    group_factor_ref,
    group_scale_ref,
    factor_ref,
    mix_grad_ref,
    shared_grad_ref,
    step_grad_ref,
    inner_taps_ref,
    shared_taps_ref,
    head_grad_ref,
    wide_grad_ref,
    total_ref,
    taken_buf,
    inner_buf,
    maps_buf,
    step_buf,
    decay_buf,
    weighted_buf,
    grown_buf,
    inner_grad_buf,
    maps_grad_buf,
    sums_buf,
    state_grad_buf,
):
    pairs = ssm_ref.shape[1] // LANES
    length = ssm_ref.shape[0]
    group_pairs = pairs // (grad_ref.shape[1] // (pairs * LANES // 2 + HD))
    low = low_lanes()
    for pair in range(pairs):
        first = slice(2 * pair * LANES, (2 * pair + 1) * LANES)
        second = slice((2 * pair + 1) * LANES, (2 * pair + 2) * LANES)
        own = slice(pair * LANES, (pair + 1) * LANES)
        taken = jnp.where(low, pltpu.roll(mix_ref[:, first], PM, 1), mix_ref[:, second])
        taken_buf[:, own] = taken
        taken = conv(taken, conv_inner_ref[:, own])
        inner_buf[:, own] = taken * sigmoid(taken)
    for block in range(shared_ref.shape[1] // LANES):
        own = slice(block * LANES, (block + 1) * LANES)
        taken = conv(shared_ref[:, own], conv_shared_ref[:, own])
        maps_buf[:, own] = (taken * sigmoid(taken)).astype(bf16)
    shifted = step_ref[...] + head_ref[1:2, :]
    steps = softplus(shifted)
    rate = -jnp.exp(head_ref[0:1, :])
    step_buf[...] = steps
    decay_buf[...] = rate * steps
    state_grad_buf[...] = jnp.zeros_like(state_grad_buf)
    head_grad_ref[...] = jnp.zeros_like(head_grad_ref)
    wide_grad_ref[...] = jnp.zeros_like(wide_grad_ref)
    mask = lower_mask()
    chunks = length // CHUNK
    lane_index = lax.broadcasted_iota(jnp.int32, (1, LANES), 1)

    def chunk(turn, carry):
        index = chunks - 1 - turn
        rows = pl.ds(pl.multiple_of(index * CHUNK, CHUNK), CHUNK)
        running = jnp.dot(mask, decay_buf[rows, :], precision=highest, preferred_element_type=f32)
        running_t = running.T
        step = step_buf[rows, :]
        step_t = step.T
        last = running[CHUNK - 1 : CHUNK, :]
        grown = jnp.exp(running)
        fading = jnp.exp(last - running)
        grown_last = jnp.exp(last)
        basis = maps_buf[rows, 0:NS]
        read = maps_buf[rows, NS : 2 * NS]
        gram = product_back(read, basis)
        state_low = states_ref[pl.ds(pl.multiple_of(index * NS, NS), NS), :]
        carried = product(read, state_low)
        state_grad_low = state_grad_buf[...].astype(bf16)
        weighted_grad = product(basis, state_grad_low)
        gram_grad = jnp.zeros((CHUNK, CHUNK), f32)
        decay_grad = jnp.zeros((CHUNK, LANES), f32)
        column_grads = []
        total = jnp.zeros((CHUNK, 1), f32)
        group_factor = group_factor_ref[rows, :]
        group_scale = group_scale_ref[rows, :]
        factor = factor_ref[rows, :]
        for pair in range(pairs):
            first = slice(2 * pair * LANES, (2 * pair + 1) * LANES)
            second = slice((2 * pair + 1) * LANES, (2 * pair + 2) * LANES)
            own = slice(pair * LANES, (pair + 1) * LANES)
            place = pair * LANES + (pair // group_pairs) * HD
            incoming = grad_ref[rows, place : place + LANES]
            head_a = mix_ref[rows, first]
            head_b = mix_ref[rows, second]
            gate = jnp.where(low, head_a, pltpu.roll(head_b, PM, 1))
            gate_sigmoid = sigmoid(gate)
            gate_act = gate * gate_sigmoid
            ssm = ssm_ref[rows, own]
            gated = ssm * gate_act
            wide_grad_ref[0:1, own] += jnp.sum(
                incoming * gated * group_factor, axis=0, keepdims=True
            )
            gated_grad = group_factor * gain_ref[:, own] * incoming - gated * group_scale
            gate_grad = gated_grad * ssm * gate_sigmoid * (1.0 + gate * (1.0 - gate_sigmoid))
            ssm_grad = gated_grad * gate_act
            inner = inner_buf[rows, own]
            wide_grad_ref[1:2, own] += jnp.sum(ssm_grad * inner, axis=0, keepdims=True)
            gate_b = pltpu.roll(gate_grad, PM, 1)
            total = total + jnp.sum(gate_grad * gate, axis=1, keepdims=True)
            mix_grad_ref[rows, first] = jnp.where(low, gate_grad * factor, 0.0).astype(bf16)
            mix_grad_ref[rows, second] = jnp.where(low, gate_b * factor, 0.0).astype(bf16)
            grad_low = ssm_grad.astype(bf16)
            mixing_grad = product_back(grad_low, stacked_pair(inner))
            spreads = []
            for side, head in enumerate((2 * pair, 2 * pair + 1)):
                spread = mask * jnp.exp(
                    jnp.minimum(running[:, head : head + 1] - running_t[head : head + 1, :], 0.0)
                )
                step_row = step_t[head : head + 1, :]
                spread_gram = gram * spread
                spreads.append(spread_gram.astype(bf16))
                own_grad = mixing_grad[:, side * CHUNK : (side + 1) * CHUNK] * step_row
                gram_grad = gram_grad + own_grad * spread
                moved = own_grad * spread_gram
                decay_grad = decay_grad + jnp.where(
                    lane_index == head, jnp.sum(moved, axis=1, keepdims=True), 0.0
                )
                column_grads.append(jnp.sum(moved, axis=0, keepdims=True))
            within = outer_sum(jnp.concatenate(spreads, axis=0), stacked_pair(ssm_grad))
            fading_grad = pair_columns(fading, pair) * weighted_grad[:, own]
            spread_grad = within + fading_grad
            step_wide = pair_columns(step, pair)
            inner_grad_buf[rows, own] = step_wide * spread_grad + skip_ref[:, own] * ssm_grad
            grown_grad = pair_columns(grown, pair) * ssm_grad
            grown_buf[:, own] = grown_grad.astype(bf16)
            weighted_buf[:, own] = (pair_columns(fading, pair) * step_wide * inner).astype(bf16)
            sums_buf[0:CHUNK, own] = (inner * spread_grad).astype(bf16)
            sums_buf[CHUNK : 2 * CHUNK, own] = (inner * fading_grad * step_wide).astype(bf16)
            sums_buf[2 * CHUNK : 3 * CHUNK, own] = (grown_grad * carried[:, own]).astype(bf16)
        head_sums = product(sums_buf[...], lanes_ref[...])
        step_part = head_sums[0:CHUNK, :]
        fading_part = head_sums[CHUNK : 2 * CHUNK, :]
        grown_part = head_sums[2 * CHUNK : 3 * CHUNK, :]
        fill = jnp.zeros((CHUNK - len(column_grads), CHUNK), f32)
        column_grad = jnp.concatenate(column_grads + [fill], axis=0).T
        decay_grad = decay_grad - column_grad + grown_part - fading_part
        state_part = jnp.zeros((1, LANES), f32)
        grown_low = grown_buf[...]
        fresh = outer_sum(read, grown_low)
        for pair in range(pairs):
            own = slice(pair * LANES, (pair + 1) * LANES)
            state_grad = state_grad_buf[:, own]
            held = jnp.sum(state_grad * state_low[:, own].astype(f32), axis=0, keepdims=True)
            for side, head in enumerate((2 * pair, 2 * pair + 1)):
                kept = jnp.where(low if side == 0 else jnp.logical_not(low), held, 0.0)
                state_part = state_part + jnp.where(
                    lane_index == head, jnp.sum(kept, axis=1, keepdims=True), 0.0
                )
            state_grad_buf[:, own] = pair_columns(grown_last, pair) * state_grad + fresh[:, own]
        last_grad = jnp.sum(fading_part, axis=0, keepdims=True) + grown_last * state_part
        decay_sum = (
            lax.dot_general(
                mask,
                decay_grad,
                (((0,), (0,)), ((), ())),
                precision=highest,
                preferred_element_type=f32,
            )
            + last_grad
        )
        raw_shift = step_ref[rows, :] + head_ref[1:2, :]
        raw_grad = (step_part + decay_sum * rate) * sigmoid(raw_shift)
        head_grad_ref[0:1, :] += jnp.sum(decay_sum * decay_buf[rows, :], axis=0, keepdims=True)
        head_grad_ref[1:2, :] += jnp.sum(raw_grad, axis=0, keepdims=True)
        step_grad_ref[rows, :] = (raw_grad * factor).astype(bf16)
        total = total + jnp.sum(raw_grad * step_ref[rows, :], axis=1, keepdims=True)
        total_ref[rows, :] = total
        gram_low = gram_grad.astype(bf16)
        maps_grad_buf[rows, 0:NS] = outer_sum(gram_low, read) + product_back(
            weighted_buf[...], state_grad_low
        )
        maps_grad_buf[rows, NS : 2 * NS] = product(gram_low, basis) + product_back(
            grown_low, state_low
        )
        return carry

    lax.fori_loop(0, chunks, chunk, 0)
    factor = factor_ref[...]
    total = total_ref[...]
    for pair in range(pairs):
        first = slice(2 * pair * LANES, (2 * pair + 1) * LANES)
        second = slice((2 * pair + 1) * LANES, (2 * pair + 2) * LANES)
        own = slice(pair * LANES, (pair + 1) * LANES)
        taken = taken_buf[:, own]
        taps = conv_inner_ref[:, own]
        before = conv(taken, taps)
        before_sigmoid = sigmoid(before)
        grad = inner_grad_buf[:, own] * before_sigmoid * (1.0 + before * (1.0 - before_sigmoid))
        grad, tap_grads = conv_back(grad, taken, taps)
        for tap, tap_grad in enumerate(tap_grads):
            inner_taps_ref[tap : tap + 1, own] = tap_grad
        total = total + jnp.sum(grad * taken, axis=1, keepdims=True)
        grad = grad * factor
        low_a = mix_grad_ref[:, first].astype(f32)
        low_b = mix_grad_ref[:, second].astype(f32)
        mix_grad_ref[:, first] = jnp.where(low, low_a, pltpu.roll(grad, PM, 1)).astype(bf16)
        mix_grad_ref[:, second] = jnp.where(low, low_b, grad).astype(bf16)
    for block in range(shared_ref.shape[1] // LANES):
        own = slice(block * LANES, (block + 1) * LANES)
        taken = shared_ref[:, own]
        taps = conv_shared_ref[:, own]
        before = conv(taken, taps)
        before_sigmoid = sigmoid(before)
        grad = maps_grad_buf[:, own] * before_sigmoid * (1.0 + before * (1.0 - before_sigmoid))
        grad, tap_grads = conv_back(grad, taken, taps)
        for tap, tap_grad in enumerate(tap_grads):
            shared_taps_ref[tap : tap + 1, own] = tap_grad
        total = total + jnp.sum(grad * taken, axis=1, keepdims=True)
        shared_grad_ref[:, own] = (grad * factor).astype(bf16)
    total_ref[...] = total


def call(kernel, outs, scratch, flops, *operands):
    return pl.pallas_call(
        kernel,
        out_shape=outs,
        in_specs=[pl.BlockSpec(memory_space=pltpu.VMEM)] * len(operands),
        out_specs=[pl.BlockSpec(memory_space=pltpu.VMEM)] * len(outs),
        scratch_shapes=scratch,
        compiler_params=pltpu.CompilerParams(vmem_limit_bytes=VMEM_LIMIT),
        cost_estimate=pl.CostEstimate(flops=flops, bytes_accessed=10**6, transcendentals=0),
    )(*operands)


def shape(dims, dtype=f32):
    return jax.ShapeDtypeStruct(dims, dtype)


def mixer_forward(
    own, other, factor, shared, step, taps, shared_taps, heads, skip, gain, attended
):
    length, width = own.shape
    channels = width // 2
    chunks = length // CHUNK
    return call(
        mixer_forward_kernel,
        [
            shape((length, channels + attended.shape[1]), bf16),
            shape((length, 1)),
            shape((length, width)),
            shape((length, channels)),
            shape((chunks * NS, channels), bf16),
        ],
        [
            pltpu.VMEM((length, channels), f32),
            pltpu.VMEM((length, channels), f32),
            pltpu.VMEM((length, 2 * NS), bf16),
            pltpu.VMEM((length, LANES), f32),
            pltpu.VMEM((length, LANES), f32),
            pltpu.VMEM((CHUNK, channels), bf16),
            pltpu.VMEM((NS, channels), f32),
        ],
        10**8,
        own, other, factor, shared, step, taps, shared_taps, heads, skip, gain, attended,
    )


def mixer_backward(
    mix, ssm, states, shared, step, taps, shared_taps, heads, skip, gain, lanes, grad,
    group_factor, group_scale, factor,
):
    length, width = mix.shape
    channels = width // 2
    return call(
        mixer_backward_kernel,
        [
            shape((length, width), bf16),
            shape((length, 2 * NS), bf16),
            shape((length, LANES), bf16),
            shape((taps.shape[0], channels)),
            shape((taps.shape[0], 2 * NS)),
            shape((8, LANES)),
            shape((8, channels)),
            shape((length, 1)),
        ],
        [
            pltpu.VMEM((length, channels), f32),
            pltpu.VMEM((length, channels), f32),
            pltpu.VMEM((length, 2 * NS), bf16),
            pltpu.VMEM((length, LANES), f32),
            pltpu.VMEM((length, LANES), f32),
            pltpu.VMEM((CHUNK, channels), bf16),
            pltpu.VMEM((CHUNK, channels), bf16),
            pltpu.VMEM((length, channels), f32),
            pltpu.VMEM((length, 2 * NS), f32),
            pltpu.VMEM((3 * CHUNK, channels), bf16),
            pltpu.VMEM((NS, channels), f32),
        ],
        10**8,
        mix, ssm, states, shared, step, taps, shared_taps, heads, skip, gain, lanes, grad,
        group_factor, group_scale, factor,
    )


def rotated(values_in, cosine, sine):
    return values_in * cosine + pltpu.roll(values_in, HD // 2, 1) * sine


def rotated_back(grad, cosine, sine):
    return grad * cosine + pltpu.roll(grad * sine, HD // 2, 1)


def attention_forward_kernel(query_ref, pair_ref, cosine_ref, sine_ref, out_ref):
    length = query_ref.shape[0]
    scale = 1.0 / math.sqrt(HD)
    block = min(256, length)
    keys = rotated(pair_ref[:, :HD], cosine_ref[...], sine_ref[...]).astype(bf16)
    vals = pair_ref[:, HD:].astype(bf16)
    for head in range(query_ref.shape[1] // HD):
        lanes = slice(head * HD, (head + 1) * HD)
        queries = rotated(query_ref[:, lanes], cosine_ref[...], sine_ref[...]).astype(bf16)
        for start in range(0, length, block):
            end = start + block
            scores = product_back(queries[start:end], keys[:end]) * scale
            rows = start + lax.broadcasted_iota(jnp.int32, (block, end), 0)
            columns = lax.broadcasted_iota(jnp.int32, (block, end), 1)
            scores = jnp.where(columns <= rows, scores, -1e30)
            exponent = jnp.exp(scores - jnp.max(scores, axis=1, keepdims=True))
            probs = exponent * (1.0 / jnp.sum(exponent, axis=1, keepdims=True))
            out_ref[start:end, lanes] = product(probs.astype(bf16), vals[:end]).astype(bf16)


def attention_backward_kernel(
    query_ref, pair_ref, cosine_ref, sine_ref, grad_ref, factor_ref,
    query_grad_ref, pair_grad_ref, total_ref, key_buf, val_buf,
):
    length = query_ref.shape[0]
    scale = 1.0 / math.sqrt(HD)
    block = min(256, length)
    cosine, sine = cosine_ref[...], sine_ref[...]
    keys = rotated(pair_ref[:, :HD], cosine, sine).astype(bf16)
    vals = pair_ref[:, HD:].astype(bf16)
    heads = query_ref.shape[1] // HD
    group = grad_ref.shape[1] // heads
    key_buf[...] = jnp.zeros_like(key_buf)
    val_buf[...] = jnp.zeros_like(val_buf)
    for head in range(heads):
        lanes = slice(head * HD, (head + 1) * HD)
        queries = rotated(query_ref[:, lanes], cosine, sine).astype(bf16)
        incoming = grad_ref[:, (head + 1) * group - HD : (head + 1) * group].astype(bf16)
        for start in range(0, length, block):
            end = start + block
            scores = product_back(queries[start:end], keys[:end]) * scale
            rows = start + lax.broadcasted_iota(jnp.int32, (block, end), 0)
            columns = lax.broadcasted_iota(jnp.int32, (block, end), 1)
            scores = jnp.where(columns <= rows, scores, -1e30)
            exponent = jnp.exp(scores - jnp.max(scores, axis=1, keepdims=True))
            probs = exponent * (1.0 / jnp.sum(exponent, axis=1, keepdims=True))
            grad_low = incoming[start:end]
            val_buf[:end, :] += outer_sum(probs.astype(bf16), grad_low)
            probs_grad = product_back(grad_low, vals[:end])
            inner = jnp.sum(probs * probs_grad, axis=1, keepdims=True)
            scores_grad = (probs * (probs_grad - inner) * scale).astype(bf16)
            query_grad = rotated_back(
                product(scores_grad, keys[:end]), cosine[start:end], sine[start:end]
            )
            key_buf[:end, :] += outer_sum(scores_grad, queries[start:end])
            taken = query_ref[start:end, lanes]
            part = jnp.sum(query_grad * taken, axis=1, keepdims=True)
            if head == 0:
                total_ref[start:end, :] = part
            else:
                total_ref[start:end, :] += part
            query_grad_ref[start:end, lanes] = (query_grad * factor_ref[start:end, :]).astype(bf16)
    key_grad = rotated_back(key_buf[...], cosine, sine)
    val_grad = val_buf[...]
    total_ref[...] += jnp.sum(
        key_grad * pair_ref[:, :HD] + val_grad * pair_ref[:, HD:], axis=1, keepdims=True
    )
    pair_grad_ref[:, :HD] = (key_grad * factor_ref[...]).astype(bf16)
    pair_grad_ref[:, HD:] = (val_grad * factor_ref[...]).astype(bf16)


def attention_forward(query, pair, cosine, sine):
    return call(
        attention_forward_kernel, [shape(query.shape, bf16)], [], 10**8,
        query, pair, cosine, sine,
    )[0]


def attention_backward(query, pair, cosine, sine, grad, factor):
    length = query.shape[0]
    return call(
        attention_backward_kernel,
        [shape(query.shape, bf16), shape(pair.shape, bf16), shape((length, 1))],
        [pltpu.VMEM((length, HD), f32), pltpu.VMEM((length, HD), f32)],
        10**8,
        query, pair, cosine, sine, grad, factor,
    )


def rope_tables(length):
    half = HD // 2
    inverse = rope_base ** (-jnp.arange(half, dtype=f32) * 2.0 / HD)
    angles = jnp.arange(length, dtype=f32)[:, None] * inverse[None, :]
    cosine, sine = jnp.cos(angles), jnp.sin(angles)
    return jnp.concatenate([cosine, cosine], axis=1), jnp.concatenate([-sine, sine], axis=1)


def to_lanes(values_in):
    return jnp.pad(values_in, ((0, 0), (0, LANES - values_in.shape[1])))


def local(
    tokens,
    norm_first,
    mixer_in,
    query_weight,
    bc_weight,
    step_weight,
    kv_weight,
    conv_inner,
    conv_shared,
    log_rate,
    step_bias,
    skip_gain,
    group_gain,
    out_weight,
    norm_second,
    gate_weight,
    up_weight,
    down_weight,
    cotangent,
):
    length = tokens.shape[0]
    row = lax.axis_index("row")
    col = lax.axis_index("col")
    me = lax.axis_index("dp")
    count = lax.axis_size("dp")
    near = me % 2
    quarter = col * 2 + row
    head_count = log_rate.shape[0]
    channels = group_gain.shape[0]
    kv_flat = kv_weight.reshape(kv_weight.shape[0], -1)
    residual = tokens.astype(f32)
    spine = Spine(norm_first[:1])

    def column_share(weight):
        rows, columns = weight.shape[0] // count, weight.shape[1] // 2
        return lax.dynamic_slice(weight, (me * rows, (1 - row) * columns), (rows, columns))

    half_rows = out_weight.shape[0] // 2
    share_rows = half_rows // count
    out_own = part_of(out_weight, row, 0)
    gate_own, up_own = part_of(gate_weight, row, 1), part_of(up_weight, row, 1)
    out_share = lax.dynamic_slice_in_dim(
        out_weight, (1 - row) * half_rows + me * share_rows, share_rows, 0
    )
    ffn_share = jnp.concatenate([column_share(gate_weight), column_share(up_weight)], axis=1)
    out_spread = Spread(swap(out_share, "row"))
    ffn_spread = Spread(swap(ffn_share, "row"))

    first_own = (residual * norm_first).astype(bf16)
    first_half = in_order(first_own, swap(first_own, "col"), col, 1)
    square_first = jnp.sum(residual * residual, axis=1)
    square_first = square_first + swap(square_first, "col")
    query_own = product(first_half, part_of(query_weight, row, 1))
    query_out = product(first_half, part_of(query_weight, 1 - row, 1)).astype(bf16)
    pair_own = product(first_half, kv_flat)
    shared_own = product(first_half, bc_weight)
    step_own = product(first_half, step_weight)
    query_width = query_own.shape[1]
    pair_width = pair_own.shape[1]
    shared_width = shared_own.shape[1]
    early = swap(
        jnp.concatenate(
            [
                query_out,
                pair_own.astype(bf16),
                part_of(shared_own, col, 1).astype(bf16),
                to_lanes(step_own).astype(bf16),
            ],
            axis=1,
        ),
        "row",
    )
    mix_other = swap(product(first_half, part_of(mixer_in, 1 - row, 1)).astype(bf16), "row")
    mix_own = product(first_half, part_of(mixer_in, row, 1))
    cot_half = in_order(cotangent, swap(cotangent, "col"), col, 1)
    hidden_back = product_back(cot_half, part_of(down_weight, 1 - row, 0)).astype(bf16)
    hidden_back_own = product_back(cot_half, part_of(down_weight, row, 0))

    out_spread.wait(spine)
    out_spread.level()
    square_first = spine.wait(square_first)
    square_far = swap(square_first, "row")
    ffn_spread.wait(spine)
    ffn_spread.level()
    out_spread.wait(spine)
    out_spread.level()
    early, square_far = spine.wait(early, square_far)
    first_factor = lax.rsqrt((square_first + square_far) / D + norm_epsilon)
    first_column = first_factor[:, None]
    query_sum = (query_own + early[:, :query_width].astype(f32)) * first_column
    place = query_width
    pair_sum = (pair_own + early[:, place : place + pair_width].astype(f32)) * first_column
    place += pair_width
    shared_sum = (
        part_of(shared_own, col, 1) + early[:, place : place + shared_width // 2].astype(f32)
    ) * first_column
    shared_sum = in_order(
        shared_sum, swap(shared_sum.astype(bf16), "col").astype(f32), col, 1
    )
    place += shared_width // 2
    step_sum = (
        step_own + early[:, place : place + step_own.shape[1]].astype(f32)
    ) * first_column
    step_sum = to_lanes(lax.dynamic_slice_in_dim(step_sum, quarter * head_count, head_count, 1))
    ffn_spread.wait(spine)
    ffn_spread.level()
    cosine, sine = rope_tables(length)
    attended = attention_forward(query_sum, pair_sum, cosine, sine)
    heads = to_lanes(jnp.stack([log_rate, step_bias] + [jnp.zeros_like(log_rate)] * 6))
    skip_wide = jnp.repeat(skip_gain, PM)[None, :]
    gain_wide = group_gain[None, :]
    out_spread.wait(spine)
    out_spread.level()
    mix_other, hidden_back = spine.wait(mix_other, hidden_back)
    hidden_back = swap(hidden_back, "row")
    ffn_spread.wait(spine)
    ffn_spread.level()
    mix_own, mix_other = spine.wait(mix_own, mix_other)
    mixed_raw, square, mix_sum, ssm, states = mixer_forward(
        mix_own, mix_other, first_column, shared_sum, step_sum, conv_inner, conv_shared,
        heads, skip_wide, gain_wide, attended,
    )
    square = spine.wait(square)
    out_other = out_spread.finish(spine)
    group_factor = lax.rsqrt(rows_total(square[:, 0]) / (HM * PM) + norm_epsilon)
    groups = attended.shape[1] // HD
    group_width = mixed_raw.shape[1] // groups
    is_normed = jnp.arange(mixed_raw.shape[1])[None, :] % group_width < group_width - HD
    mixed = (
        mixed_raw.astype(f32) * jnp.where(is_normed, group_factor[:, None], 1.0)
    ).astype(bf16)

    out_far = sum_cols(product(mixed, out_other), col)
    out_far = swap(out_far.astype(bf16), "row")
    out_near = sum_cols(product(mixed, out_own), col)
    out_far = spine.wait(out_far)
    second = residual + out_near + out_far.astype(f32)
    second_own = (second * norm_second).astype(bf16)
    second_far = swap(second_own, "row")
    second_half = in_order(second_own, swap(second_own, "col"), col, 1)
    second_near = swap_dp(second_own, 1)
    second_square = jnp.sum(second * second, axis=1)
    second_square = second_square + swap(second_square, "col")
    second_square_far = swap(second_square, "row")
    gate_width = gate_own.shape[1]
    gate_part, up_part = product(second_half, gate_own), product(second_half, up_own)
    second_far, second_near = spine.wait(second_far, second_near)
    second_far = in_order(second_far, swap(second_far, "col"), col, 1)
    second_far_near = swap(second_near, "row")
    second_near = in_order(second_near, swap(second_near, "col"), col, 1)
    ffn_other = ffn_spread.finish(spine)
    second_factor = lax.rsqrt((second_square + second_square_far) / D + norm_epsilon)
    second_column = second_factor[:, None]
    gate_sum = (gate_part + product(second_far, ffn_other[:, :gate_width])) * second_column
    up_sum = (up_part + product(second_far, ffn_other[:, gate_width:])) * second_column
    gate_sigmoid = jax.nn.sigmoid(gate_sum)
    gate_act = gate_sum * gate_sigmoid
    hidden_back = spine.wait(hidden_back)
    hidden_grad = hidden_back_own + hidden_back.astype(f32)
    gate_grad = hidden_grad * up_sum * gate_sigmoid * (1.0 + gate_sum * (1.0 - gate_sigmoid))
    up_grad = hidden_grad * gate_act
    hidden = (gate_act * up_sum).astype(bf16)
    ffn_grad = jnp.concatenate(
        [(gate_grad * second_column).astype(bf16), (up_grad * second_column).astype(bf16)], axis=1
    )
    second_total = jnp.sum(gate_grad * gate_sum + up_grad * up_sum, axis=1)
    second_total = second_total + swap(second_total, "col")
    second_total_far = swap(second_total, "row")
    ffn_send = swap_dp(part_of(ffn_grad, 1 - near, 1), 1)
    back_far = sum_cols(product_back(ffn_grad, ffn_other), col)
    back_far = swap(back_far.astype(bf16), "row")
    back_near = sum_cols(
        product_back(ffn_grad[:, :gate_width], gate_own)
        + product_back(ffn_grad[:, gate_width:], up_own),
        col,
    )
    second_total_far, second_far_near = spine.wait(second_total_far, second_far_near)
    second_far_near = in_order(second_far_near, swap(second_far_near, "col"), col, 1)
    back_far = spine.wait(back_far)
    second_in_grad = back_near + back_far.astype(f32)
    second_grad = (
        cotangent.astype(f32)
        + norm_second * second_in_grad
        - second * (second_factor**2 * (second_total + second_total_far) / D)[:, None]
    )
    norm_second_grad = jnp.sum(second_in_grad * second, axis=0)
    branch = second_grad.astype(bf16)
    branch_far = swap(branch, "row")
    branch_half = in_order(branch, swap(branch, "col"), col, 1)
    branch_near = swap_dp(branch, 1)

    branch_half, ffn_send = spine.wait(branch_half, ffn_send)
    ffn_kept = part_of(ffn_grad, near, 1)
    ffn_scatter = Scatter(
        spine,
        (outer_sum(second_half, ffn_kept) + outer_sum(second_near, ffn_send)).astype(bf16),
        True,
    )
    ffn_scatter_far = Scatter(
        spine,
        (outer_sum(second_far, ffn_kept) + outer_sum(second_far_near, ffn_send)).astype(bf16),
        True,
    )
    branch_far = spine.wait(branch_far)
    branch_far = in_order(branch_far, swap(branch_far, "col"), col, 1)
    mixed_grad = product_back(branch_half, out_own) + product_back(branch_far, out_other)

    group_total = jnp.sum(jnp.where(is_normed, mixed_grad * mixed.astype(f32), 0.0), axis=1)
    group_total = group_total + swap(group_total, "col")
    group_total_far = swap(group_total, "row")
    query_grad, pair_grad, attention_total = attention_backward(
        query_sum, pair_sum, cosine, sine, mixed_grad, first_column
    )
    group_total_far, attention_total = spine.wait(group_total_far, attention_total)
    group_scale = group_factor**2 * (group_total + group_total_far) / (HM * PM)
    group_scale, mixed_send, first_send = spine.wait(group_scale, mixed, first_own)
    mixed_near = swap_dp(near_blocks(mixed_send, 1 - near), 1)
    mixed_kept = near_blocks(mixed_send, near)
    mixed_kept_far = swap(mixed_kept, "row")
    first_far = swap(first_send, "row")
    first_near = swap_dp(first_send, 1)
    lanes = (
        jnp.arange(channels)[:, None] // PM == jnp.arange(LANES)[None, :]
    ).astype(bf16)
    (
        mix_grad,
        shared_grad,
        step_grad,
        conv_inner_grad,
        conv_shared_part,
        head_grads,
        wide_grads,
        mixer_total,
    ) = mixer_backward(
        mix_sum, ssm, states, shared_sum, step_sum, conv_inner, conv_shared, heads, skip_wide,
        gain_wide, lanes, mixed_grad, group_factor[:, None], group_scale[:, None], first_column,
    )
    mix_grad, shared_grad = spine.wait(mix_grad, shared_grad)
    own_grads = jnp.concatenate([mix_grad, query_grad], axis=1)
    grads_send = swap_dp(part_of(own_grads, 1 - near, 1), 1)
    shared_low = (shared_grad.astype(f32) + swap(shared_grad, "col").astype(f32)).astype(bf16)
    late = jnp.concatenate(
        [part_of(shared_low, col, 1), pair_grad, step_grad], axis=1
    )
    late_far = swap(late, "row")
    ffn_scatter.add()
    ffn_scatter_far.add()
    mixed_near, first_near = spine.wait(mixed_near, first_near)
    mixed_near_far = swap(mixed_near, "row")
    first_far_near = swap(first_near, "row")
    mixed_kept_far, branch_near = spine.wait(mixed_kept_far, branch_near)
    mixed_kept = in_order(mixed_kept, mixed_kept_far, row, 1)
    branch_near = in_order(branch_near, swap(branch_near, "col"), col, 1)
    first_near = in_order(first_near, swap(first_near, "col"), col, 1)
    first_far, late_far = spine.wait(first_far, late_far)
    first_far = in_order(first_far, swap(first_far, "col"), col, 1)
    half = shared_width // 2
    late_sum = (late[:, : half + pair_width].astype(f32) + late_far[:, : half + pair_width].astype(f32)).astype(bf16)
    shared_part, pair_low = late_sum[:, :half], late_sum[:, half:]
    step_two = in_order(
        late[:, half + pair_width :][:, :head_count],
        late_far[:, half + pair_width :][:, :head_count],
        row,
        1,
    )
    step_all = in_order(step_two, swap(step_two, "col"), col, 1)
    shared_low = in_order(shared_part, swap(shared_part, "col"), col, 1)
    rest = jnp.concatenate([pair_low, shared_part, to_lanes(step_all)], axis=1)
    rest_send = swap_dp(part_of(rest, 1 - near, 1), 1)
    mixed_near_far = spine.wait(mixed_near_far)
    mixed_near = in_order(mixed_near, mixed_near_far, row, 1)
    out_scatter = Scatter(
        spine,
        (outer_sum(mixed_kept, branch_half) + outer_sum(mixed_near, branch_near)).astype(bf16),
        False,
        f32,
    )
    first_far_near, grads_send = spine.wait(first_far_near, grads_send)
    first_far_near = in_order(first_far_near, swap(first_far_near, "col"), col, 1)
    grads_kept = part_of(own_grads, near, 1)
    mixer_scatter_far = Scatter(
        spine,
        (outer_sum(first_far, grads_kept) + outer_sum(first_far_near, grads_send)).astype(bf16),
        True,
    )
    rest_send, hidden = spine.wait(rest_send, hidden)
    hidden_half = swap(hidden, "row")
    hidden_near = swap_dp(near_blocks(hidden, 1 - near), 1)
    cot_near = swap_dp(cotangent, 1)
    mixer_scatter = Scatter(
        spine,
        (
            outer_sum(
                first_half, jnp.concatenate([grads_kept, part_of(rest, near, 1)], axis=1)
            )
            + outer_sum(first_near, jnp.concatenate([grads_send, rest_send], axis=1))
        ).astype(bf16),
        True,
    )

    def both_halves(scattered, sent):
        kept = lax.dynamic_index_in_dim(scattered, near, 0, keepdims=False)
        return jnp.where(near == 0, kept, sent), jnp.where(near == 0, sent, kept)

    def to_neighbour(scattered):
        return swap_dp(lax.dynamic_index_in_dim(scattered, 1 - near, 0, keepdims=False), 1)

    ffn_near = ffn_scatter.finish()
    ffn_near_sent = to_neighbour(ffn_near)
    ffn_far = ffn_scatter_far.finish()
    ffn_far_sent = to_neighbour(ffn_far)
    hidden_half, hidden_near, cot_near, mix_send = spine.wait(
        hidden_half, hidden_near, cot_near, own_grads
    )
    hidden_half = in_order(hidden, hidden_half, row, 1)
    hidden_near_far = swap(hidden_near, "row")
    own_grads_far = swap(mix_send, "row")
    cot_near = in_order(cot_near, swap(cot_near, "col"), col, 1)
    layer_out = (second + sum_cols(product(hidden_half, down_weight), col)).astype(bf16)
    out_scatter.add()
    ffn_far_sent, ffn_near_sent, hidden_near_far = spine.wait(
        ffn_far_sent, ffn_near_sent, hidden_near_far
    )
    hidden_near = in_order(hidden_near, hidden_near_far, row, 1)
    down_scatter = Scatter(
        spine,
        (
            outer_sum(near_blocks(hidden_half, near), cot_half)
            + outer_sum(hidden_near, cot_near)
        ).astype(bf16),
        False,
        f32,
    )
    ffn_near = both_halves(ffn_near, ffn_near_sent)
    ffn_far = swap(jnp.stack(both_halves(ffn_far, ffn_far_sent)), "row")
    out_weight_grad = out_scatter.finish()[0]
    mixer_scatter_far.add()
    mixer_scatter.add()
    own_grads_far = spine.wait(own_grads_far)
    mix_half = in_order(mix_grad, own_grads_far[:, : mix_grad.shape[1]], row, 1)
    query_half = in_order(query_grad, own_grads_far[:, mix_grad.shape[1] :], row, 1)
    first_in_partial = (
        product_back(mix_half, mixer_in)
        + product_back(query_half, query_weight)
        + product_back(pair_low, kv_flat)
        + 0.5 * (product_back(shared_low, bc_weight) + product_back(step_all, step_weight))
    )
    first_in_grad = sum_cols(first_in_partial, col)
    first_total = (attention_total + mixer_total)[:, 0]
    first_total = first_total + swap(first_total, "col")
    first_total_far = swap(first_total, "row")
    conv_shared_sum = conv_shared_part + swap(conv_shared_part, "col")
    conv_shared_far = swap(conv_shared_sum, "row")
    mixer_far = mixer_scatter_far.finish()
    mixer_far_sent = to_neighbour(mixer_far)
    first_total_far, conv_shared_far, ffn_far = spine.wait(first_total_far, conv_shared_far, ffn_far)
    gate_weight_grad = in_order(ffn_near[0], ffn_far[0], row, 1).astype(f32)
    up_weight_grad = in_order(ffn_near[1], ffn_far[1], row, 1).astype(f32)
    input_grad = (
        second_grad
        + norm_first * first_in_grad
        - residual * (first_factor**2 * (first_total + first_total_far) / D)[:, None]
    )
    norm_first_grad = jnp.sum(first_in_grad * residual, axis=0)
    conv_shared_sum = conv_shared_sum + conv_shared_far
    skip_grad = wide_grads[1].reshape(head_count, PM).sum(axis=1)
    pieces = [
        norm_first_grad,
        norm_second_grad,
        conv_inner_grad.reshape(-1),
        conv_shared_sum.reshape(-1),
        wide_grads[0],
        jnp.pad(head_grads[0, :head_count], (0, LANES - head_count)),
        jnp.pad(head_grads[1, :head_count], (0, LANES - head_count)),
        jnp.pad(skip_grad, (0, LANES - head_count)),
    ]
    small = jnp.concatenate(pieces).reshape(-1, LANES)
    bits = dp_bits()
    small_far = swap_dp(small, bits[0])
    mixer_far_sent = spine.wait(mixer_far_sent)
    mixer_far = swap(jnp.concatenate(both_halves(mixer_far, mixer_far_sent), axis=1), "row")
    mixer_near = mixer_scatter.finish()
    mixer_near_sent = to_neighbour(mixer_near)
    small = small + spine.wait(small_far)
    small_far = swap_dp(small, bits[1])
    down_scatter.add()
    small = small + spine.wait(small_far)
    small_far = swap_dp(small, bits[2])
    mixer_near_sent, mixer_far = spine.wait(mixer_near_sent, mixer_far)
    mixer_near = both_halves(mixer_near, mixer_near_sent)
    kept_width = grads_kept.shape[1]
    mix_width = mix_grad.shape[1]
    own_sums = jnp.concatenate([mixer_near[0][:, :kept_width], mixer_near[1][:, :kept_width]], axis=1)
    rest_sums = jnp.concatenate(
        [mixer_near[0][:, kept_width:], mixer_near[1][:, kept_width:]], axis=1
    ).astype(f32)
    mixer_in_grad = in_order(own_sums[:, :mix_width], mixer_far[:, :mix_width], row, 1).astype(f32)
    query_weight_grad = in_order(
        own_sums[:, mix_width:], mixer_far[:, mix_width:], row, 1
    ).astype(f32)
    kv_weight_grad = rest_sums[:, :pair_width].reshape((-1,) + kv_weight.shape[1:])
    place = pair_width
    bc_own = rest_sums[:, place : place + shared_width // 2].astype(bf16)
    bc_weight_grad = in_order(bc_own, swap(bc_own, "col"), col, 1).astype(f32)
    place += shared_width // 2
    step_weight_grad = rest_sums[:, place : place + step_weight.shape[1]]
    for bit in bits[3:]:
        small = small + spine.wait(small_far)
        small_far = swap_dp(small, bit)
    small = small + spine.wait(small_far)
    down_weight_grad = down_scatter.finish()[0]
    small = small.reshape(-1)
    sums, place = [], 0
    for piece in pieces:
        sums.append(small[place : place + piece.shape[0]])
        place += piece.shape[0]

    def own_block(values_in, axis):
        size = values_in.shape[axis] // count
        return lax.dynamic_slice_in_dim(values_in, me * size, size, axis)

    return (
        layer_out,
        input_grad,
        own_block(sums[0], 0),
        mixer_in_grad,
        query_weight_grad,
        bc_weight_grad,
        step_weight_grad,
        kv_weight_grad,
        own_block(sums[2].reshape(conv_inner.shape), 1),
        own_block(sums[3].reshape(conv_shared.shape), 1),
        sums[5][:head_count],
        sums[6][:head_count],
        sums[7][:head_count],
        own_block(sums[4], 0),
        out_weight_grad,
        own_block(sums[1], 0),
        gate_weight_grad,
        up_weight_grad,
        down_weight_grad,
    )


def solution(mesh):
    in_specs = (
        P("dp", ("row", "col")),
        P(("row", "col")),
        P("row", "col"),
        P("row", "col"),
        P("row", None),
        P("row", None),
        P("row", "col", None),
        P(None, ("col", "row")),
        P(),
        P(("col", "row")),
        P(("col", "row")),
        P(("col", "row")),
        P(("col", "row")),
        P("col", "row"),
        P(("row", "col")),
        P("row", "col"),
        P("row", "col"),
        P("col", "row"),
        P("dp", ("row", "col")),
    )
    out_specs = (
        P("dp", ("row", "col")),
        P("dp", ("row", "col")),
        P(("row", "col", "dp")),
        P(("row", "dp"), "col"),
        P(("row", "dp"), "col"),
        P(("row", "dp"), None),
        P(("row", "dp"), None),
        P(("row", "dp"), "col", None),
        P(None, ("col", "row", "dp")),
        P(None, "dp"),
        P(("col", "row")),
        P(("col", "row")),
        P(("col", "row")),
        P(("col", "row", "dp")),
        P(("col", "dp"), "row"),
        P(("row", "col", "dp")),
        P(("row", "dp"), "col"),
        P(("row", "dp"), "col"),
        P(("col", "dp"), "row"),
    )
    return jax.shard_map(local, mesh=mesh, in_specs=in_specs, out_specs=out_specs, check_vma=False)
```

```python
from functools import partial
import math

import jax
import jax.numpy as jnp
from jax import lax
from jax.experimental import pallas as pl
from jax.experimental.pallas import tpu as pltpu
from jax.sharding import PartitionSpec as P

D = 2048
HM = 48
PM = 64
NS = 256
HD = 128
MIX = 4096
LANES = 128
CHUNK = 128

norm_epsilon = 1e-05
rope_base = 10000.0
highest = lax.Precision.HIGHEST
f32 = jnp.float32
bf16 = jnp.bfloat16
VMEM_LIMIT = 56 * 1024 * 1024


def product(left_side, right_side):
    return jnp.dot(left_side, right_side, preferred_element_type=f32)


def product_back(left_side, right_side):
    return lax.dot_general(
        left_side, right_side, (((1,), (1,)), ((), ())), preferred_element_type=f32
    )


def outer_sum(left_side, right_side):
    return lax.dot_general(
        left_side, right_side, (((0,), (0,)), ((), ())), preferred_element_type=f32
    )


def swap(values_in, axis):
    return lax.ppermute(values_in, axis, [(0, 1), (1, 0)])


def in_order(own, other, place, axis):
    return jnp.concatenate(
        [jnp.where(place == 0, own, other), jnp.where(place == 0, other, own)], axis=axis
    )


def part_of(values_in, place, axis):
    size = values_in.shape[axis] // 2
    return lax.dynamic_slice_in_dim(values_in, place * size, size, axis)


def rows_total(values_in):
    values_in = values_in + swap(values_in, "col")
    return values_in + swap(values_in, "row")


def sum_cols(values_in, col):
    sent = swap(part_of(values_in, 1 - col, 1).astype(bf16), "col")
    return part_of(values_in, col, 1) + sent.astype(f32)


def near_blocks(values_in, near):
    size = MIX // 2 // lax.axis_size("dp")
    places = range(0, values_in.shape[1], 2 * size)
    return jnp.concatenate(
        [
            jnp.where(
                near == 0,
                values_in[:, place : place + size],
                values_in[:, place + size : place + 2 * size],
            )
            for place in places
        ],
        axis=1,
    )


def dp_bits():
    bits, bit = [], 1
    while bit < lax.axis_size("dp"):
        bits.append(bit)
        bit *= 2
    return bits


def swap_dp(values_in, bit):
    return lax.ppermute(values_in, "dp", [(i, i ^ bit) for i in range(lax.axis_size("dp"))])


def tie(*values_in):
    return lax.optimization_barrier(values_in)


class Spine:
    def __init__(self, token):
        self.token = token

    def wait(self, *values_in):
        tied = tie(self.token, *values_in)
        self.token = tied[0]
        return tied[1] if len(tied) == 2 else tied[1:]


class Scatter:
    def __init__(self, spine, grads, pairs, dtype=bf16):
        self.spine, self.dtype = spine, dtype
        self.bits = dp_bits()[1:]
        blocks = lax.axis_size("dp") // 2 * (2 if pairs else 1)
        rest = (blocks // 2 ** len(self.bits), grads.shape[0] // blocks) + grads.shape[1:]
        self.left = self.bits[::-1]
        self.parts = grads.reshape((2,) * len(self.bits) + rest)
        self.send()

    def send(self):
        bit = self.bits[len(self.bits) - len(self.left)]
        axis = self.left.index(bit)
        mine = (lax.axis_index("dp") // bit) % 2
        send = lax.dynamic_index_in_dim(self.parts, 1 - mine, axis, keepdims=False)
        self.parts = lax.dynamic_index_in_dim(self.parts, mine, axis, keepdims=False)
        self.arrived = swap_dp(send, bit)
        self.left.pop(axis)

    def add(self):
        arrived = self.spine.wait(self.arrived)
        total = self.parts.astype(f32) + arrived.astype(f32)
        self.parts = total.astype(bf16 if self.left else self.dtype)
        if self.left:
            self.send()

    def finish(self):
        while self.left:
            self.add()
        self.add()
        return self.parts


def place_kernel(count, owners, where_ref, *refs):
    pieces, out_ref = refs[:count], refs[count]
    rows = pieces[0].shape[0]
    for turn in range(count):
        start = pl.multiple_of((where_ref[0] ^ owners[turn]) * rows, rows)
        out_ref[pl.ds(start, rows), :] = pieces[turn][...]


def place_pieces(pieces, owners):
    count = len(pieces)
    rows, columns = pieces[0].shape
    return pl.pallas_call(
        partial(place_kernel, count, owners),
        out_shape=jax.ShapeDtypeStruct((count * rows, columns), pieces[0].dtype),
        in_specs=[pl.BlockSpec(memory_space=pltpu.SMEM)]
        + [pl.BlockSpec(memory_space=pltpu.VMEM)] * count,
        out_specs=pl.BlockSpec(memory_space=pltpu.VMEM),
        compiler_params=pltpu.CompilerParams(vmem_limit_bytes=VMEM_LIMIT),
        cost_estimate=pl.CostEstimate(
            flops=0, bytes_accessed=4 * count * rows * columns, transcendentals=0
        ),
    )(lax.axis_index("dp").astype(jnp.int32)[None], *pieces)


class Spread:
    def __init__(self, mine):
        self.pieces, self.owners = [mine], [0]
        self.bits = [dp_bits()[::-1]]
        self.first = 0

    def wait(self, spine):
        arrived = spine.wait(*self.pieces[self.first :])
        self.pieces[self.first :] = arrived if isinstance(arrived, (tuple, list)) else [arrived]

    def level(self):
        start, self.first = self.first, len(self.pieces)
        sends = [
            (-bit, turn) for turn in range(start, self.first) for bit in self.bits[turn]
        ]
        for bit, turn in sorted(sends):
            self.pieces.append(swap_dp(self.pieces[turn], -bit))
            self.owners.append(self.owners[turn] ^ -bit)
            self.bits.append([lower for lower in self.bits[turn] if lower < -bit])

    def finish(self, spine):
        self.wait(spine)
        while len(self.pieces) < lax.axis_size("dp"):
            self.level()
            self.wait(spine)
        return place_pieces(self.pieces, self.owners)


def sigmoid(values_in):
    return 1.0 / (1.0 + jnp.exp(-values_in))


def softplus(values_in):
    return jnp.maximum(values_in, 0.0) + jnp.log1p(jnp.exp(-jnp.abs(values_in)))


def low_lanes():
    return lax.broadcasted_iota(jnp.int32, (1, LANES), 1) < PM


def pair_columns(values_in, pair):
    return jnp.where(
        low_lanes(), values_in[:, 2 * pair : 2 * pair + 1], values_in[:, 2 * pair + 1 : 2 * pair + 2]
    )


def shift_down(values_in, count):
    if count == 0:
        return values_in
    rows = lax.broadcasted_iota(jnp.int32, values_in.shape, 0)
    return jnp.where(rows >= count, pltpu.roll(values_in, count, 0), 0.0)


def shift_up(values_in, count):
    if count == 0:
        return values_in
    length = values_in.shape[0]
    rows = lax.broadcasted_iota(jnp.int32, values_in.shape, 0)
    return jnp.where(rows < length - count, pltpu.roll(values_in, length - count, 0), 0.0)


def conv(values_in, taps):
    count = taps.shape[0]
    total = values_in * taps[count - 1 : count, :]
    for tap in range(count - 1):
        total = total + taps[tap : tap + 1, :] * shift_down(values_in, count - 1 - tap)
    return total


def conv_back(grad, values_in, taps):
    count = taps.shape[0]
    total = grad * taps[count - 1 : count, :]
    for tap in range(count - 1):
        total = total + taps[tap : tap + 1, :] * shift_up(grad, count - 1 - tap)
    tap_grads = [
        jnp.sum(grad * shift_down(values_in, count - 1 - tap), axis=0, keepdims=True)
        for tap in range(count)
    ]
    return total, tap_grads


def stacked_pair(values_in):
    low = low_lanes()
    return jnp.concatenate(
        [jnp.where(low, values_in, 0.0), jnp.where(low, 0.0, values_in)], axis=0
    ).astype(bf16)


def lower_mask():
    rows = lax.broadcasted_iota(jnp.int32, (CHUNK, CHUNK), 0)
    columns = lax.broadcasted_iota(jnp.int32, (CHUNK, CHUNK), 1)
    return (rows >= columns).astype(f32)


def mixer_forward_kernel(
    own_ref,
    other_ref,
    factor_ref,
    shared_ref,
    step_ref,
    conv_inner_ref,
    conv_shared_ref,
    head_ref,
    skip_ref,
    gain_ref,
    attended_ref,
    mixed_ref,
    square_ref,
    mix_ref,
    ssm_ref,
    states_ref,
    inner_buf,
    gate_buf,
    maps_buf,
    step_buf,
    decay_buf,
    weighted_buf,
    state_buf,
):
    pairs = ssm_ref.shape[1] // LANES
    length = own_ref.shape[0]
    groups = attended_ref.shape[1] // HD
    group_pairs = pairs // groups
    low = low_lanes()
    factor = factor_ref[...]
    for group in range(groups):
        place = ((group + 1) * group_pairs + group) * LANES
        mixed_ref[:, place : place + HD] = attended_ref[:, group * HD : (group + 1) * HD]
    for pair in range(pairs):
        first = slice(2 * pair * LANES, (2 * pair + 1) * LANES)
        second = slice((2 * pair + 1) * LANES, (2 * pair + 2) * LANES)
        own = slice(pair * LANES, (pair + 1) * LANES)
        head_a = (own_ref[:, first] + other_ref[:, first].astype(f32)) * factor
        head_b = (own_ref[:, second] + other_ref[:, second].astype(f32)) * factor
        mix_ref[:, first] = head_a
        mix_ref[:, second] = head_b
        taken = jnp.where(low, pltpu.roll(head_a, PM, 1), head_b)
        gate_buf[:, own] = jnp.where(low, head_a, pltpu.roll(head_b, PM, 1))
        taken = conv(taken, conv_inner_ref[:, own])
        inner_buf[:, own] = taken * sigmoid(taken)
    for block in range(shared_ref.shape[1] // LANES):
        own = slice(block * LANES, (block + 1) * LANES)
        taken = conv(shared_ref[:, own], conv_shared_ref[:, own])
        maps_buf[:, own] = (taken * sigmoid(taken)).astype(bf16)
    steps = softplus(step_ref[...] + head_ref[1:2, :])
    step_buf[...] = steps
    decay_buf[...] = -jnp.exp(head_ref[0:1, :]) * steps
    state_buf[...] = jnp.zeros_like(state_buf)
    mask = lower_mask()

    def chunk(index, carry):
        rows = pl.ds(pl.multiple_of(index * CHUNK, CHUNK), CHUNK)
        running = jnp.dot(mask, decay_buf[rows, :], precision=highest, preferred_element_type=f32)
        running_t = running.T
        step = step_buf[rows, :]
        step_t = step.T
        last = running[CHUNK - 1 : CHUNK, :]
        grown = jnp.exp(running)
        tail = jnp.exp(last - running) * step
        grown_last = jnp.exp(last)
        basis = maps_buf[rows, 0:NS]
        read = maps_buf[rows, NS : 2 * NS]
        gram = product_back(read, basis)
        state_low = state_buf[...].astype(bf16)
        states_ref[pl.ds(pl.multiple_of(index * NS, NS), NS), :] = state_low
        carried = product(read, state_low)
        square = jnp.zeros((CHUNK, 1), f32)
        for pair in range(pairs):
            own = slice(pair * LANES, (pair + 1) * LANES)
            inner = inner_buf[rows, own]
            mixing = []
            for head in (2 * pair, 2 * pair + 1):
                spread = jnp.exp(
                    jnp.minimum(running[:, head : head + 1] - running_t[head : head + 1, :], 0.0)
                )
                mixing.append(
                    (gram * spread * mask * step_t[head : head + 1, :]).astype(bf16)
                )
            ssm = product(jnp.concatenate(mixing, axis=1), stacked_pair(inner))
            ssm = ssm + pair_columns(grown, pair) * carried[:, own] + skip_ref[:, own] * inner
            ssm_ref[rows, own] = ssm
            weighted_buf[:, own] = (pair_columns(tail, pair) * inner).astype(bf16)
            gate = gate_buf[rows, own]
            gated = ssm * gate * sigmoid(gate)
            square = square + jnp.sum(gated * gated, axis=1, keepdims=True)
            place = pair * LANES + (pair // group_pairs) * HD
            mixed_ref[rows, place : place + LANES] = (gated * gain_ref[:, own]).astype(bf16)
        square_ref[rows, :] = square
        fresh = outer_sum(basis, weighted_buf[...])
        for pair in range(pairs):
            own = slice(pair * LANES, (pair + 1) * LANES)
            state_buf[:, own] = (
                pair_columns(grown_last, pair) * state_buf[:, own] + fresh[:, own]
            )
        return carry

    lax.fori_loop(0, length // CHUNK, chunk, 0)


def mixer_backward_kernel(
    mix_ref,
    ssm_ref,
    states_ref,
    shared_ref,
    step_ref,
    conv_inner_ref,
    conv_shared_ref,
    head_ref,
    skip_ref,
    gain_ref,
    lanes_ref,
    grad_ref,
    group_factor_ref,
    group_scale_ref,
    factor_ref,
    query_grad_ref,
    mix_grad_ref,
    shared_grad_ref,
    step_grad_ref,
    inner_taps_ref,
    shared_taps_ref,
    head_grad_ref,
    wide_grad_ref,
    total_ref,
    taken_buf,
    inner_buf,
    maps_buf,
    step_buf,
    decay_buf,
    weighted_buf,
    grown_buf,
    inner_grad_buf,
    maps_grad_buf,
    sums_buf,
    state_grad_buf,
):
    pairs = ssm_ref.shape[1] // LANES
    length = ssm_ref.shape[0]
    group_pairs = pairs // (grad_ref.shape[1] // (pairs * LANES // 2 + HD))
    low = low_lanes()
    mix_grad_ref[:, 2 * pairs * LANES :] = query_grad_ref[...]
    for pair in range(pairs):
        first = slice(2 * pair * LANES, (2 * pair + 1) * LANES)
        second = slice((2 * pair + 1) * LANES, (2 * pair + 2) * LANES)
        own = slice(pair * LANES, (pair + 1) * LANES)
        taken = jnp.where(low, pltpu.roll(mix_ref[:, first], PM, 1), mix_ref[:, second])
        taken_buf[:, own] = taken
        taken = conv(taken, conv_inner_ref[:, own])
        inner_buf[:, own] = taken * sigmoid(taken)
    for block in range(shared_ref.shape[1] // LANES):
        own = slice(block * LANES, (block + 1) * LANES)
        taken = conv(shared_ref[:, own], conv_shared_ref[:, own])
        maps_buf[:, own] = (taken * sigmoid(taken)).astype(bf16)
    shifted = step_ref[...] + head_ref[1:2, :]
    steps = softplus(shifted)
    rate = -jnp.exp(head_ref[0:1, :])
    step_buf[...] = steps
    decay_buf[...] = rate * steps
    state_grad_buf[...] = jnp.zeros_like(state_grad_buf)
    head_grad_ref[...] = jnp.zeros_like(head_grad_ref)
    wide_grad_ref[...] = jnp.zeros_like(wide_grad_ref)
    mask = lower_mask()
    chunks = length // CHUNK
    lane_index = lax.broadcasted_iota(jnp.int32, (1, LANES), 1)

    def chunk(turn, carry):
        index = chunks - 1 - turn
        rows = pl.ds(pl.multiple_of(index * CHUNK, CHUNK), CHUNK)
        running = jnp.dot(mask, decay_buf[rows, :], precision=highest, preferred_element_type=f32)
        running_t = running.T
        step = step_buf[rows, :]
        step_t = step.T
        last = running[CHUNK - 1 : CHUNK, :]
        grown = jnp.exp(running)
        fading = jnp.exp(last - running)
        grown_last = jnp.exp(last)
        basis = maps_buf[rows, 0:NS]
        read = maps_buf[rows, NS : 2 * NS]
        gram = product_back(read, basis)
        state_low = states_ref[pl.ds(pl.multiple_of(index * NS, NS), NS), :]
        carried = product(read, state_low)
        state_grad_low = state_grad_buf[...].astype(bf16)
        weighted_grad = product(basis, state_grad_low)
        gram_grad = jnp.zeros((CHUNK, CHUNK), f32)
        decay_grad = jnp.zeros((CHUNK, LANES), f32)
        column_grads = []
        total = jnp.zeros((CHUNK, 1), f32)
        group_factor = group_factor_ref[rows, :]
        group_scale = group_scale_ref[rows, :]
        factor = factor_ref[rows, :]
        for pair in range(pairs):
            first = slice(2 * pair * LANES, (2 * pair + 1) * LANES)
            second = slice((2 * pair + 1) * LANES, (2 * pair + 2) * LANES)
            own = slice(pair * LANES, (pair + 1) * LANES)
            place = pair * LANES + (pair // group_pairs) * HD
            incoming = grad_ref[rows, place : place + LANES]
            head_a = mix_ref[rows, first]
            head_b = mix_ref[rows, second]
            gate = jnp.where(low, head_a, pltpu.roll(head_b, PM, 1))
            gate_sigmoid = sigmoid(gate)
            gate_act = gate * gate_sigmoid
            ssm = ssm_ref[rows, own]
            gated = ssm * gate_act
            wide_grad_ref[0:1, own] += jnp.sum(
                incoming * gated * group_factor, axis=0, keepdims=True
            )
            gated_grad = group_factor * gain_ref[:, own] * incoming - gated * group_scale
            gate_grad = gated_grad * ssm * gate_sigmoid * (1.0 + gate * (1.0 - gate_sigmoid))
            ssm_grad = gated_grad * gate_act
            inner = inner_buf[rows, own]
            wide_grad_ref[1:2, own] += jnp.sum(ssm_grad * inner, axis=0, keepdims=True)
            gate_b = pltpu.roll(gate_grad, PM, 1)
            total = total + jnp.sum(gate_grad * gate, axis=1, keepdims=True)
            mix_grad_ref[rows, first] = jnp.where(low, gate_grad * factor, 0.0).astype(bf16)
            mix_grad_ref[rows, second] = jnp.where(low, gate_b * factor, 0.0).astype(bf16)
            grad_low = ssm_grad.astype(bf16)
            mixing_grad = product_back(grad_low, stacked_pair(inner))
            spreads = []
            for side, head in enumerate((2 * pair, 2 * pair + 1)):
                spread = mask * jnp.exp(
                    jnp.minimum(running[:, head : head + 1] - running_t[head : head + 1, :], 0.0)
                )
                step_row = step_t[head : head + 1, :]
                spread_gram = gram * spread
                spreads.append(spread_gram.astype(bf16))
                own_grad = mixing_grad[:, side * CHUNK : (side + 1) * CHUNK] * step_row
                gram_grad = gram_grad + own_grad * spread
                moved = own_grad * spread_gram
                decay_grad = decay_grad + jnp.where(
                    lane_index == head, jnp.sum(moved, axis=1, keepdims=True), 0.0
                )
                column_grads.append(jnp.sum(moved, axis=0, keepdims=True))
            within = outer_sum(jnp.concatenate(spreads, axis=0), stacked_pair(ssm_grad))
            fading_grad = pair_columns(fading, pair) * weighted_grad[:, own]
            spread_grad = within + fading_grad
            step_wide = pair_columns(step, pair)
            inner_grad_buf[rows, own] = step_wide * spread_grad + skip_ref[:, own] * ssm_grad
            grown_grad = pair_columns(grown, pair) * ssm_grad
            grown_buf[:, own] = grown_grad.astype(bf16)
            weighted_buf[:, own] = (pair_columns(fading, pair) * step_wide * inner).astype(bf16)
            sums_buf[0:CHUNK, own] = (inner * spread_grad).astype(bf16)
            sums_buf[CHUNK : 2 * CHUNK, own] = (inner * fading_grad * step_wide).astype(bf16)
            sums_buf[2 * CHUNK : 3 * CHUNK, own] = (grown_grad * carried[:, own]).astype(bf16)
        head_sums = product(sums_buf[...], lanes_ref[...])
        step_part = head_sums[0:CHUNK, :]
        fading_part = head_sums[CHUNK : 2 * CHUNK, :]
        grown_part = head_sums[2 * CHUNK : 3 * CHUNK, :]
        fill = jnp.zeros((CHUNK - len(column_grads), CHUNK), f32)
        column_grad = jnp.concatenate(column_grads + [fill], axis=0).T
        decay_grad = decay_grad - column_grad + grown_part - fading_part
        state_part = jnp.zeros((1, LANES), f32)
        grown_low = grown_buf[...]
        fresh = outer_sum(read, grown_low)
        for pair in range(pairs):
            own = slice(pair * LANES, (pair + 1) * LANES)
            state_grad = state_grad_buf[:, own]
            held = jnp.sum(state_grad * state_low[:, own].astype(f32), axis=0, keepdims=True)
            for side, head in enumerate((2 * pair, 2 * pair + 1)):
                kept = jnp.where(low if side == 0 else jnp.logical_not(low), held, 0.0)
                state_part = state_part + jnp.where(
                    lane_index == head, jnp.sum(kept, axis=1, keepdims=True), 0.0
                )
            state_grad_buf[:, own] = pair_columns(grown_last, pair) * state_grad + fresh[:, own]
        last_grad = jnp.sum(fading_part, axis=0, keepdims=True) + grown_last * state_part
        decay_sum = (
            lax.dot_general(
                mask,
                decay_grad,
                (((0,), (0,)), ((), ())),
                precision=highest,
                preferred_element_type=f32,
            )
            + last_grad
        )
        raw_shift = step_ref[rows, :] + head_ref[1:2, :]
        raw_grad = (step_part + decay_sum * rate) * sigmoid(raw_shift)
        head_grad_ref[0:1, :] += jnp.sum(decay_sum * decay_buf[rows, :], axis=0, keepdims=True)
        head_grad_ref[1:2, :] += jnp.sum(raw_grad, axis=0, keepdims=True)
        step_grad_ref[rows, :] = (raw_grad * factor).astype(bf16)
        total = total + jnp.sum(raw_grad * step_ref[rows, :], axis=1, keepdims=True)
        total_ref[rows, :] = total
        gram_low = gram_grad.astype(bf16)
        maps_grad_buf[rows, 0:NS] = outer_sum(gram_low, read) + product_back(
            weighted_buf[...], state_grad_low
        )
        maps_grad_buf[rows, NS : 2 * NS] = product(gram_low, basis) + product_back(
            grown_low, state_low
        )
        return carry

    lax.fori_loop(0, chunks, chunk, 0)
    factor = factor_ref[...]
    total = total_ref[...]
    for pair in range(pairs):
        first = slice(2 * pair * LANES, (2 * pair + 1) * LANES)
        second = slice((2 * pair + 1) * LANES, (2 * pair + 2) * LANES)
        own = slice(pair * LANES, (pair + 1) * LANES)
        taken = taken_buf[:, own]
        taps = conv_inner_ref[:, own]
        before = conv(taken, taps)
        before_sigmoid = sigmoid(before)
        grad = inner_grad_buf[:, own] * before_sigmoid * (1.0 + before * (1.0 - before_sigmoid))
        grad, tap_grads = conv_back(grad, taken, taps)
        for tap, tap_grad in enumerate(tap_grads):
            inner_taps_ref[tap : tap + 1, own] = tap_grad
        total = total + jnp.sum(grad * taken, axis=1, keepdims=True)
        grad = grad * factor
        low_a = mix_grad_ref[:, first].astype(f32)
        low_b = mix_grad_ref[:, second].astype(f32)
        mix_grad_ref[:, first] = jnp.where(low, low_a, pltpu.roll(grad, PM, 1)).astype(bf16)
        mix_grad_ref[:, second] = jnp.where(low, low_b, grad).astype(bf16)
    for block in range(shared_ref.shape[1] // LANES):
        own = slice(block * LANES, (block + 1) * LANES)
        taken = shared_ref[:, own]
        taps = conv_shared_ref[:, own]
        before = conv(taken, taps)
        before_sigmoid = sigmoid(before)
        grad = maps_grad_buf[:, own] * before_sigmoid * (1.0 + before * (1.0 - before_sigmoid))
        grad, tap_grads = conv_back(grad, taken, taps)
        for tap, tap_grad in enumerate(tap_grads):
            shared_taps_ref[tap : tap + 1, own] = tap_grad
        total = total + jnp.sum(grad * taken, axis=1, keepdims=True)
        shared_grad_ref[:, own] = (grad * factor).astype(bf16)
    total_ref[...] = total


def call(kernel, outs, scratch, flops, *operands):
    return pl.pallas_call(
        kernel,
        out_shape=outs,
        in_specs=[pl.BlockSpec(memory_space=pltpu.VMEM)] * len(operands),
        out_specs=[pl.BlockSpec(memory_space=pltpu.VMEM)] * len(outs),
        scratch_shapes=scratch,
        compiler_params=pltpu.CompilerParams(vmem_limit_bytes=VMEM_LIMIT),
        cost_estimate=pl.CostEstimate(flops=flops, bytes_accessed=10**6, transcendentals=0),
    )(*operands)


def shape(dims, dtype=f32):
    return jax.ShapeDtypeStruct(dims, dtype)


def mixer_forward(
    own, other, factor, shared, step, taps, shared_taps, heads, skip, gain, attended
):
    length, width = own.shape
    channels = width // 2
    chunks = length // CHUNK
    return call(
        mixer_forward_kernel,
        [
            shape((length, channels + attended.shape[1]), bf16),
            shape((length, 1)),
            shape((length, width)),
            shape((length, channels)),
            shape((chunks * NS, channels), bf16),
        ],
        [
            pltpu.VMEM((length, channels), f32),
            pltpu.VMEM((length, channels), f32),
            pltpu.VMEM((length, 2 * NS), bf16),
            pltpu.VMEM((length, LANES), f32),
            pltpu.VMEM((length, LANES), f32),
            pltpu.VMEM((CHUNK, channels), bf16),
            pltpu.VMEM((NS, channels), f32),
        ],
        10**8,
        own, other, factor, shared, step, taps, shared_taps, heads, skip, gain, attended,
    )


def mixer_backward(
    mix, ssm, states, shared, step, taps, shared_taps, heads, skip, gain, lanes, grad,
    group_factor, group_scale, factor, query_grad,
):
    length, width = mix.shape
    channels = width // 2
    return call(
        mixer_backward_kernel,
        [
            shape((length, width + query_grad.shape[1]), bf16),
            shape((length, 2 * NS), bf16),
            shape((length, LANES), bf16),
            shape((taps.shape[0], channels)),
            shape((taps.shape[0], 2 * NS)),
            shape((8, LANES)),
            shape((8, channels)),
            shape((length, 1)),
        ],
        [
            pltpu.VMEM((length, channels), f32),
            pltpu.VMEM((length, channels), f32),
            pltpu.VMEM((length, 2 * NS), bf16),
            pltpu.VMEM((length, LANES), f32),
            pltpu.VMEM((length, LANES), f32),
            pltpu.VMEM((CHUNK, channels), bf16),
            pltpu.VMEM((CHUNK, channels), bf16),
            pltpu.VMEM((length, channels), f32),
            pltpu.VMEM((length, 2 * NS), f32),
            pltpu.VMEM((3 * CHUNK, channels), bf16),
            pltpu.VMEM((NS, channels), f32),
        ],
        10**8,
        mix, ssm, states, shared, step, taps, shared_taps, heads, skip, gain, lanes, grad,
        group_factor, group_scale, factor, query_grad,
    )


def rotated(values_in, cosine, sine):
    return values_in * cosine + pltpu.roll(values_in, HD // 2, 1) * sine


def rotated_back(grad, cosine, sine):
    return grad * cosine + pltpu.roll(grad * sine, HD // 2, 1)


def attention_forward_kernel(query_ref, pair_ref, cosine_ref, sine_ref, out_ref):
    length = query_ref.shape[0]
    scale = 1.0 / math.sqrt(HD)
    block = min(256, length)
    keys = rotated(pair_ref[:, :HD], cosine_ref[...], sine_ref[...]).astype(bf16)
    vals = pair_ref[:, HD:].astype(bf16)
    for head in range(query_ref.shape[1] // HD):
        lanes = slice(head * HD, (head + 1) * HD)
        queries = rotated(query_ref[:, lanes], cosine_ref[...], sine_ref[...]).astype(bf16)
        for start in range(0, length, block):
            end = start + block
            scores = product_back(queries[start:end], keys[:end]) * scale
            rows = start + lax.broadcasted_iota(jnp.int32, (block, end), 0)
            columns = lax.broadcasted_iota(jnp.int32, (block, end), 1)
            scores = jnp.where(columns <= rows, scores, -1e30)
            exponent = jnp.exp(scores - jnp.max(scores, axis=1, keepdims=True))
            probs = exponent * (1.0 / jnp.sum(exponent, axis=1, keepdims=True))
            out_ref[start:end, lanes] = product(probs.astype(bf16), vals[:end]).astype(bf16)


def attention_backward_kernel(
    query_ref, pair_ref, cosine_ref, sine_ref, grad_ref, factor_ref,
    query_grad_ref, pair_grad_ref, total_ref, key_buf, val_buf,
):
    length = query_ref.shape[0]
    scale = 1.0 / math.sqrt(HD)
    block = min(256, length)
    cosine, sine = cosine_ref[...], sine_ref[...]
    keys = rotated(pair_ref[:, :HD], cosine, sine).astype(bf16)
    vals = pair_ref[:, HD:].astype(bf16)
    heads = query_ref.shape[1] // HD
    group = grad_ref.shape[1] // heads
    key_buf[...] = jnp.zeros_like(key_buf)
    val_buf[...] = jnp.zeros_like(val_buf)
    for head in range(heads):
        lanes = slice(head * HD, (head + 1) * HD)
        queries = rotated(query_ref[:, lanes], cosine, sine).astype(bf16)
        incoming = grad_ref[:, (head + 1) * group - HD : (head + 1) * group].astype(bf16)
        for start in range(0, length, block):
            end = start + block
            scores = product_back(queries[start:end], keys[:end]) * scale
            rows = start + lax.broadcasted_iota(jnp.int32, (block, end), 0)
            columns = lax.broadcasted_iota(jnp.int32, (block, end), 1)
            scores = jnp.where(columns <= rows, scores, -1e30)
            exponent = jnp.exp(scores - jnp.max(scores, axis=1, keepdims=True))
            probs = exponent * (1.0 / jnp.sum(exponent, axis=1, keepdims=True))
            grad_low = incoming[start:end]
            val_buf[:end, :] += outer_sum(probs.astype(bf16), grad_low)
            probs_grad = product_back(grad_low, vals[:end])
            inner = jnp.sum(probs * probs_grad, axis=1, keepdims=True)
            scores_grad = (probs * (probs_grad - inner) * scale).astype(bf16)
            query_grad = rotated_back(
                product(scores_grad, keys[:end]), cosine[start:end], sine[start:end]
            )
            key_buf[:end, :] += outer_sum(scores_grad, queries[start:end])
            taken = query_ref[start:end, lanes]
            part = jnp.sum(query_grad * taken, axis=1, keepdims=True)
            if head == 0:
                total_ref[start:end, :] = part
            else:
                total_ref[start:end, :] += part
            query_grad_ref[start:end, lanes] = (query_grad * factor_ref[start:end, :]).astype(bf16)
    key_grad = rotated_back(key_buf[...], cosine, sine)
    val_grad = val_buf[...]
    total_ref[...] += jnp.sum(
        key_grad * pair_ref[:, :HD] + val_grad * pair_ref[:, HD:], axis=1, keepdims=True
    )
    pair_grad_ref[:, :HD] = (key_grad * factor_ref[...]).astype(bf16)
    pair_grad_ref[:, HD:] = (val_grad * factor_ref[...]).astype(bf16)


def attention_forward(query, pair, cosine, sine):
    return call(
        attention_forward_kernel, [shape(query.shape, bf16)], [], 10**8,
        query, pair, cosine, sine,
    )[0]


def attention_backward(query, pair, cosine, sine, grad, factor):
    length = query.shape[0]
    return call(
        attention_backward_kernel,
        [shape(query.shape, bf16), shape(pair.shape, bf16), shape((length, 1))],
        [pltpu.VMEM((length, HD), f32), pltpu.VMEM((length, HD), f32)],
        10**8,
        query, pair, cosine, sine, grad, factor,
    )


def rope_tables(length):
    half = HD // 2
    inverse = rope_base ** (-jnp.arange(half, dtype=f32) * 2.0 / HD)
    angles = jnp.arange(length, dtype=f32)[:, None] * inverse[None, :]
    cosine, sine = jnp.cos(angles), jnp.sin(angles)
    return jnp.concatenate([cosine, cosine], axis=1), jnp.concatenate([-sine, sine], axis=1)


def to_lanes(values_in):
    return jnp.pad(values_in, ((0, 0), (0, LANES - values_in.shape[1])))


def local(
    tokens,
    norm_first,
    mixer_in,
    query_weight,
    bc_weight,
    step_weight,
    kv_weight,
    conv_inner,
    conv_shared,
    log_rate,
    step_bias,
    skip_gain,
    group_gain,
    out_weight,
    norm_second,
    gate_weight,
    up_weight,
    down_weight,
    cotangent,
):
    length = tokens.shape[0]
    row = lax.axis_index("row")
    col = lax.axis_index("col")
    me = lax.axis_index("dp")
    count = lax.axis_size("dp")
    near = me % 2
    quarter = col * 2 + row
    head_count = log_rate.shape[0]
    channels = group_gain.shape[0]
    kv_flat = kv_weight.reshape(kv_weight.shape[0], -1)
    residual = tokens.astype(f32)
    spine = Spine(jnp.zeros((1, LANES), f32))

    def column_share(weight):
        rows, columns = weight.shape[0] // count, weight.shape[1] // 2
        return lax.dynamic_slice(weight, (me * rows, (1 - row) * columns), (rows, columns))

    half_rows = out_weight.shape[0] // 2
    share_rows = half_rows // count
    out_own = part_of(out_weight, row, 0)
    gate_own, up_own = part_of(gate_weight, row, 1), part_of(up_weight, row, 1)
    out_share = lax.dynamic_slice_in_dim(
        out_weight, (1 - row) * half_rows + me * share_rows, share_rows, 0
    )
    ffn_share = jnp.concatenate([column_share(gate_weight), column_share(up_weight)], axis=1)
    out_spread = Spread(swap(out_share, "row"))
    ffn_spread = Spread(swap(ffn_share, "row"))

    first_own = (residual * norm_first).astype(bf16)
    first_half = in_order(first_own, swap(first_own, "col"), col, 1)
    square_first = jnp.sum(residual * residual, axis=1)
    square_first = square_first + swap(square_first, "col")
    square_far = swap(square_first, "row")
    query_own = product(first_half, part_of(query_weight, row, 1))
    query_out = product(first_half, part_of(query_weight, 1 - row, 1)).astype(bf16)
    pair_own = product(first_half, kv_flat)
    shared_own = product(first_half, bc_weight)
    step_own = product(first_half, step_weight)
    query_width = query_own.shape[1]
    pair_width = pair_own.shape[1]
    shared_width = shared_own.shape[1]
    early = swap(
        jnp.concatenate(
            [
                query_out,
                pair_own.astype(bf16),
                part_of(shared_own, col, 1).astype(bf16),
                to_lanes(step_own).astype(bf16),
            ],
            axis=1,
        ),
        "row",
    )
    mix_out = product(first_half, part_of(mixer_in, 1 - row, 1)).astype(bf16)
    mix_own = product(first_half, part_of(mixer_in, row, 1))
    cot_near = swap_dp(cotangent, 1)
    cot_half = in_order(cotangent, swap(cotangent, "col"), col, 1)
    hidden_back = product_back(cot_half, part_of(down_weight, 1 - row, 0)).astype(bf16)
    hidden_back_own = product_back(cot_half, part_of(down_weight, row, 0))

    out_spread.wait(spine)
    out_spread.level()
    ffn_spread.wait(spine)
    ffn_spread.level()
    out_spread.wait(spine)
    out_spread.level()
    cot_near, early, square_far, mix_out = spine.wait(cot_near, early, square_far, mix_out)
    mix_other = swap(mix_out, "row")
    first_factor = lax.rsqrt((square_first + square_far) / D + norm_epsilon)
    first_column = first_factor[:, None]
    query_sum = (query_own + early[:, :query_width].astype(f32)) * first_column
    place = query_width
    pair_sum = (pair_own + early[:, place : place + pair_width].astype(f32)) * first_column
    place += pair_width
    shared_sum = (
        part_of(shared_own, col, 1) + early[:, place : place + shared_width // 2].astype(f32)
    ) * first_column
    shared_sum = in_order(
        shared_sum, swap(shared_sum.astype(bf16), "col").astype(f32), col, 1
    )
    place += shared_width // 2
    step_sum = (
        step_own + early[:, place : place + step_own.shape[1]].astype(f32)
    ) * first_column
    step_sum = to_lanes(lax.dynamic_slice_in_dim(step_sum, quarter * head_count, head_count, 1))
    ffn_spread.wait(spine)
    ffn_spread.level()
    cosine, sine = rope_tables(length)
    attended = attention_forward(query_sum, pair_sum, cosine, sine)
    heads = to_lanes(jnp.stack([log_rate, step_bias] + [jnp.zeros_like(log_rate)] * 6))
    skip_wide = jnp.repeat(skip_gain, PM)[None, :]
    gain_wide = group_gain[None, :]
    out_spread.wait(spine)
    out_spread.level()
    mix_other, hidden_back = spine.wait(mix_other, hidden_back)
    hidden_back = swap(hidden_back, "row")
    mixed_raw, square, mix_sum, ssm, states = mixer_forward(
        mix_own, mix_other, first_column, shared_sum, step_sum, conv_inner, conv_shared,
        heads, skip_wide, gain_wide, attended,
    )
    square, hidden_back = spine.wait(square, hidden_back)
    square_total = square[:, 0] + swap(square[:, 0], "col")
    square_far = swap(square_total, "row")
    ffn_spread.wait(spine)
    ffn_spread.level()
    out_other = out_spread.finish(spine)
    square_far, first_send = spine.wait(square_far, first_own)
    first_near = swap_dp(first_send, 1)
    group_factor = lax.rsqrt((square_total + square_far) / (HM * PM) + norm_epsilon)
    groups = attended.shape[1] // HD
    group_width = mixed_raw.shape[1] // groups
    is_normed = jnp.arange(mixed_raw.shape[1])[None, :] % group_width < group_width - HD
    mixed = (
        mixed_raw.astype(f32) * jnp.where(is_normed, group_factor[:, None], 1.0)
    ).astype(bf16)

    out_far = sum_cols(product(mixed, out_other), col)
    out_far = swap(out_far.astype(bf16), "row")
    out_near = sum_cols(product(mixed, out_own), col)
    ffn_other = ffn_spread.finish(spine)
    out_far, mixed_send = spine.wait(out_far, mixed)
    mixed_near = swap_dp(near_blocks(mixed_send, 1 - near), 1)
    mixed_kept = near_blocks(mixed_send, near)
    second = residual + out_near + out_far.astype(f32)
    second_own = (second * norm_second).astype(bf16)
    second_far = swap(second_own, "row")
    second_half = in_order(second_own, swap(second_own, "col"), col, 1)
    second_near = swap_dp(second_own, 1)
    second_square = jnp.sum(second * second, axis=1)
    second_square = second_square + swap(second_square, "col")
    second_square_far = swap(second_square, "row")
    gate_width = gate_own.shape[1]
    gate_part, up_part = product(second_half, gate_own), product(second_half, up_own)
    second_far, second_near = spine.wait(second_far, second_near)
    second_far = in_order(second_far, swap(second_far, "col"), col, 1)
    second_far_near = swap(second_near, "row")
    second_near = in_order(second_near, swap(second_near, "col"), col, 1)
    second_factor = lax.rsqrt((second_square + second_square_far) / D + norm_epsilon)
    second_column = second_factor[:, None]
    gate_sum = (gate_part + product(second_far, ffn_other[:, :gate_width])) * second_column
    up_sum = (up_part + product(second_far, ffn_other[:, gate_width:])) * second_column
    gate_sigmoid = jax.nn.sigmoid(gate_sum)
    gate_act = gate_sum * gate_sigmoid
    hidden_grad = hidden_back_own + hidden_back.astype(f32)
    gate_grad = hidden_grad * up_sum * gate_sigmoid * (1.0 + gate_sum * (1.0 - gate_sigmoid))
    up_grad = hidden_grad * gate_act
    hidden = (gate_act * up_sum).astype(bf16)
    ffn_grad = jnp.concatenate(
        [(gate_grad * second_column).astype(bf16), (up_grad * second_column).astype(bf16)], axis=1
    )
    second_total = jnp.sum(gate_grad * gate_sum + up_grad * up_sum, axis=1)
    second_total = second_total + swap(second_total, "col")
    second_total_far = swap(second_total, "row")
    ffn_send = swap_dp(part_of(ffn_grad, 1 - near, 1), 1)
    back_far = sum_cols(product_back(ffn_grad, ffn_other), col).astype(bf16)
    second_total_far, back_far, mixed_near = spine.wait(second_total_far, back_far, mixed_near)
    back_far = swap(back_far, "row")
    back_near = sum_cols(
        product_back(ffn_grad[:, :gate_width], gate_own)
        + product_back(ffn_grad[:, gate_width:], up_own),
        col,
    )
    second_far_near = spine.wait(second_far_near)
    second_far_near = in_order(second_far_near, swap(second_far_near, "col"), col, 1)
    back_far, ffn_send = spine.wait(back_far, ffn_send)
    second_in_grad = back_near + back_far.astype(f32)
    second_grad = (
        cotangent.astype(f32)
        + norm_second * second_in_grad
        - second * (second_factor**2 * (second_total + second_total_far) / D)[:, None]
    )
    norm_second_grad = jnp.sum(second_in_grad * second, axis=0)
    branch = second_grad.astype(bf16)
    branch_far = swap(branch, "row")
    branch_half = in_order(branch, swap(branch, "col"), col, 1)
    branch_near = swap_dp(branch, 1)

    def both_halves(scattered, sent):
        kept = lax.dynamic_index_in_dim(scattered, near, 0, keepdims=False)
        return jnp.where(near == 0, kept, sent), jnp.where(near == 0, sent, kept)

    def to_neighbour(scattered):
        return swap_dp(lax.dynamic_index_in_dim(scattered, 1 - near, 0, keepdims=False), 1)

    branch_half, mixed_near, mixed_kept, hidden_send = spine.wait(
        branch_half, mixed_near, mixed_kept, hidden
    )
    mixed_near_far = swap(mixed_near, "row")
    mixed_kept_far = swap(mixed_kept, "row")
    hidden_near = swap_dp(near_blocks(hidden_send, 1 - near), 1)
    ffn_kept = part_of(ffn_grad, near, 1)
    ffn_scatter = Scatter(
        spine,
        (outer_sum(second_half, ffn_kept) + outer_sum(second_near, ffn_send)).astype(bf16),
        True,
    )
    ffn_scatter_far = Scatter(
        spine,
        (outer_sum(second_far, ffn_kept) + outer_sum(second_far_near, ffn_send)).astype(bf16),
        True,
    )
    branch_far = spine.wait(branch_far)
    branch_far = in_order(branch_far, swap(branch_far, "col"), col, 1)
    mixed_grad = product_back(branch_half, out_own) + product_back(branch_far, out_other)

    group_total = jnp.sum(jnp.where(is_normed, mixed_grad * mixed.astype(f32), 0.0), axis=1)
    group_total = group_total + swap(group_total, "col")
    group_total_far = swap(group_total, "row")
    query_grad, pair_grad, attention_total = attention_backward(
        query_sum, pair_sum, cosine, sine, mixed_grad, first_column
    )
    group_total_far, attention_total = spine.wait(group_total_far, attention_total)
    group_scale = group_factor**2 * (group_total + group_total_far) / (HM * PM)
    group_scale, first_send, first_near = spine.wait(group_scale, first_own, first_near)
    first_far = swap(first_send, "row")
    first_far_near = swap(first_near, "row")
    first_near = in_order(first_near, swap(first_near, "col"), col, 1)
    lanes = (
        jnp.arange(channels)[:, None] // PM == jnp.arange(LANES)[None, :]
    ).astype(bf16)
    (
        own_grads,
        shared_grad,
        step_grad,
        conv_inner_grad,
        conv_shared_part,
        head_grads,
        wide_grads,
        mixer_total,
    ) = mixer_backward(
        mix_sum, ssm, states, shared_sum, step_sum, conv_inner, conv_shared, heads, skip_wide,
        gain_wide, lanes, mixed_grad, group_factor[:, None], group_scale[:, None], first_column,
        query_grad,
    )
    mixer_total = spine.wait(mixer_total)
    ffn_scatter.add()
    ffn_scatter_far.add()
    own_grads, shared_grad = spine.wait(own_grads, shared_grad)
    mix_width = mix_sum.shape[1]
    grads_send = swap_dp(part_of(own_grads, 1 - near, 1), 1)
    shared_low = (shared_grad.astype(f32) + swap(shared_grad, "col").astype(f32)).astype(bf16)
    late = jnp.concatenate([part_of(shared_low, col, 1), pair_grad, step_grad], axis=1)
    late_far = swap(late, "row")
    mixed_kept_far, mixed_near_far, branch_near = spine.wait(
        mixed_kept_far, mixed_near_far, branch_near
    )
    mixed_kept = in_order(mixed_kept, mixed_kept_far, row, 1)
    mixed_near = in_order(mixed_near, mixed_near_far, row, 1)
    branch_near = in_order(branch_near, swap(branch_near, "col"), col, 1)
    out_scatter = Scatter(
        spine,
        (outer_sum(mixed_kept, branch_half) + outer_sum(mixed_near, branch_near)).astype(bf16),
        False,
        f32,
    )
    ffn_near = ffn_scatter.finish()
    ffn_near_sent = to_neighbour(ffn_near)
    ffn_far = ffn_scatter_far.finish()
    ffn_far_sent = to_neighbour(ffn_far)
    first_far, first_far_near, grads_send = spine.wait(first_far, first_far_near, grads_send)
    first_far = in_order(first_far, swap(first_far, "col"), col, 1)
    first_far_near = in_order(first_far_near, swap(first_far_near, "col"), col, 1)
    grads_kept = part_of(own_grads, near, 1)
    mixer_scatter_far = Scatter(
        spine,
        (outer_sum(first_far, grads_kept) + outer_sum(first_far_near, grads_send)).astype(bf16),
        True,
    )
    out_scatter.add()
    late_far, hidden_send, hidden_near = spine.wait(late_far, hidden, hidden_near)
    hidden_far = swap(hidden_send, "row")
    hidden_near_far = swap(hidden_near, "row")
    half = shared_width // 2
    late_sum = (late[:, : half + pair_width].astype(f32) + late_far[:, : half + pair_width].astype(f32)).astype(bf16)
    shared_part, pair_low = late_sum[:, :half], late_sum[:, half:]
    step_two = in_order(
        late[:, half + pair_width :][:, :head_count],
        late_far[:, half + pair_width :][:, :head_count],
        row,
        1,
    )
    step_all = in_order(step_two, swap(step_two, "col"), col, 1)
    shared_low = in_order(shared_part, swap(shared_part, "col"), col, 1)
    rest = jnp.concatenate(
        [pair_low, shared_part, to_lanes(step_all), jnp.zeros((length, LANES), bf16)], axis=1
    )
    rest_send = swap_dp(part_of(rest, 1 - near, 1), 1)
    mixer_scatter_far.add()
    rest_send = spine.wait(rest_send)
    mixer_scatter = Scatter(
        spine,
        (
            outer_sum(
                first_half, jnp.concatenate([grads_kept, part_of(rest, near, 1)], axis=1)
            )
            + outer_sum(first_near, jnp.concatenate([grads_send, rest_send], axis=1))
        ).astype(bf16),
        True,
    )

    out_weight_grad = out_scatter.finish()[0]
    hidden_far, hidden_near_far, grads_again = spine.wait(hidden_far, hidden_near_far, own_grads)
    own_grads_far = swap(grads_again, "row")
    hidden_half = in_order(hidden, hidden_far, row, 1)
    hidden_near = in_order(hidden_near, hidden_near_far, row, 1)
    cot_near = in_order(cot_near, swap(cot_near, "col"), col, 1)
    down_scatter = Scatter(
        spine,
        (
            outer_sum(near_blocks(hidden_half, near), cot_half)
            + outer_sum(hidden_near, cot_near)
        ).astype(bf16),
        False,
        f32,
    )
    mixer_far = mixer_scatter_far.finish()
    mixer_far_sent = to_neighbour(mixer_far)
    mixer_scatter.add()
    layer_out = (second + sum_cols(product(hidden_half, down_weight), col)).astype(bf16)
    ffn_far_sent, ffn_near_sent = spine.wait(ffn_far_sent, ffn_near_sent)
    ffn_near = both_halves(ffn_near, ffn_near_sent)
    ffn_far = swap(jnp.stack(both_halves(ffn_far, ffn_far_sent)), "row")
    down_scatter.add()
    own_grads_far = spine.wait(own_grads_far)
    mix_half = in_order(own_grads[:, :mix_width], own_grads_far[:, :mix_width], row, 1)
    query_half = in_order(own_grads[:, mix_width:], own_grads_far[:, mix_width:], row, 1)
    first_in_partial = (
        product_back(mix_half, mixer_in)
        + product_back(query_half, query_weight)
        + product_back(pair_low, kv_flat)
        + 0.5 * (product_back(shared_low, bc_weight) + product_back(step_all, step_weight))
    )
    first_in_grad = sum_cols(first_in_partial, col)
    first_total = (attention_total + mixer_total)[:, 0]
    first_total = first_total + swap(first_total, "col")
    first_total_far = swap(first_total, "row")
    conv_shared_sum = conv_shared_part + swap(conv_shared_part, "col")
    conv_shared_far = swap(conv_shared_sum, "row")
    first_total_far, conv_shared_far, ffn_far = spine.wait(first_total_far, conv_shared_far, ffn_far)
    gate_weight_grad = in_order(ffn_near[0], ffn_far[0], row, 1).astype(f32)
    up_weight_grad = in_order(ffn_near[1], ffn_far[1], row, 1).astype(f32)
    input_grad = (
        second_grad
        + norm_first * first_in_grad
        - residual * (first_factor**2 * (first_total + first_total_far) / D)[:, None]
    )
    norm_first_grad = jnp.sum(first_in_grad * residual, axis=0)
    conv_shared_sum = conv_shared_sum + conv_shared_far
    skip_grad = wide_grads[1].reshape(head_count, PM).sum(axis=1)
    pieces = [
        norm_first_grad,
        norm_second_grad,
        conv_inner_grad.reshape(-1),
        conv_shared_sum.reshape(-1),
        wide_grads[0],
        jnp.pad(head_grads[0, :head_count], (0, LANES - head_count)),
        jnp.pad(head_grads[1, :head_count], (0, LANES - head_count)),
        jnp.pad(skip_grad, (0, LANES - head_count)),
    ]
    small = jnp.concatenate(pieces).reshape(-1, LANES)
    bits = dp_bits()
    small_far = swap_dp(small, bits[0])
    mixer_far_sent = spine.wait(mixer_far_sent)
    mixer_far = swap(jnp.concatenate(both_halves(mixer_far, mixer_far_sent), axis=1), "row")
    small = small + spine.wait(small_far)
    small_far = swap_dp(small, bits[1])
    mixer_near = mixer_scatter.finish()
    mixer_near_sent = to_neighbour(mixer_near)
    small = small + spine.wait(small_far)
    small_far = swap_dp(small, bits[2])
    mixer_near_sent, mixer_far = spine.wait(mixer_near_sent, mixer_far)
    mixer_near = both_halves(mixer_near, mixer_near_sent)
    kept_width = grads_kept.shape[1]
    own_sums = jnp.concatenate([mixer_near[0][:, :kept_width], mixer_near[1][:, :kept_width]], axis=1)
    rest_sums = jnp.concatenate(
        [mixer_near[0][:, kept_width:], mixer_near[1][:, kept_width:]], axis=1
    ).astype(f32)
    mixer_in_grad = in_order(own_sums[:, :mix_width], mixer_far[:, :mix_width], row, 1).astype(f32)
    query_weight_grad = in_order(
        own_sums[:, mix_width:], mixer_far[:, mix_width:], row, 1
    ).astype(f32)
    kv_weight_grad = rest_sums[:, :pair_width].reshape((-1,) + kv_weight.shape[1:])
    place = pair_width
    bc_own = rest_sums[:, place : place + shared_width // 2].astype(bf16)
    bc_weight_grad = in_order(bc_own, swap(bc_own, "col"), col, 1).astype(f32)
    place += shared_width // 2
    step_weight_grad = rest_sums[:, place : place + step_weight.shape[1]]
    for bit in bits[3:]:
        small = small + spine.wait(small_far)
        small_far = swap_dp(small, bit)
    small = small + spine.wait(small_far)
    down_weight_grad = down_scatter.finish()[0]
    small = (small + spine.token).reshape(-1)
    sums, place = [], 0
    for piece in pieces:
        sums.append(small[place : place + piece.shape[0]])
        place += piece.shape[0]

    def own_block(values_in, axis):
        size = values_in.shape[axis] // count
        return lax.dynamic_slice_in_dim(values_in, me * size, size, axis)

    return (
        layer_out,
        input_grad,
        own_block(sums[0], 0),
        mixer_in_grad,
        query_weight_grad,
        bc_weight_grad,
        step_weight_grad,
        kv_weight_grad,
        own_block(sums[2].reshape(conv_inner.shape), 1),
        own_block(sums[3].reshape(conv_shared.shape), 1),
        sums[5][:head_count],
        sums[6][:head_count],
        sums[7][:head_count],
        own_block(sums[4], 0),
        out_weight_grad,
        own_block(sums[1], 0),
        gate_weight_grad,
        up_weight_grad,
        down_weight_grad,
    )


def solution(mesh):
    in_specs = (
        P("dp", ("row", "col")),
        P(("row", "col")),
        P("row", "col"),
        P("row", "col"),
        P("row", None),
        P("row", None),
        P("row", "col", None),
        P(None, ("col", "row")),
        P(),
        P(("col", "row")),
        P(("col", "row")),
        P(("col", "row")),
        P(("col", "row")),
        P("col", "row"),
        P(("row", "col")),
        P("row", "col"),
        P("row", "col"),
        P("col", "row"),
        P("dp", ("row", "col")),
    )
    out_specs = (
        P("dp", ("row", "col")),
        P("dp", ("row", "col")),
        P(("row", "col", "dp")),
        P(("row", "dp"), "col"),
        P(("row", "dp"), "col"),
        P(("row", "dp"), None),
        P(("row", "dp"), None),
        P(("row", "dp"), "col", None),
        P(None, ("col", "row", "dp")),
        P(None, "dp"),
        P(("col", "row")),
        P(("col", "row")),
        P(("col", "row")),
        P(("col", "row", "dp")),
        P(("col", "dp"), "row"),
        P(("row", "col", "dp")),
        P(("row", "dp"), "col"),
        P(("row", "dp"), "col"),
        P(("col", "dp"), "row"),
    )
    return jax.shard_map(local, mesh=mesh, in_specs=in_specs, out_specs=out_specs, check_vma=False)
```

```python
from functools import partial
import math

import jax
import jax.numpy as jnp
from jax import lax
from jax.experimental import pallas as pl
from jax.experimental.pallas import tpu as pltpu
from jax.sharding import PartitionSpec as P

D = 2048
HM = 48
PM = 64
NS = 256
HD = 128
MIX = 4096
LANES = 128
CHUNK = 128

norm_epsilon = 1e-05
rope_base = 10000.0
highest = lax.Precision.HIGHEST
f32 = jnp.float32
bf16 = jnp.bfloat16
VMEM_LIMIT = 56 * 1024 * 1024


def product(left_side, right_side):
    return jnp.dot(left_side, right_side, preferred_element_type=f32)


def product_back(left_side, right_side):
    return lax.dot_general(
        left_side, right_side, (((1,), (1,)), ((), ())), preferred_element_type=f32
    )


def outer_sum(left_side, right_side):
    return lax.dot_general(
        left_side, right_side, (((0,), (0,)), ((), ())), preferred_element_type=f32
    )


def swap(values_in, axis):
    return lax.ppermute(values_in, axis, [(0, 1), (1, 0)])


def in_order(own, other, place, axis):
    return jnp.concatenate(
        [jnp.where(place == 0, own, other), jnp.where(place == 0, other, own)], axis=axis
    )


def part_of(values_in, place, axis):
    size = values_in.shape[axis] // 2
    return lax.dynamic_slice_in_dim(values_in, place * size, size, axis)


def rows_total(values_in):
    values_in = values_in + swap(values_in, "col")
    return values_in + swap(values_in, "row")


def sum_cols(values_in, col):
    sent = swap(part_of(values_in, 1 - col, 1).astype(bf16), "col")
    return part_of(values_in, col, 1) + sent.astype(f32)


def near_blocks(values_in, near):
    size = MIX // 2 // lax.axis_size("dp")
    places = range(0, values_in.shape[1], 2 * size)
    return jnp.concatenate(
        [
            jnp.where(
                near == 0,
                values_in[:, place : place + size],
                values_in[:, place + size : place + 2 * size],
            )
            for place in places
        ],
        axis=1,
    )


def dp_bits():
    bits, bit = [], 1
    while bit < lax.axis_size("dp"):
        bits.append(bit)
        bit *= 2
    return bits


def swap_dp(values_in, bit):
    return lax.ppermute(values_in, "dp", [(i, i ^ bit) for i in range(lax.axis_size("dp"))])


def tie(*values_in):
    return lax.optimization_barrier(values_in)


class Spine:
    def __init__(self, token):
        self.token = token

    def wait(self, *values_in):
        tied = tie(self.token, *values_in)
        self.token = tied[0]
        return tied[1] if len(tied) == 2 else tied[1:]


class Scatter:
    def __init__(self, spine, grads, pairs, dtype=bf16):
        self.spine, self.dtype = spine, dtype
        self.bits = dp_bits()[1:]
        blocks = lax.axis_size("dp") // 2 * (2 if pairs else 1)
        rest = (blocks // 2 ** len(self.bits), grads.shape[0] // blocks) + grads.shape[1:]
        self.left = self.bits[::-1]
        self.parts = grads.reshape((2,) * len(self.bits) + rest)
        self.send()

    def send(self):
        bit = self.bits[len(self.bits) - len(self.left)]
        axis = self.left.index(bit)
        mine = (lax.axis_index("dp") // bit) % 2
        send = lax.dynamic_index_in_dim(self.parts, 1 - mine, axis, keepdims=False)
        self.parts = lax.dynamic_index_in_dim(self.parts, mine, axis, keepdims=False)
        self.arrived = swap_dp(send, bit)
        self.left.pop(axis)

    def add(self):
        arrived = self.spine.wait(self.arrived)
        total = self.parts.astype(f32) + arrived.astype(f32)
        self.parts = total.astype(bf16 if self.left else self.dtype)
        if self.left:
            self.send()

    def finish(self):
        while self.left:
            self.add()
        self.add()
        return self.parts


def far_sum(grads):
    count = lax.axis_size("dp")
    groups = [list(range(start, count, 2)) for start in range(2)]
    return lax.psum_scatter(
        grads, "dp", scatter_dimension=0, axis_index_groups=groups, tiled=True
    )


def both_rows_kernel(own_ref, far_ref, near_ref, far_near_ref, kept_ref, sent_ref, out_ref, sums):
    blocks, _, rows, _ = out_ref.shape
    for side, left_ref, right_ref in ((0, own_ref, near_ref), (1, far_ref, far_near_ref)):
        sums[...] = outer_sum(left_ref[...], kept_ref[...]) + outer_sum(
            right_ref[...], sent_ref[...]
        )
        for block in range(blocks):
            out_ref[block, side] = sums[block * rows : (block + 1) * rows, :].astype(bf16)


def place_kernel(count, owners, where_ref, *refs):
    pieces, out_ref = refs[:count], refs[count]
    rows = pieces[0].shape[0]
    for turn in range(count):
        start = pl.multiple_of((where_ref[0] ^ owners[turn]) * rows, rows)
        out_ref[pl.ds(start, rows), :] = pieces[turn][...]


def place_pieces(pieces, owners):
    count = len(pieces)
    rows, columns = pieces[0].shape
    return pl.pallas_call(
        partial(place_kernel, count, owners),
        out_shape=jax.ShapeDtypeStruct((count * rows, columns), pieces[0].dtype),
        in_specs=[pl.BlockSpec(memory_space=pltpu.SMEM)]
        + [pl.BlockSpec(memory_space=pltpu.VMEM)] * count,
        out_specs=pl.BlockSpec(memory_space=pltpu.VMEM),
        compiler_params=pltpu.CompilerParams(vmem_limit_bytes=VMEM_LIMIT),
        cost_estimate=pl.CostEstimate(
            flops=0, bytes_accessed=4 * count * rows * columns, transcendentals=0
        ),
    )(lax.axis_index("dp").astype(jnp.int32)[None], *pieces)


class Spread:
    def __init__(self, mine):
        self.pieces, self.owners = [mine], [0]
        self.bits = [dp_bits()[::-1]]
        self.first = 0

    def wait(self, spine):
        arrived = spine.wait(*self.pieces[self.first :])
        self.pieces[self.first :] = arrived if isinstance(arrived, (tuple, list)) else [arrived]

    def level(self):
        start, self.first = self.first, len(self.pieces)
        sends = [
            (-bit, turn) for turn in range(start, self.first) for bit in self.bits[turn]
        ]
        for bit, turn in sorted(sends):
            self.pieces.append(swap_dp(self.pieces[turn], -bit))
            self.owners.append(self.owners[turn] ^ -bit)
            self.bits.append([lower for lower in self.bits[turn] if lower < -bit])

    def finish(self, spine):
        self.wait(spine)
        while len(self.pieces) < lax.axis_size("dp"):
            self.level()
            self.wait(spine)
        return place_pieces(self.pieces, self.owners)


def sigmoid(values_in):
    return 1.0 / (1.0 + jnp.exp(-values_in))


def softplus(values_in):
    return jnp.maximum(values_in, 0.0) + jnp.log1p(jnp.exp(-jnp.abs(values_in)))


def low_lanes():
    return lax.broadcasted_iota(jnp.int32, (1, LANES), 1) < PM


def pair_columns(values_in, pair):
    return jnp.where(
        low_lanes(), values_in[:, 2 * pair : 2 * pair + 1], values_in[:, 2 * pair + 1 : 2 * pair + 2]
    )


def shift_down(values_in, count):
    if count == 0:
        return values_in
    rows = lax.broadcasted_iota(jnp.int32, values_in.shape, 0)
    return jnp.where(rows >= count, pltpu.roll(values_in, count, 0), 0.0)


def shift_up(values_in, count):
    if count == 0:
        return values_in
    length = values_in.shape[0]
    rows = lax.broadcasted_iota(jnp.int32, values_in.shape, 0)
    return jnp.where(rows < length - count, pltpu.roll(values_in, length - count, 0), 0.0)


def conv(values_in, taps):
    count = taps.shape[0]
    total = values_in * taps[count - 1 : count, :]
    for tap in range(count - 1):
        total = total + taps[tap : tap + 1, :] * shift_down(values_in, count - 1 - tap)
    return total


def conv_back(grad, values_in, taps):
    count = taps.shape[0]
    total = grad * taps[count - 1 : count, :]
    for tap in range(count - 1):
        total = total + taps[tap : tap + 1, :] * shift_up(grad, count - 1 - tap)
    tap_grads = [
        jnp.sum(grad * shift_down(values_in, count - 1 - tap), axis=0, keepdims=True)
        for tap in range(count)
    ]
    return total, tap_grads


def stacked_pair(values_in):
    low = low_lanes()
    return jnp.concatenate(
        [jnp.where(low, values_in, 0.0), jnp.where(low, 0.0, values_in)], axis=0
    ).astype(bf16)


def lower_mask():
    rows = lax.broadcasted_iota(jnp.int32, (CHUNK, CHUNK), 0)
    columns = lax.broadcasted_iota(jnp.int32, (CHUNK, CHUNK), 1)
    return (rows >= columns).astype(f32)


def mixer_forward_kernel(
    own_ref,
    other_ref,
    factor_ref,
    shared_ref,
    step_ref,
    conv_inner_ref,
    conv_shared_ref,
    head_ref,
    skip_ref,
    gain_ref,
    attended_ref,
    mixed_ref,
    square_ref,
    mix_ref,
    ssm_ref,
    states_ref,
    inner_buf,
    gate_buf,
    maps_buf,
    step_buf,
    decay_buf,
    weighted_buf,
    state_buf,
):
    pairs = ssm_ref.shape[1] // LANES
    length = own_ref.shape[0]
    groups = attended_ref.shape[1] // HD
    group_pairs = pairs // groups
    low = low_lanes()
    factor = factor_ref[...]
    for group in range(groups):
        place = ((group + 1) * group_pairs + group) * LANES
        mixed_ref[:, place : place + HD] = attended_ref[:, group * HD : (group + 1) * HD]
    for pair in range(pairs):
        first = slice(2 * pair * LANES, (2 * pair + 1) * LANES)
        second = slice((2 * pair + 1) * LANES, (2 * pair + 2) * LANES)
        own = slice(pair * LANES, (pair + 1) * LANES)
        head_a = (own_ref[:, first] + other_ref[:, first].astype(f32)) * factor
        head_b = (own_ref[:, second] + other_ref[:, second].astype(f32)) * factor
        mix_ref[:, first] = head_a
        mix_ref[:, second] = head_b
        taken = jnp.where(low, pltpu.roll(head_a, PM, 1), head_b)
        gate_buf[:, own] = jnp.where(low, head_a, pltpu.roll(head_b, PM, 1))
        taken = conv(taken, conv_inner_ref[:, own])
        inner_buf[:, own] = taken * sigmoid(taken)
    for block in range(shared_ref.shape[1] // LANES):
        own = slice(block * LANES, (block + 1) * LANES)
        taken = conv(shared_ref[:, own], conv_shared_ref[:, own])
        maps_buf[:, own] = (taken * sigmoid(taken)).astype(bf16)
    steps = softplus(step_ref[...] + head_ref[1:2, :])
    step_buf[...] = steps
    decay_buf[...] = -jnp.exp(head_ref[0:1, :]) * steps
    state_buf[...] = jnp.zeros_like(state_buf)
    mask = lower_mask()

    def chunk(index, carry):
        rows = pl.ds(pl.multiple_of(index * CHUNK, CHUNK), CHUNK)
        running = jnp.dot(mask, decay_buf[rows, :], precision=highest, preferred_element_type=f32)
        running_t = running.T
        step = step_buf[rows, :]
        step_t = step.T
        last = running[CHUNK - 1 : CHUNK, :]
        grown = jnp.exp(running)
        tail = jnp.exp(last - running) * step
        grown_last = jnp.exp(last)
        basis = maps_buf[rows, 0:NS]
        read = maps_buf[rows, NS : 2 * NS]
        gram = product_back(read, basis)
        state_low = state_buf[...].astype(bf16)
        states_ref[pl.ds(pl.multiple_of(index * NS, NS), NS), :] = state_low
        carried = product(read, state_low)
        square = jnp.zeros((CHUNK, 1), f32)
        for pair in range(pairs):
            own = slice(pair * LANES, (pair + 1) * LANES)
            inner = inner_buf[rows, own]
            mixing = []
            for head in (2 * pair, 2 * pair + 1):
                spread = jnp.exp(
                    jnp.minimum(running[:, head : head + 1] - running_t[head : head + 1, :], 0.0)
                )
                mixing.append(
                    (gram * spread * mask * step_t[head : head + 1, :]).astype(bf16)
                )
            ssm = product(jnp.concatenate(mixing, axis=1), stacked_pair(inner))
            ssm = ssm + pair_columns(grown, pair) * carried[:, own] + skip_ref[:, own] * inner
            ssm_ref[rows, own] = ssm
            weighted_buf[:, own] = (pair_columns(tail, pair) * inner).astype(bf16)
            gate = gate_buf[rows, own]
            gated = ssm * gate * sigmoid(gate)
            square = square + jnp.sum(gated * gated, axis=1, keepdims=True)
            place = pair * LANES + (pair // group_pairs) * HD
            mixed_ref[rows, place : place + LANES] = (gated * gain_ref[:, own]).astype(bf16)
        square_ref[rows, :] = square
        fresh = outer_sum(basis, weighted_buf[...])
        for pair in range(pairs):
            own = slice(pair * LANES, (pair + 1) * LANES)
            state_buf[:, own] = (
                pair_columns(grown_last, pair) * state_buf[:, own] + fresh[:, own]
            )
        return carry

    lax.fori_loop(0, length // CHUNK, chunk, 0)


def mixer_backward_kernel(
    mix_ref,
    ssm_ref,
    states_ref,
    shared_ref,
    step_ref,
    conv_inner_ref,
    conv_shared_ref,
    head_ref,
    skip_ref,
    gain_ref,
    lanes_ref,
    grad_ref,
    group_factor_ref,
    group_scale_ref,
    factor_ref,
    query_grad_ref,
    mix_grad_ref,
    shared_grad_ref,
    step_grad_ref,
    inner_taps_ref,
    shared_taps_ref,
    head_grad_ref,
    wide_grad_ref,
    total_ref,
    taken_buf,
    inner_buf,
    maps_buf,
    step_buf,
    decay_buf,
    weighted_buf,
    grown_buf,
    inner_grad_buf,
    maps_grad_buf,
    sums_buf,
    state_grad_buf,
):
    pairs = ssm_ref.shape[1] // LANES
    length = ssm_ref.shape[0]
    group_pairs = pairs // (grad_ref.shape[1] // (pairs * LANES // 2 + HD))
    low = low_lanes()
    mix_grad_ref[:, 2 * pairs * LANES :] = query_grad_ref[...]
    for pair in range(pairs):
        first = slice(2 * pair * LANES, (2 * pair + 1) * LANES)
        second = slice((2 * pair + 1) * LANES, (2 * pair + 2) * LANES)
        own = slice(pair * LANES, (pair + 1) * LANES)
        taken = jnp.where(low, pltpu.roll(mix_ref[:, first], PM, 1), mix_ref[:, second])
        taken_buf[:, own] = taken
        taken = conv(taken, conv_inner_ref[:, own])
        inner_buf[:, own] = taken * sigmoid(taken)
    for block in range(shared_ref.shape[1] // LANES):
        own = slice(block * LANES, (block + 1) * LANES)
        taken = conv(shared_ref[:, own], conv_shared_ref[:, own])
        maps_buf[:, own] = (taken * sigmoid(taken)).astype(bf16)
    shifted = step_ref[...] + head_ref[1:2, :]
    steps = softplus(shifted)
    rate = -jnp.exp(head_ref[0:1, :])
    step_buf[...] = steps
    decay_buf[...] = rate * steps
    state_grad_buf[...] = jnp.zeros_like(state_grad_buf)
    head_grad_ref[...] = jnp.zeros_like(head_grad_ref)
    wide_grad_ref[...] = jnp.zeros_like(wide_grad_ref)
    mask = lower_mask()
    chunks = length // CHUNK
    lane_index = lax.broadcasted_iota(jnp.int32, (1, LANES), 1)

    def chunk(turn, carry):
        index = chunks - 1 - turn
        rows = pl.ds(pl.multiple_of(index * CHUNK, CHUNK), CHUNK)
        running = jnp.dot(mask, decay_buf[rows, :], precision=highest, preferred_element_type=f32)
        running_t = running.T
        step = step_buf[rows, :]
        step_t = step.T
        last = running[CHUNK - 1 : CHUNK, :]
        grown = jnp.exp(running)
        fading = jnp.exp(last - running)
        grown_last = jnp.exp(last)
        basis = maps_buf[rows, 0:NS]
        read = maps_buf[rows, NS : 2 * NS]
        gram = product_back(read, basis)
        state_low = states_ref[pl.ds(pl.multiple_of(index * NS, NS), NS), :]
        carried = product(read, state_low)
        state_grad_low = state_grad_buf[...].astype(bf16)
        weighted_grad = product(basis, state_grad_low)
        gram_grad = jnp.zeros((CHUNK, CHUNK), f32)
        decay_grad = jnp.zeros((CHUNK, LANES), f32)
        column_grads = []
        total = jnp.zeros((CHUNK, 1), f32)
        group_factor = group_factor_ref[rows, :]
        group_scale = group_scale_ref[rows, :]
        factor = factor_ref[rows, :]
        for pair in range(pairs):
            first = slice(2 * pair * LANES, (2 * pair + 1) * LANES)
            second = slice((2 * pair + 1) * LANES, (2 * pair + 2) * LANES)
            own = slice(pair * LANES, (pair + 1) * LANES)
            place = pair * LANES + (pair // group_pairs) * HD
            incoming = grad_ref[rows, place : place + LANES]
            head_a = mix_ref[rows, first]
            head_b = mix_ref[rows, second]
            gate = jnp.where(low, head_a, pltpu.roll(head_b, PM, 1))
            gate_sigmoid = sigmoid(gate)
            gate_act = gate * gate_sigmoid
            ssm = ssm_ref[rows, own]
            gated = ssm * gate_act
            wide_grad_ref[0:1, own] += jnp.sum(
                incoming * gated * group_factor, axis=0, keepdims=True
            )
            gated_grad = group_factor * gain_ref[:, own] * incoming - gated * group_scale
            gate_grad = gated_grad * ssm * gate_sigmoid * (1.0 + gate * (1.0 - gate_sigmoid))
            ssm_grad = gated_grad * gate_act
            inner = inner_buf[rows, own]
            wide_grad_ref[1:2, own] += jnp.sum(ssm_grad * inner, axis=0, keepdims=True)
            gate_b = pltpu.roll(gate_grad, PM, 1)
            total = total + jnp.sum(gate_grad * gate, axis=1, keepdims=True)
            mix_grad_ref[rows, first] = jnp.where(low, gate_grad * factor, 0.0).astype(bf16)
            mix_grad_ref[rows, second] = jnp.where(low, gate_b * factor, 0.0).astype(bf16)
            grad_low = ssm_grad.astype(bf16)
            mixing_grad = product_back(grad_low, stacked_pair(inner))
            spreads = []
            for side, head in enumerate((2 * pair, 2 * pair + 1)):
                spread = mask * jnp.exp(
                    jnp.minimum(running[:, head : head + 1] - running_t[head : head + 1, :], 0.0)
                )
                step_row = step_t[head : head + 1, :]
                spread_gram = gram * spread
                spreads.append(spread_gram.astype(bf16))
                own_grad = mixing_grad[:, side * CHUNK : (side + 1) * CHUNK] * step_row
                gram_grad = gram_grad + own_grad * spread
                moved = own_grad * spread_gram
                decay_grad = decay_grad + jnp.where(
                    lane_index == head, jnp.sum(moved, axis=1, keepdims=True), 0.0
                )
                column_grads.append(jnp.sum(moved, axis=0, keepdims=True))
            within = outer_sum(jnp.concatenate(spreads, axis=0), stacked_pair(ssm_grad))
            fading_grad = pair_columns(fading, pair) * weighted_grad[:, own]
            spread_grad = within + fading_grad
            step_wide = pair_columns(step, pair)
            inner_grad_buf[rows, own] = step_wide * spread_grad + skip_ref[:, own] * ssm_grad
            grown_grad = pair_columns(grown, pair) * ssm_grad
            grown_buf[:, own] = grown_grad.astype(bf16)
            weighted_buf[:, own] = (pair_columns(fading, pair) * step_wide * inner).astype(bf16)
            sums_buf[0:CHUNK, own] = (inner * spread_grad).astype(bf16)
            sums_buf[CHUNK : 2 * CHUNK, own] = (inner * fading_grad * step_wide).astype(bf16)
            sums_buf[2 * CHUNK : 3 * CHUNK, own] = (grown_grad * carried[:, own]).astype(bf16)
        head_sums = product(sums_buf[...], lanes_ref[...])
        step_part = head_sums[0:CHUNK, :]
        fading_part = head_sums[CHUNK : 2 * CHUNK, :]
        grown_part = head_sums[2 * CHUNK : 3 * CHUNK, :]
        fill = jnp.zeros((CHUNK - len(column_grads), CHUNK), f32)
        column_grad = jnp.concatenate(column_grads + [fill], axis=0).T
        decay_grad = decay_grad - column_grad + grown_part - fading_part
        state_part = jnp.zeros((1, LANES), f32)
        grown_low = grown_buf[...]
        fresh = outer_sum(read, grown_low)
        for pair in range(pairs):
            own = slice(pair * LANES, (pair + 1) * LANES)
            state_grad = state_grad_buf[:, own]
            held = jnp.sum(state_grad * state_low[:, own].astype(f32), axis=0, keepdims=True)
            for side, head in enumerate((2 * pair, 2 * pair + 1)):
                kept = jnp.where(low if side == 0 else jnp.logical_not(low), held, 0.0)
                state_part = state_part + jnp.where(
                    lane_index == head, jnp.sum(kept, axis=1, keepdims=True), 0.0
                )
            state_grad_buf[:, own] = pair_columns(grown_last, pair) * state_grad + fresh[:, own]
        last_grad = jnp.sum(fading_part, axis=0, keepdims=True) + grown_last * state_part
        decay_sum = (
            lax.dot_general(
                mask,
                decay_grad,
                (((0,), (0,)), ((), ())),
                precision=highest,
                preferred_element_type=f32,
            )
            + last_grad
        )
        raw_shift = step_ref[rows, :] + head_ref[1:2, :]
        raw_grad = (step_part + decay_sum * rate) * sigmoid(raw_shift)
        head_grad_ref[0:1, :] += jnp.sum(decay_sum * decay_buf[rows, :], axis=0, keepdims=True)
        head_grad_ref[1:2, :] += jnp.sum(raw_grad, axis=0, keepdims=True)
        step_grad_ref[rows, :] = (raw_grad * factor).astype(bf16)
        total = total + jnp.sum(raw_grad * step_ref[rows, :], axis=1, keepdims=True)
        total_ref[rows, :] = total
        gram_low = gram_grad.astype(bf16)
        maps_grad_buf[rows, 0:NS] = outer_sum(gram_low, read) + product_back(
            weighted_buf[...], state_grad_low
        )
        maps_grad_buf[rows, NS : 2 * NS] = product(gram_low, basis) + product_back(
            grown_low, state_low
        )
        return carry

    lax.fori_loop(0, chunks, chunk, 0)
    factor = factor_ref[...]
    total = total_ref[...]
    for pair in range(pairs):
        first = slice(2 * pair * LANES, (2 * pair + 1) * LANES)
        second = slice((2 * pair + 1) * LANES, (2 * pair + 2) * LANES)
        own = slice(pair * LANES, (pair + 1) * LANES)
        taken = taken_buf[:, own]
        taps = conv_inner_ref[:, own]
        before = conv(taken, taps)
        before_sigmoid = sigmoid(before)
        grad = inner_grad_buf[:, own] * before_sigmoid * (1.0 + before * (1.0 - before_sigmoid))
        grad, tap_grads = conv_back(grad, taken, taps)
        for tap, tap_grad in enumerate(tap_grads):
            inner_taps_ref[tap : tap + 1, own] = tap_grad
        total = total + jnp.sum(grad * taken, axis=1, keepdims=True)
        grad = grad * factor
        low_a = mix_grad_ref[:, first].astype(f32)
        low_b = mix_grad_ref[:, second].astype(f32)
        mix_grad_ref[:, first] = jnp.where(low, low_a, pltpu.roll(grad, PM, 1)).astype(bf16)
        mix_grad_ref[:, second] = jnp.where(low, low_b, grad).astype(bf16)
    for block in range(shared_ref.shape[1] // LANES):
        own = slice(block * LANES, (block + 1) * LANES)
        taken = shared_ref[:, own]
        taps = conv_shared_ref[:, own]
        before = conv(taken, taps)
        before_sigmoid = sigmoid(before)
        grad = maps_grad_buf[:, own] * before_sigmoid * (1.0 + before * (1.0 - before_sigmoid))
        grad, tap_grads = conv_back(grad, taken, taps)
        for tap, tap_grad in enumerate(tap_grads):
            shared_taps_ref[tap : tap + 1, own] = tap_grad
        total = total + jnp.sum(grad * taken, axis=1, keepdims=True)
        shared_grad_ref[:, own] = (grad * factor).astype(bf16)
    total_ref[...] = total


def call(kernel, outs, scratch, flops, *operands):
    return pl.pallas_call(
        kernel,
        out_shape=outs,
        in_specs=[pl.BlockSpec(memory_space=pltpu.VMEM)] * len(operands),
        out_specs=[pl.BlockSpec(memory_space=pltpu.VMEM)] * len(outs),
        scratch_shapes=scratch,
        compiler_params=pltpu.CompilerParams(vmem_limit_bytes=VMEM_LIMIT),
        cost_estimate=pl.CostEstimate(flops=flops, bytes_accessed=10**6, transcendentals=0),
    )(*operands)


def shape(dims, dtype=f32):
    return jax.ShapeDtypeStruct(dims, dtype)


def mixer_forward(
    own, other, factor, shared, step, taps, shared_taps, heads, skip, gain, attended
):
    length, width = own.shape
    channels = width // 2
    chunks = length // CHUNK
    return call(
        mixer_forward_kernel,
        [
            shape((length, channels + attended.shape[1]), bf16),
            shape((length, 1)),
            shape((length, width)),
            shape((length, channels)),
            shape((chunks * NS, channels), bf16),
        ],
        [
            pltpu.VMEM((length, channels), f32),
            pltpu.VMEM((length, channels), f32),
            pltpu.VMEM((length, 2 * NS), bf16),
            pltpu.VMEM((length, LANES), f32),
            pltpu.VMEM((length, LANES), f32),
            pltpu.VMEM((CHUNK, channels), bf16),
            pltpu.VMEM((NS, channels), f32),
        ],
        10**8,
        own, other, factor, shared, step, taps, shared_taps, heads, skip, gain, attended,
    )


def mixer_backward(
    mix, ssm, states, shared, step, taps, shared_taps, heads, skip, gain, lanes, grad,
    group_factor, group_scale, factor, query_grad,
):
    length, width = mix.shape
    channels = width // 2
    return call(
        mixer_backward_kernel,
        [
            shape((length, width + query_grad.shape[1]), bf16),
            shape((length, 2 * NS), bf16),
            shape((length, LANES), bf16),
            shape((taps.shape[0], channels)),
            shape((taps.shape[0], 2 * NS)),
            shape((8, LANES)),
            shape((8, channels)),
            shape((length, 1)),
        ],
        [
            pltpu.VMEM((length, channels), f32),
            pltpu.VMEM((length, channels), f32),
            pltpu.VMEM((length, 2 * NS), bf16),
            pltpu.VMEM((length, LANES), f32),
            pltpu.VMEM((length, LANES), f32),
            pltpu.VMEM((CHUNK, channels), bf16),
            pltpu.VMEM((CHUNK, channels), bf16),
            pltpu.VMEM((length, channels), f32),
            pltpu.VMEM((length, 2 * NS), f32),
            pltpu.VMEM((3 * CHUNK, channels), bf16),
            pltpu.VMEM((NS, channels), f32),
        ],
        10**8,
        mix, ssm, states, shared, step, taps, shared_taps, heads, skip, gain, lanes, grad,
        group_factor, group_scale, factor, query_grad,
    )


def rotated(values_in, cosine, sine):
    return values_in * cosine + pltpu.roll(values_in, HD // 2, 1) * sine


def rotated_back(grad, cosine, sine):
    return grad * cosine + pltpu.roll(grad * sine, HD // 2, 1)


def attention_forward_kernel(query_ref, pair_ref, cosine_ref, sine_ref, out_ref):
    length = query_ref.shape[0]
    scale = 1.0 / math.sqrt(HD)
    block = min(256, length)
    keys = rotated(pair_ref[:, :HD], cosine_ref[...], sine_ref[...]).astype(bf16)
    vals = pair_ref[:, HD:].astype(bf16)
    for head in range(query_ref.shape[1] // HD):
        lanes = slice(head * HD, (head + 1) * HD)
        queries = rotated(query_ref[:, lanes], cosine_ref[...], sine_ref[...]).astype(bf16)
        for start in range(0, length, block):
            end = start + block
            scores = product_back(queries[start:end], keys[:end]) * scale
            rows = start + lax.broadcasted_iota(jnp.int32, (block, end), 0)
            columns = lax.broadcasted_iota(jnp.int32, (block, end), 1)
            scores = jnp.where(columns <= rows, scores, -1e30)
            exponent = jnp.exp(scores - jnp.max(scores, axis=1, keepdims=True))
            probs = exponent * (1.0 / jnp.sum(exponent, axis=1, keepdims=True))
            out_ref[start:end, lanes] = product(probs.astype(bf16), vals[:end]).astype(bf16)


def attention_backward_kernel(
    query_ref, pair_ref, cosine_ref, sine_ref, grad_ref, factor_ref,
    query_grad_ref, pair_grad_ref, total_ref, key_buf, val_buf,
):
    length = query_ref.shape[0]
    scale = 1.0 / math.sqrt(HD)
    block = min(256, length)
    cosine, sine = cosine_ref[...], sine_ref[...]
    keys = rotated(pair_ref[:, :HD], cosine, sine).astype(bf16)
    vals = pair_ref[:, HD:].astype(bf16)
    heads = query_ref.shape[1] // HD
    group = grad_ref.shape[1] // heads
    key_buf[...] = jnp.zeros_like(key_buf)
    val_buf[...] = jnp.zeros_like(val_buf)
    for head in range(heads):
        lanes = slice(head * HD, (head + 1) * HD)
        queries = rotated(query_ref[:, lanes], cosine, sine).astype(bf16)
        incoming = grad_ref[:, (head + 1) * group - HD : (head + 1) * group].astype(bf16)
        for start in range(0, length, block):
            end = start + block
            scores = product_back(queries[start:end], keys[:end]) * scale
            rows = start + lax.broadcasted_iota(jnp.int32, (block, end), 0)
            columns = lax.broadcasted_iota(jnp.int32, (block, end), 1)
            scores = jnp.where(columns <= rows, scores, -1e30)
            exponent = jnp.exp(scores - jnp.max(scores, axis=1, keepdims=True))
            probs = exponent * (1.0 / jnp.sum(exponent, axis=1, keepdims=True))
            grad_low = incoming[start:end]
            val_buf[:end, :] += outer_sum(probs.astype(bf16), grad_low)
            probs_grad = product_back(grad_low, vals[:end])
            inner = jnp.sum(probs * probs_grad, axis=1, keepdims=True)
            scores_grad = (probs * (probs_grad - inner) * scale).astype(bf16)
            query_grad = rotated_back(
                product(scores_grad, keys[:end]), cosine[start:end], sine[start:end]
            )
            key_buf[:end, :] += outer_sum(scores_grad, queries[start:end])
            taken = query_ref[start:end, lanes]
            part = jnp.sum(query_grad * taken, axis=1, keepdims=True)
            if head == 0:
                total_ref[start:end, :] = part
            else:
                total_ref[start:end, :] += part
            query_grad_ref[start:end, lanes] = (query_grad * factor_ref[start:end, :]).astype(bf16)
    key_grad = rotated_back(key_buf[...], cosine, sine)
    val_grad = val_buf[...]
    total_ref[...] += jnp.sum(
        key_grad * pair_ref[:, :HD] + val_grad * pair_ref[:, HD:], axis=1, keepdims=True
    )
    pair_grad_ref[:, :HD] = (key_grad * factor_ref[...]).astype(bf16)
    pair_grad_ref[:, HD:] = (val_grad * factor_ref[...]).astype(bf16)


def attention_forward(query, pair, cosine, sine):
    return call(
        attention_forward_kernel, [shape(query.shape, bf16)], [], 10**8,
        query, pair, cosine, sine,
    )[0]


def attention_backward(query, pair, cosine, sine, grad, factor):
    length = query.shape[0]
    return call(
        attention_backward_kernel,
        [shape(query.shape, bf16), shape(pair.shape, bf16), shape((length, 1))],
        [pltpu.VMEM((length, HD), f32), pltpu.VMEM((length, HD), f32)],
        10**8,
        query, pair, cosine, sine, grad, factor,
    )


def rope_tables(length):
    half = HD // 2
    inverse = rope_base ** (-jnp.arange(half, dtype=f32) * 2.0 / HD)
    angles = jnp.arange(length, dtype=f32)[:, None] * inverse[None, :]
    cosine, sine = jnp.cos(angles), jnp.sin(angles)
    return jnp.concatenate([cosine, cosine], axis=1), jnp.concatenate([-sine, sine], axis=1)


def to_lanes(values_in):
    return jnp.pad(values_in, ((0, 0), (0, LANES - values_in.shape[1])))


def local(
    tokens,
    norm_first,
    mixer_in,
    query_weight,
    bc_weight,
    step_weight,
    kv_weight,
    conv_inner,
    conv_shared,
    log_rate,
    step_bias,
    skip_gain,
    group_gain,
    out_weight,
    norm_second,
    gate_weight,
    up_weight,
    down_weight,
    cotangent,
):
    length = tokens.shape[0]
    row = lax.axis_index("row")
    col = lax.axis_index("col")
    me = lax.axis_index("dp")
    count = lax.axis_size("dp")
    near = me % 2
    quarter = col * 2 + row
    head_count = log_rate.shape[0]
    channels = group_gain.shape[0]
    kv_flat = kv_weight.reshape(kv_weight.shape[0], -1)
    residual = tokens.astype(f32)
    spine = Spine(jnp.zeros((1, LANES), f32))

    def column_share(weight):
        rows, columns = weight.shape[0] // count, weight.shape[1] // 2
        return lax.dynamic_slice(weight, (me * rows, (1 - row) * columns), (rows, columns))

    half_rows = out_weight.shape[0] // 2
    share_rows = half_rows // count
    out_own = part_of(out_weight, row, 0)
    gate_own, up_own = part_of(gate_weight, row, 1), part_of(up_weight, row, 1)
    out_share = lax.dynamic_slice_in_dim(
        out_weight, (1 - row) * half_rows + me * share_rows, share_rows, 0
    )
    ffn_share = jnp.concatenate([column_share(gate_weight), column_share(up_weight)], axis=1)
    out_share, ffn_share, residual = tie(out_share, ffn_share, residual)
    out_spread = Spread(swap(out_share, "row"))
    ffn_spread = Spread(swap(ffn_share, "row"))

    first_own = (residual * norm_first).astype(bf16)
    first_half = in_order(first_own, swap(first_own, "col"), col, 1)
    square_first = jnp.sum(residual * residual, axis=1)
    square_first = square_first + swap(square_first, "col")
    square_far = swap(square_first, "row")
    query_own = product(first_half, part_of(query_weight, row, 1))
    query_out = product(first_half, part_of(query_weight, 1 - row, 1)).astype(bf16)
    pair_own = product(first_half, kv_flat)
    shared_own = product(first_half, bc_weight)
    step_own = product(first_half, step_weight)
    query_width = query_own.shape[1]
    pair_width = pair_own.shape[1]
    shared_width = shared_own.shape[1]
    early = swap(
        jnp.concatenate(
            [
                query_out,
                pair_own.astype(bf16),
                part_of(shared_own, col, 1).astype(bf16),
                to_lanes(step_own).astype(bf16),
            ],
            axis=1,
        ),
        "row",
    )
    mix_out = product(first_half, part_of(mixer_in, 1 - row, 1)).astype(bf16)
    mix_own = product(first_half, part_of(mixer_in, row, 1))
    cot_near = swap_dp(cotangent, 1)
    cot_half = in_order(cotangent, swap(cotangent, "col"), col, 1)
    hidden_back = product_back(cot_half, part_of(down_weight, 1 - row, 0)).astype(bf16)
    hidden_back_own = product_back(cot_half, part_of(down_weight, row, 0))

    out_spread.wait(spine)
    out_spread.level()
    ffn_spread.wait(spine)
    ffn_spread.level()
    cot_near, early, square_far, mix_out = spine.wait(cot_near, early, square_far, mix_out)
    mix_other = swap(mix_out, "row")
    out_spread.wait(spine)
    out_spread.level()
    first_factor = lax.rsqrt((square_first + square_far) / D + norm_epsilon)
    first_column = first_factor[:, None]
    query_sum = (query_own + early[:, :query_width].astype(f32)) * first_column
    place = query_width
    pair_sum = (pair_own + early[:, place : place + pair_width].astype(f32)) * first_column
    place += pair_width
    shared_sum = (
        part_of(shared_own, col, 1) + early[:, place : place + shared_width // 2].astype(f32)
    ) * first_column
    shared_sum = in_order(
        shared_sum, swap(shared_sum.astype(bf16), "col").astype(f32), col, 1
    )
    place += shared_width // 2
    step_sum = (
        step_own + early[:, place : place + step_own.shape[1]].astype(f32)
    ) * first_column
    step_sum = to_lanes(lax.dynamic_slice_in_dim(step_sum, quarter * head_count, head_count, 1))
    ffn_spread.wait(spine)
    ffn_spread.level()
    cosine, sine = rope_tables(length)
    attended = attention_forward(query_sum, pair_sum, cosine, sine)
    heads = to_lanes(jnp.stack([log_rate, step_bias] + [jnp.zeros_like(log_rate)] * 6))
    skip_wide = jnp.repeat(skip_gain, PM)[None, :]
    gain_wide = group_gain[None, :]
    out_spread.wait(spine)
    out_spread.level()
    out_other = out_spread.finish(spine)
    mix_other, hidden_back, attended, shared_sum, step_sum = spine.wait(
        mix_other, hidden_back, attended, shared_sum, step_sum
    )
    hidden_back = swap(hidden_back, "row")
    mixed_raw, square, mix_sum, ssm, states = mixer_forward(
        mix_own, mix_other, first_column, shared_sum, step_sum, conv_inner, conv_shared,
        heads, skip_wide, gain_wide, attended,
    )
    square, hidden_back = spine.wait(square, hidden_back)
    square_total = square[:, 0] + swap(square[:, 0], "col")
    square_far = swap(square_total, "row")
    ffn_spread.wait(spine)
    ffn_spread.level()
    square_far = spine.wait(square_far)
    group_factor = lax.rsqrt((square_total + square_far) / (HM * PM) + norm_epsilon)
    groups = attended.shape[1] // HD
    group_width = mixed_raw.shape[1] // groups
    is_normed = jnp.arange(mixed_raw.shape[1])[None, :] % group_width < group_width - HD
    mixed = (
        mixed_raw.astype(f32) * jnp.where(is_normed, group_factor[:, None], 1.0)
    ).astype(bf16)

    out_far = sum_cols(product(mixed, out_other), col)
    out_far = swap(out_far.astype(bf16), "row")
    out_near = sum_cols(product(mixed, out_own), col)
    ffn_other = ffn_spread.finish(spine)
    out_far = spine.wait(out_far)
    second = residual + out_near + out_far.astype(f32)
    second_own = (second * norm_second).astype(bf16)
    second_far = swap(second_own, "row")
    second_half = in_order(second_own, swap(second_own, "col"), col, 1)
    second_near = swap_dp(second_own, 1)
    second_square = jnp.sum(second * second, axis=1)
    second_square = second_square + swap(second_square, "col")
    second_square_far = swap(second_square, "row")
    gate_width = gate_own.shape[1]
    gate_part, up_part = product(second_half, gate_own), product(second_half, up_own)
    second_far, second_near, first_send = spine.wait(second_far, second_near, first_own)
    second_far_near = swap_dp(second_far, 1)
    first_row = swap(first_send, "row")
    first_near = swap_dp(first_send, 1)
    second_far = in_order(second_far, swap(second_far, "col"), col, 1)
    second_near = in_order(second_near, swap(second_near, "col"), col, 1)
    second_factor = lax.rsqrt((second_square + second_square_far) / D + norm_epsilon)
    second_column = second_factor[:, None]
    gate_sum = (gate_part + product(second_far, ffn_other[:, :gate_width])) * second_column
    up_sum = (up_part + product(second_far, ffn_other[:, gate_width:])) * second_column
    gate_sigmoid = jax.nn.sigmoid(gate_sum)
    gate_act = gate_sum * gate_sigmoid
    second_far_near, hidden_back = spine.wait(second_far_near, hidden_back)
    second_far_near = in_order(second_far_near, swap(second_far_near, "col"), col, 1)
    hidden_grad = hidden_back_own + hidden_back.astype(f32)
    gate_grad = hidden_grad * up_sum * gate_sigmoid * (1.0 + gate_sum * (1.0 - gate_sigmoid))
    up_grad = hidden_grad * gate_act
    hidden = (gate_act * up_sum).astype(bf16)
    ffn_grad = jnp.concatenate(
        [(gate_grad * second_column).astype(bf16), (up_grad * second_column).astype(bf16)], axis=1
    )
    second_total = jnp.sum(gate_grad * gate_sum + up_grad * up_sum, axis=1)
    second_total = second_total + swap(second_total, "col")
    second_total_far = swap(second_total, "row")
    ffn_send = swap_dp(part_of(ffn_grad, 1 - near, 1), 1)
    back_far = sum_cols(product_back(ffn_grad, ffn_other), col).astype(bf16)
    second_total_far, back_far, first_row, first_near = spine.wait(
        second_total_far, back_far, first_row, first_near
    )
    back_far = swap(back_far, "row")
    back_near = sum_cols(
        product_back(ffn_grad[:, :gate_width], gate_own)
        + product_back(ffn_grad[:, gate_width:], up_own),
        col,
    )
    back_far, ffn_send = spine.wait(back_far, ffn_send)
    second_in_grad = back_near + back_far.astype(f32)
    second_grad = (
        cotangent.astype(f32)
        + norm_second * second_in_grad
        - second * (second_factor**2 * (second_total + second_total_far) / D)[:, None]
    )
    norm_second_grad = jnp.sum(second_in_grad * second, axis=0)
    branch = second_grad.astype(bf16)
    branch_far = swap(branch, "row")
    branch_half = in_order(branch, swap(branch, "col"), col, 1)

    def both_halves(scattered, sent):
        kept = lax.dynamic_index_in_dim(scattered, near, 0, keepdims=False)
        return jnp.where(near == 0, kept, sent), jnp.where(near == 0, sent, kept)

    def to_neighbour(scattered):
        return swap_dp(lax.dynamic_index_in_dim(scattered, 1 - near, 0, keepdims=False), 1)

    branch_half = spine.wait(branch_half)
    ffn_kept = part_of(ffn_grad, near, 1)
    blocks = count // 2
    ffn_sums = call(
        both_rows_kernel,
        [shape((blocks, 2, second_half.shape[1] // blocks, ffn_kept.shape[1]), bf16)],
        [pltpu.VMEM((second_half.shape[1], ffn_kept.shape[1]), f32)],
        10**6,
        second_half, second_far, second_near, second_far_near, ffn_kept, ffn_send,
    )[0]
    ffn_sums = spine.wait(ffn_sums)
    ffn_sums = far_sum(ffn_sums.reshape(-1, ffn_kept.shape[1]))
    mixed_send, hidden_send = spine.wait(mixed, hidden)
    near_pack = jnp.concatenate(
        [
            near_blocks(mixed_send, 1 - near),
            branch,
            near_blocks(hidden_send, 1 - near),
            first_row,
        ],
        axis=1,
    )
    near_pack = swap_dp(near_pack, 1)
    branch_far = spine.wait(branch_far)
    branch_far = in_order(branch_far, swap(branch_far, "col"), col, 1)
    mixed_grad = product_back(branch_half, out_own) + product_back(branch_far, out_other)

    group_total = jnp.sum(jnp.where(is_normed, mixed_grad * mixed.astype(f32), 0.0), axis=1)
    group_total = group_total + swap(group_total, "col")
    group_total_far = swap(group_total, "row")
    query_grad, pair_grad, attention_total = attention_backward(
        query_sum, pair_sum, cosine, sine, mixed_grad, first_column
    )
    group_total_far, attention_total = spine.wait(group_total_far, attention_total)
    group_scale = group_factor**2 * (group_total + group_total_far) / (HM * PM)
    size = branch.shape[1]

    def piece(pack, turn):
        return pack[:, turn * size : (turn + 1) * size]

    group_scale, mixed_kept = spine.wait(group_scale, near_blocks(mixed, near))
    mixed_kept_far = swap(mixed_kept, "row")
    first_pair = jnp.concatenate([first_row, first_near], axis=1)
    first_pair_col = swap(first_pair, "col")
    first_far = in_order(piece(first_pair, 0), piece(first_pair_col, 0), col, 1)
    first_near = in_order(piece(first_pair, 1), piece(first_pair_col, 1), col, 1)
    lanes = (
        jnp.arange(channels)[:, None] // PM == jnp.arange(LANES)[None, :]
    ).astype(bf16)
    (
        own_grads,
        shared_grad,
        step_grad,
        conv_inner_grad,
        conv_shared_part,
        head_grads,
        wide_grads,
        mixer_total,
    ) = mixer_backward(
        mix_sum, ssm, states, shared_sum, step_sum, conv_inner, conv_shared, heads, skip_wide,
        gain_wide, lanes, mixed_grad, group_factor[:, None], group_scale[:, None], first_column,
        query_grad,
    )
    mixed_kept_far, first_far, first_near = spine.wait(mixed_kept_far, first_far, first_near)
    own_grads, shared_grad, near_pack = spine.wait(own_grads, shared_grad, near_pack)
    mix_width = mix_sum.shape[1]
    grads_send = swap_dp(part_of(own_grads, 1 - near, 1), 1)
    grads_kept = part_of(own_grads, near, 1)
    shared_low = (shared_grad.astype(f32) + swap(shared_grad, "col").astype(f32)).astype(bf16)
    late = jnp.concatenate([part_of(shared_low, col, 1), pair_grad, step_grad], axis=1)
    late_far = swap(late, "row")
    first_far_near = piece(near_pack, 3)
    first_far_near = in_order(first_far_near, swap(first_far_near, "col"), col, 1)
    grads_send, mixed_send, hidden_send = spine.wait(
        grads_send, piece(near_pack, 0), piece(near_pack, 2)
    )
    near_far = swap(jnp.concatenate([mixed_send, hidden_send], axis=1), "row")
    mixer_scatter_far = Scatter(
        spine,
        (outer_sum(first_far, grads_kept) + outer_sum(first_far_near, grads_send)).astype(bf16),
        True,
    )
    late_far, mixer_scatter_far.parts = spine.wait(late_far, mixer_scatter_far.parts)
    half = shared_width // 2
    late_sum = (
        late[:, : half + pair_width].astype(f32) + late_far[:, : half + pair_width].astype(f32)
    ).astype(bf16)
    shared_part, pair_low = late_sum[:, :half], late_sum[:, half:]
    step_two = in_order(
        late[:, half + pair_width :][:, :head_count],
        late_far[:, half + pair_width :][:, :head_count],
        row,
        1,
    )
    step_all = in_order(step_two, swap(step_two, "col"), col, 1)
    rest = jnp.concatenate(
        [pair_low, shared_part, to_lanes(step_all), jnp.zeros((length, LANES), bf16)], axis=1
    )
    rest_send = swap_dp(part_of(rest, 1 - near, 1), 1)
    rest_send = spine.wait(rest_send)
    mixer_scatter = Scatter(
        spine,
        (
            outer_sum(
                first_half, jnp.concatenate([grads_kept, part_of(rest, near, 1)], axis=1)
            )
            + outer_sum(first_near, jnp.concatenate([grads_send, rest_send], axis=1))
        ).astype(bf16),
        True,
    )
    near_far, mixer_scatter.parts, hidden_send, ffn_sums = spine.wait(
        near_far, mixer_scatter.parts, hidden, ffn_sums
    )
    hidden_far = swap(hidden_send, "row")
    mixed_kept = in_order(mixed_kept, mixed_kept_far, row, 1)
    mixed_near = in_order(piece(near_pack, 0), piece(near_far, 0), row, 1)
    branch_near = in_order(piece(near_pack, 1), swap(piece(near_pack, 1), "col"), col, 1)
    out_sums = far_sum(
        spine.wait(
            (
                outer_sum(mixed_kept, branch_half) + outer_sum(mixed_near, branch_near)
            ).astype(bf16)
        )
    )
    ffn_sums = ffn_sums.reshape(2, 2, -1, ffn_kept.shape[1])
    ffn_sent = swap_dp(lax.dynamic_index_in_dim(ffn_sums, 1 - near, 1, keepdims=False), 1)
    mixer_scatter_far.add()
    hidden_far, grads_again = spine.wait(hidden_far, own_grads)
    own_grads_far = swap(grads_again, "row")
    hidden_half = in_order(hidden, hidden_far, row, 1)
    hidden_near = in_order(piece(near_pack, 2), piece(near_far, 1), row, 1)
    cot_near = in_order(cot_near, swap(cot_near, "col"), col, 1)
    down_sums = far_sum(
        spine.wait(
            (
                outer_sum(near_blocks(hidden_half, near), cot_half)
                + outer_sum(hidden_near, cot_near)
            ).astype(bf16)
        )
    )
    ffn_sent, layer_half = spine.wait(ffn_sent, hidden_half)
    ffn_near = both_halves(ffn_sums[0], ffn_sent[0])
    ffn_far = swap(jnp.stack(both_halves(ffn_sums[1], ffn_sent[1])), "row")
    mixer_scatter.add()
    layer_out = (second + sum_cols(product(layer_half, down_weight), col)).astype(bf16)
    mixer_far = mixer_scatter_far.finish()
    mixer_far_sent = to_neighbour(mixer_far)
    first_total, conv_shared_part, own_grads_far = spine.wait(
        (attention_total + mixer_total)[:, 0], conv_shared_part, own_grads_far
    )
    first_total = first_total + swap(first_total, "col")
    first_total_far = swap(first_total, "row")
    conv_shared_sum = conv_shared_part + swap(conv_shared_part, "col")
    conv_shared_far = swap(conv_shared_sum, "row")
    mix_half = in_order(own_grads[:, :mix_width], own_grads_far[:, :mix_width], row, 1)
    query_half = in_order(own_grads[:, mix_width:], own_grads_far[:, mix_width:], row, 1)
    shared_low = in_order(shared_part, swap(shared_part, "col"), col, 1)
    first_in_partial = (
        product_back(mix_half, mixer_in)
        + product_back(query_half, query_weight)
        + product_back(pair_low, kv_flat)
        + 0.5 * (product_back(shared_low, bc_weight) + product_back(step_all, step_weight))
    )
    first_in_grad = sum_cols(first_in_partial, col)
    mixer_far_sent, first_total_far, conv_shared_far = spine.wait(
        mixer_far_sent, first_total_far, conv_shared_far
    )
    mixer_far = swap(jnp.concatenate(both_halves(mixer_far, mixer_far_sent), axis=1), "row")
    input_grad = (
        second_grad
        + norm_first * first_in_grad
        - residual * (first_factor**2 * (first_total + first_total_far) / D)[:, None]
    )
    norm_first_grad = jnp.sum(first_in_grad * residual, axis=0)
    conv_shared_sum = conv_shared_sum + conv_shared_far
    skip_grad = wide_grads[1].reshape(head_count, PM).sum(axis=1)
    pieces = [
        norm_first_grad,
        norm_second_grad,
        conv_inner_grad.reshape(-1),
        conv_shared_sum.reshape(-1),
        wide_grads[0],
        jnp.pad(head_grads[0, :head_count], (0, LANES - head_count)),
        jnp.pad(head_grads[1, :head_count], (0, LANES - head_count)),
        jnp.pad(skip_grad, (0, LANES - head_count)),
    ]
    small = jnp.concatenate(pieces).reshape(-1, LANES)
    bits = dp_bits()
    small_far = swap_dp(small, bits[0])
    ffn_far = spine.wait(ffn_far)
    gate_weight_grad = in_order(ffn_near[0], ffn_far[0], row, 1).astype(f32)
    up_weight_grad = in_order(ffn_near[1], ffn_far[1], row, 1).astype(f32)
    small = small + spine.wait(small_far)
    small_far = swap_dp(small, bits[1])
    out_weight_grad, down_weight_grad = spine.wait(out_sums, down_sums)
    mixer_near = mixer_scatter.finish()
    mixer_near_sent = to_neighbour(mixer_near)
    small_far, mixer_far = spine.wait(small_far, mixer_far)
    small = small + small_far
    small_far = swap_dp(small, bits[2])
    mixer_near_sent = spine.wait(mixer_near_sent)
    mixer_near = both_halves(mixer_near, mixer_near_sent)
    kept_width = grads_kept.shape[1]
    own_sums = jnp.concatenate([mixer_near[0][:, :kept_width], mixer_near[1][:, :kept_width]], axis=1)
    rest_sums = jnp.concatenate(
        [mixer_near[0][:, kept_width:], mixer_near[1][:, kept_width:]], axis=1
    ).astype(f32)
    mixer_in_grad = in_order(own_sums[:, :mix_width], mixer_far[:, :mix_width], row, 1).astype(f32)
    query_weight_grad = in_order(
        own_sums[:, mix_width:], mixer_far[:, mix_width:], row, 1
    ).astype(f32)
    kv_weight_grad = rest_sums[:, :pair_width].reshape((-1,) + kv_weight.shape[1:])
    place = pair_width
    bc_own = rest_sums[:, place : place + shared_width // 2].astype(bf16)
    bc_weight_grad = in_order(bc_own, swap(bc_own, "col"), col, 1).astype(f32)
    place += shared_width // 2
    step_weight_grad = rest_sums[:, place : place + step_weight.shape[1]]
    for bit in bits[3:]:
        small = small + spine.wait(small_far)
        small_far = swap_dp(small, bit)
    small = small + spine.wait(small_far)
    out_weight_grad, down_weight_grad = out_weight_grad.astype(f32), down_weight_grad.astype(f32)
    small = (small + spine.token).reshape(-1)
    sums, place = [], 0
    for piece in pieces:
        sums.append(small[place : place + piece.shape[0]])
        place += piece.shape[0]

    def own_block(values_in, axis):
        size = values_in.shape[axis] // count
        return lax.dynamic_slice_in_dim(values_in, me * size, size, axis)

    return (
        layer_out,
        input_grad,
        own_block(sums[0], 0),
        mixer_in_grad,
        query_weight_grad,
        bc_weight_grad,
        step_weight_grad,
        kv_weight_grad,
        own_block(sums[2].reshape(conv_inner.shape), 1),
        own_block(sums[3].reshape(conv_shared.shape), 1),
        sums[5][:head_count],
        sums[6][:head_count],
        sums[7][:head_count],
        own_block(sums[4], 0),
        out_weight_grad,
        own_block(sums[1], 0),
        gate_weight_grad,
        up_weight_grad,
        down_weight_grad,
    )


def solution(mesh):
    in_specs = (
        P("dp", ("row", "col")),
        P(("row", "col")),
        P("row", "col"),
        P("row", "col"),
        P("row", None),
        P("row", None),
        P("row", "col", None),
        P(None, ("col", "row")),
        P(),
        P(("col", "row")),
        P(("col", "row")),
        P(("col", "row")),
        P(("col", "row")),
        P("col", "row"),
        P(("row", "col")),
        P("row", "col"),
        P("row", "col"),
        P("col", "row"),
        P("dp", ("row", "col")),
    )
    out_specs = (
        P("dp", ("row", "col")),
        P("dp", ("row", "col")),
        P(("row", "col", "dp")),
        P(("row", "dp"), "col"),
        P(("row", "dp"), "col"),
        P(("row", "dp"), None),
        P(("row", "dp"), None),
        P(("row", "dp"), "col", None),
        P(None, ("col", "row", "dp")),
        P(None, "dp"),
        P(("col", "row")),
        P(("col", "row")),
        P(("col", "row")),
        P(("col", "row", "dp")),
        P(("col", "dp"), "row"),
        P(("row", "col", "dp")),
        P(("row", "dp"), "col"),
        P(("row", "dp"), "col"),
        P(("col", "dp"), "row"),
    )
    return jax.shard_map(local, mesh=mesh, in_specs=in_specs, out_specs=out_specs, check_vma=False)
```

```python
from functools import partial
import math

import jax
import jax.numpy as jnp
from jax import lax
from jax.experimental import pallas as pl
from jax.experimental.pallas import tpu as pltpu
from jax.sharding import PartitionSpec as P

D = 2048
HM = 48
PM = 64
NS = 256
HD = 128
MIX = 4096
LANES = 128
CHUNK = 128

norm_epsilon = 1e-05
rope_base = 10000.0
highest = lax.Precision.HIGHEST
f32 = jnp.float32
bf16 = jnp.bfloat16
VMEM_LIMIT = 56 * 1024 * 1024


def product(left_side, right_side):
    return jnp.dot(left_side, right_side, preferred_element_type=f32)


def product_back(left_side, right_side):
    return lax.dot_general(
        left_side, right_side, (((1,), (1,)), ((), ())), preferred_element_type=f32
    )


def outer_sum(left_side, right_side):
    return lax.dot_general(
        left_side, right_side, (((0,), (0,)), ((), ())), preferred_element_type=f32
    )


def swap(values_in, axis):
    return lax.ppermute(values_in, axis, [(0, 1), (1, 0)])


def in_order(own, other, place, axis):
    return jnp.concatenate(
        [jnp.where(place == 0, own, other), jnp.where(place == 0, other, own)], axis=axis
    )


def part_of(values_in, place, axis):
    size = values_in.shape[axis] // 2
    return lax.dynamic_slice_in_dim(values_in, place * size, size, axis)


def rows_total(values_in):
    values_in = values_in + swap(values_in, "col")
    return values_in + swap(values_in, "row")


def sum_cols(values_in, col):
    sent = swap(part_of(values_in, 1 - col, 1).astype(bf16), "col")
    return part_of(values_in, col, 1) + sent.astype(f32)


def near_blocks(values_in, near):
    size = MIX // 2 // lax.axis_size("dp")
    places = range(0, values_in.shape[1], 2 * size)
    return jnp.concatenate(
        [
            jnp.where(
                near == 0,
                values_in[:, place : place + size],
                values_in[:, place + size : place + 2 * size],
            )
            for place in places
        ],
        axis=1,
    )


def dp_bits():
    bits, bit = [], 1
    while bit < lax.axis_size("dp"):
        bits.append(bit)
        bit *= 2
    return bits


def swap_dp(values_in, bit):
    return lax.ppermute(values_in, "dp", [(i, i ^ bit) for i in range(lax.axis_size("dp"))])


def tie(*values_in):
    return lax.optimization_barrier(values_in)


class Spine:
    def __init__(self, token):
        self.token = token

    def wait(self, *values_in):
        tied = tie(self.token, *values_in)
        self.token = tied[0]
        return tied[1] if len(tied) == 2 else tied[1:]


class Scatter:
    def __init__(self, spine, grads, pairs, dtype=bf16):
        self.spine, self.dtype = spine, dtype
        self.bits = dp_bits()[1:]
        blocks = lax.axis_size("dp") // 2 * (2 if pairs else 1)
        rest = (blocks // 2 ** len(self.bits), grads.shape[0] // blocks) + grads.shape[1:]
        self.left = self.bits[::-1]
        self.parts = grads.reshape((2,) * len(self.bits) + rest)
        self.send()

    def send(self):
        bit = self.bits[len(self.bits) - len(self.left)]
        axis = self.left.index(bit)
        mine = (lax.axis_index("dp") // bit) % 2
        send = lax.dynamic_index_in_dim(self.parts, 1 - mine, axis, keepdims=False)
        self.parts = lax.dynamic_index_in_dim(self.parts, mine, axis, keepdims=False)
        self.arrived = swap_dp(send, bit)
        self.left.pop(axis)

    def add(self):
        arrived = self.spine.wait(self.arrived)
        total = self.parts.astype(f32) + arrived.astype(f32)
        self.parts = total.astype(bf16 if self.left else self.dtype)
        if self.left:
            self.send()

    def finish(self):
        while self.left:
            self.add()
        self.add()
        return self.parts


def far_sum(grads):
    count = lax.axis_size("dp")
    groups = [list(range(start, count, 2)) for start in range(2)]
    return lax.psum_scatter(
        grads, "dp", scatter_dimension=0, axis_index_groups=groups, tiled=True
    )


def both_rows_kernel(own_ref, far_ref, near_ref, far_near_ref, kept_ref, sent_ref, out_ref, sums):
    blocks, _, rows, _ = out_ref.shape
    for side, left_ref, right_ref in ((0, own_ref, near_ref), (1, far_ref, far_near_ref)):
        sums[...] = outer_sum(left_ref[...], kept_ref[...]) + outer_sum(
            right_ref[...], sent_ref[...]
        )
        for block in range(blocks):
            out_ref[block, side] = sums[block * rows : (block + 1) * rows, :].astype(bf16)


def place_kernel(count, owners, where_ref, *refs):
    pieces, out_ref = refs[:count], refs[count]
    rows = pieces[0].shape[0]
    for turn in range(count):
        start = pl.multiple_of((where_ref[0] ^ owners[turn]) * rows, rows)
        out_ref[pl.ds(start, rows), :] = pieces[turn][...]


def place_pieces(pieces, owners):
    count = len(pieces)
    rows, columns = pieces[0].shape
    return pl.pallas_call(
        partial(place_kernel, count, owners),
        out_shape=jax.ShapeDtypeStruct((count * rows, columns), pieces[0].dtype),
        in_specs=[pl.BlockSpec(memory_space=pltpu.SMEM)]
        + [pl.BlockSpec(memory_space=pltpu.VMEM)] * count,
        out_specs=pl.BlockSpec(memory_space=pltpu.VMEM),
        compiler_params=pltpu.CompilerParams(vmem_limit_bytes=VMEM_LIMIT),
        cost_estimate=pl.CostEstimate(
            flops=0, bytes_accessed=4 * count * rows * columns, transcendentals=0
        ),
    )(lax.axis_index("dp").astype(jnp.int32)[None], *pieces)


class Spread:
    def __init__(self, mine):
        self.pieces, self.owners = [mine], [0]
        self.bits = [dp_bits()[::-1]]
        self.first = 0

    def wait(self, spine):
        arrived = spine.wait(*self.pieces[self.first :])
        self.pieces[self.first :] = arrived if isinstance(arrived, (tuple, list)) else [arrived]

    def level(self):
        start, self.first = self.first, len(self.pieces)
        sends = [
            (-bit, turn) for turn in range(start, self.first) for bit in self.bits[turn]
        ]
        for bit, turn in sorted(sends):
            self.pieces.append(swap_dp(self.pieces[turn], -bit))
            self.owners.append(self.owners[turn] ^ -bit)
            self.bits.append([lower for lower in self.bits[turn] if lower < -bit])

    def finish(self, spine):
        self.wait(spine)
        while len(self.pieces) < lax.axis_size("dp"):
            self.level()
            self.wait(spine)
        return place_pieces(self.pieces, self.owners)


def sigmoid(values_in):
    return 1.0 / (1.0 + jnp.exp(-values_in))


def softplus(values_in):
    return jnp.maximum(values_in, 0.0) + jnp.log1p(jnp.exp(-jnp.abs(values_in)))


def low_lanes():
    return lax.broadcasted_iota(jnp.int32, (1, LANES), 1) < PM


def pair_columns(values_in, pair):
    return jnp.where(
        low_lanes(), values_in[:, 2 * pair : 2 * pair + 1], values_in[:, 2 * pair + 1 : 2 * pair + 2]
    )


def shift_down(values_in, count):
    if count == 0:
        return values_in
    rows = lax.broadcasted_iota(jnp.int32, values_in.shape, 0)
    return jnp.where(rows >= count, pltpu.roll(values_in, count, 0), 0.0)


def shift_up(values_in, count):
    if count == 0:
        return values_in
    length = values_in.shape[0]
    rows = lax.broadcasted_iota(jnp.int32, values_in.shape, 0)
    return jnp.where(rows < length - count, pltpu.roll(values_in, length - count, 0), 0.0)


def conv(values_in, taps):
    count = taps.shape[0]
    total = values_in * taps[count - 1 : count, :]
    for tap in range(count - 1):
        total = total + taps[tap : tap + 1, :] * shift_down(values_in, count - 1 - tap)
    return total


def conv_back(grad, values_in, taps):
    count = taps.shape[0]
    total = grad * taps[count - 1 : count, :]
    for tap in range(count - 1):
        total = total + taps[tap : tap + 1, :] * shift_up(grad, count - 1 - tap)
    tap_grads = [
        jnp.sum(grad * shift_down(values_in, count - 1 - tap), axis=0, keepdims=True)
        for tap in range(count)
    ]
    return total, tap_grads


def stacked_pair(values_in):
    low = low_lanes()
    return jnp.concatenate(
        [jnp.where(low, values_in, 0.0), jnp.where(low, 0.0, values_in)], axis=0
    ).astype(bf16)


def lower_mask():
    rows = lax.broadcasted_iota(jnp.int32, (CHUNK, CHUNK), 0)
    columns = lax.broadcasted_iota(jnp.int32, (CHUNK, CHUNK), 1)
    return (rows >= columns).astype(f32)


def mixer_forward_kernel(
    own_ref,
    other_ref,
    factor_ref,
    shared_ref,
    step_ref,
    conv_inner_ref,
    conv_shared_ref,
    head_ref,
    skip_ref,
    gain_ref,
    attended_ref,
    mixed_ref,
    square_ref,
    mix_ref,
    ssm_ref,
    states_ref,
    inner_buf,
    gate_buf,
    maps_buf,
    step_buf,
    decay_buf,
    weighted_buf,
    state_buf,
):
    pairs = ssm_ref.shape[1] // LANES
    length = own_ref.shape[0]
    groups = attended_ref.shape[1] // HD
    group_pairs = pairs // groups
    low = low_lanes()
    factor = factor_ref[...]
    for group in range(groups):
        place = ((group + 1) * group_pairs + group) * LANES
        mixed_ref[:, place : place + HD] = attended_ref[:, group * HD : (group + 1) * HD]
    for pair in range(pairs):
        first = slice(2 * pair * LANES, (2 * pair + 1) * LANES)
        second = slice((2 * pair + 1) * LANES, (2 * pair + 2) * LANES)
        own = slice(pair * LANES, (pair + 1) * LANES)
        head_a = (own_ref[:, first] + other_ref[:, first].astype(f32)) * factor
        head_b = (own_ref[:, second] + other_ref[:, second].astype(f32)) * factor
        mix_ref[:, first] = head_a
        mix_ref[:, second] = head_b
        taken = jnp.where(low, pltpu.roll(head_a, PM, 1), head_b)
        gate_buf[:, own] = jnp.where(low, head_a, pltpu.roll(head_b, PM, 1))
        taken = conv(taken, conv_inner_ref[:, own])
        inner_buf[:, own] = taken * sigmoid(taken)
    for block in range(shared_ref.shape[1] // LANES):
        own = slice(block * LANES, (block + 1) * LANES)
        taken = conv(shared_ref[:, own], conv_shared_ref[:, own])
        maps_buf[:, own] = (taken * sigmoid(taken)).astype(bf16)
    steps = softplus(step_ref[...] + head_ref[1:2, :])
    step_buf[...] = steps
    decay_buf[...] = -jnp.exp(head_ref[0:1, :]) * steps
    state_buf[...] = jnp.zeros_like(state_buf)
    mask = lower_mask()

    def chunk(index, carry):
        rows = pl.ds(pl.multiple_of(index * CHUNK, CHUNK), CHUNK)
        running = jnp.dot(mask, decay_buf[rows, :], precision=highest, preferred_element_type=f32)
        running_t = running.T
        step = step_buf[rows, :]
        step_t = step.T
        last = running[CHUNK - 1 : CHUNK, :]
        grown = jnp.exp(running)
        tail = jnp.exp(last - running) * step
        grown_last = jnp.exp(last)
        basis = maps_buf[rows, 0:NS]
        read = maps_buf[rows, NS : 2 * NS]
        gram = product_back(read, basis)
        state_low = state_buf[...].astype(bf16)
        states_ref[pl.ds(pl.multiple_of(index * NS, NS), NS), :] = state_low
        carried = product(read, state_low)
        square = jnp.zeros((CHUNK, 1), f32)
        for pair in range(pairs):
            own = slice(pair * LANES, (pair + 1) * LANES)
            inner = inner_buf[rows, own]
            mixing = []
            for head in (2 * pair, 2 * pair + 1):
                spread = jnp.exp(
                    jnp.minimum(running[:, head : head + 1] - running_t[head : head + 1, :], 0.0)
                )
                mixing.append(
                    (gram * spread * mask * step_t[head : head + 1, :]).astype(bf16)
                )
            ssm = product(jnp.concatenate(mixing, axis=1), stacked_pair(inner))
            ssm = ssm + pair_columns(grown, pair) * carried[:, own] + skip_ref[:, own] * inner
            ssm_ref[rows, own] = ssm
            weighted_buf[:, own] = (pair_columns(tail, pair) * inner).astype(bf16)
            gate = gate_buf[rows, own]
            gated = ssm * gate * sigmoid(gate)
            square = square + jnp.sum(gated * gated, axis=1, keepdims=True)
            place = pair * LANES + (pair // group_pairs) * HD
            mixed_ref[rows, place : place + LANES] = (gated * gain_ref[:, own]).astype(bf16)
        square_ref[rows, :] = square
        fresh = outer_sum(basis, weighted_buf[...])
        for pair in range(pairs):
            own = slice(pair * LANES, (pair + 1) * LANES)
            state_buf[:, own] = (
                pair_columns(grown_last, pair) * state_buf[:, own] + fresh[:, own]
            )
        return carry

    lax.fori_loop(0, length // CHUNK, chunk, 0)


def mixer_backward_kernel(
    mix_ref,
    ssm_ref,
    states_ref,
    shared_ref,
    step_ref,
    conv_inner_ref,
    conv_shared_ref,
    head_ref,
    skip_ref,
    gain_ref,
    lanes_ref,
    grad_ref,
    group_factor_ref,
    group_scale_ref,
    factor_ref,
    query_grad_ref,
    mix_grad_ref,
    shared_grad_ref,
    step_grad_ref,
    inner_taps_ref,
    shared_taps_ref,
    head_grad_ref,
    wide_grad_ref,
    total_ref,
    taken_buf,
    inner_buf,
    maps_buf,
    step_buf,
    decay_buf,
    weighted_buf,
    grown_buf,
    inner_grad_buf,
    maps_grad_buf,
    sums_buf,
    state_grad_buf,
):
    pairs = ssm_ref.shape[1] // LANES
    length = ssm_ref.shape[0]
    group_pairs = pairs // (grad_ref.shape[1] // (pairs * LANES // 2 + HD))
    low = low_lanes()
    mix_grad_ref[:, 2 * pairs * LANES :] = query_grad_ref[...]
    for pair in range(pairs):
        first = slice(2 * pair * LANES, (2 * pair + 1) * LANES)
        second = slice((2 * pair + 1) * LANES, (2 * pair + 2) * LANES)
        own = slice(pair * LANES, (pair + 1) * LANES)
        taken = jnp.where(low, pltpu.roll(mix_ref[:, first], PM, 1), mix_ref[:, second])
        taken_buf[:, own] = taken
        taken = conv(taken, conv_inner_ref[:, own])
        inner_buf[:, own] = taken * sigmoid(taken)
    for block in range(shared_ref.shape[1] // LANES):
        own = slice(block * LANES, (block + 1) * LANES)
        taken = conv(shared_ref[:, own], conv_shared_ref[:, own])
        maps_buf[:, own] = (taken * sigmoid(taken)).astype(bf16)
    shifted = step_ref[...] + head_ref[1:2, :]
    steps = softplus(shifted)
    rate = -jnp.exp(head_ref[0:1, :])
    step_buf[...] = steps
    decay_buf[...] = rate * steps
    state_grad_buf[...] = jnp.zeros_like(state_grad_buf)
    head_grad_ref[...] = jnp.zeros_like(head_grad_ref)
    wide_grad_ref[...] = jnp.zeros_like(wide_grad_ref)
    mask = lower_mask()
    chunks = length // CHUNK
    lane_index = lax.broadcasted_iota(jnp.int32, (1, LANES), 1)

    def chunk(turn, carry):
        index = chunks - 1 - turn
        rows = pl.ds(pl.multiple_of(index * CHUNK, CHUNK), CHUNK)
        running = jnp.dot(mask, decay_buf[rows, :], precision=highest, preferred_element_type=f32)
        running_t = running.T
        step = step_buf[rows, :]
        step_t = step.T
        last = running[CHUNK - 1 : CHUNK, :]
        grown = jnp.exp(running)
        fading = jnp.exp(last - running)
        grown_last = jnp.exp(last)
        basis = maps_buf[rows, 0:NS]
        read = maps_buf[rows, NS : 2 * NS]
        gram = product_back(read, basis)
        state_low = states_ref[pl.ds(pl.multiple_of(index * NS, NS), NS), :]
        carried = product(read, state_low)
        state_grad_low = state_grad_buf[...].astype(bf16)
        weighted_grad = product(basis, state_grad_low)
        gram_grad = jnp.zeros((CHUNK, CHUNK), f32)
        decay_grad = jnp.zeros((CHUNK, LANES), f32)
        column_grads = []
        total = jnp.zeros((CHUNK, 1), f32)
        group_factor = group_factor_ref[rows, :]
        group_scale = group_scale_ref[rows, :]
        factor = factor_ref[rows, :]
        for pair in range(pairs):
            first = slice(2 * pair * LANES, (2 * pair + 1) * LANES)
            second = slice((2 * pair + 1) * LANES, (2 * pair + 2) * LANES)
            own = slice(pair * LANES, (pair + 1) * LANES)
            place = pair * LANES + (pair // group_pairs) * HD
            incoming = grad_ref[rows, place : place + LANES]
            head_a = mix_ref[rows, first]
            head_b = mix_ref[rows, second]
            gate = jnp.where(low, head_a, pltpu.roll(head_b, PM, 1))
            gate_sigmoid = sigmoid(gate)
            gate_act = gate * gate_sigmoid
            ssm = ssm_ref[rows, own]
            gated = ssm * gate_act
            wide_grad_ref[0:1, own] += jnp.sum(
                incoming * gated * group_factor, axis=0, keepdims=True
            )
            gated_grad = group_factor * gain_ref[:, own] * incoming - gated * group_scale
            gate_grad = gated_grad * ssm * gate_sigmoid * (1.0 + gate * (1.0 - gate_sigmoid))
            ssm_grad = gated_grad * gate_act
            inner = inner_buf[rows, own]
            wide_grad_ref[1:2, own] += jnp.sum(ssm_grad * inner, axis=0, keepdims=True)
            gate_b = pltpu.roll(gate_grad, PM, 1)
            total = total + jnp.sum(gate_grad * gate, axis=1, keepdims=True)
            mix_grad_ref[rows, first] = jnp.where(low, gate_grad * factor, 0.0).astype(bf16)
            mix_grad_ref[rows, second] = jnp.where(low, gate_b * factor, 0.0).astype(bf16)
            grad_low = ssm_grad.astype(bf16)
            mixing_grad = product_back(grad_low, stacked_pair(inner))
            spreads = []
            for side, head in enumerate((2 * pair, 2 * pair + 1)):
                spread = mask * jnp.exp(
                    jnp.minimum(running[:, head : head + 1] - running_t[head : head + 1, :], 0.0)
                )
                step_row = step_t[head : head + 1, :]
                spread_gram = gram * spread
                spreads.append(spread_gram.astype(bf16))
                own_grad = mixing_grad[:, side * CHUNK : (side + 1) * CHUNK] * step_row
                gram_grad = gram_grad + own_grad * spread
                moved = own_grad * spread_gram
                decay_grad = decay_grad + jnp.where(
                    lane_index == head, jnp.sum(moved, axis=1, keepdims=True), 0.0
                )
                column_grads.append(jnp.sum(moved, axis=0, keepdims=True))
            within = outer_sum(jnp.concatenate(spreads, axis=0), stacked_pair(ssm_grad))
            fading_grad = pair_columns(fading, pair) * weighted_grad[:, own]
            spread_grad = within + fading_grad
            step_wide = pair_columns(step, pair)
            inner_grad_buf[rows, own] = step_wide * spread_grad + skip_ref[:, own] * ssm_grad
            grown_grad = pair_columns(grown, pair) * ssm_grad
            grown_buf[:, own] = grown_grad.astype(bf16)
            weighted_buf[:, own] = (pair_columns(fading, pair) * step_wide * inner).astype(bf16)
            sums_buf[0:CHUNK, own] = (inner * spread_grad).astype(bf16)
            sums_buf[CHUNK : 2 * CHUNK, own] = (inner * fading_grad * step_wide).astype(bf16)
            sums_buf[2 * CHUNK : 3 * CHUNK, own] = (grown_grad * carried[:, own]).astype(bf16)
        head_sums = product(sums_buf[...], lanes_ref[...])
        step_part = head_sums[0:CHUNK, :]
        fading_part = head_sums[CHUNK : 2 * CHUNK, :]
        grown_part = head_sums[2 * CHUNK : 3 * CHUNK, :]
        fill = jnp.zeros((CHUNK - len(column_grads), CHUNK), f32)
        column_grad = jnp.concatenate(column_grads + [fill], axis=0).T
        decay_grad = decay_grad - column_grad + grown_part - fading_part
        state_part = jnp.zeros((1, LANES), f32)
        grown_low = grown_buf[...]
        fresh = outer_sum(read, grown_low)
        for pair in range(pairs):
            own = slice(pair * LANES, (pair + 1) * LANES)
            state_grad = state_grad_buf[:, own]
            held = jnp.sum(state_grad * state_low[:, own].astype(f32), axis=0, keepdims=True)
            for side, head in enumerate((2 * pair, 2 * pair + 1)):
                kept = jnp.where(low if side == 0 else jnp.logical_not(low), held, 0.0)
                state_part = state_part + jnp.where(
                    lane_index == head, jnp.sum(kept, axis=1, keepdims=True), 0.0
                )
            state_grad_buf[:, own] = pair_columns(grown_last, pair) * state_grad + fresh[:, own]
        last_grad = jnp.sum(fading_part, axis=0, keepdims=True) + grown_last * state_part
        decay_sum = (
            lax.dot_general(
                mask,
                decay_grad,
                (((0,), (0,)), ((), ())),
                precision=highest,
                preferred_element_type=f32,
            )
            + last_grad
        )
        raw_shift = step_ref[rows, :] + head_ref[1:2, :]
        raw_grad = (step_part + decay_sum * rate) * sigmoid(raw_shift)
        head_grad_ref[0:1, :] += jnp.sum(decay_sum * decay_buf[rows, :], axis=0, keepdims=True)
        head_grad_ref[1:2, :] += jnp.sum(raw_grad, axis=0, keepdims=True)
        step_grad_ref[rows, :] = (raw_grad * factor).astype(bf16)
        total = total + jnp.sum(raw_grad * step_ref[rows, :], axis=1, keepdims=True)
        total_ref[rows, :] = total
        gram_low = gram_grad.astype(bf16)
        maps_grad_buf[rows, 0:NS] = outer_sum(gram_low, read) + product_back(
            weighted_buf[...], state_grad_low
        )
        maps_grad_buf[rows, NS : 2 * NS] = product(gram_low, basis) + product_back(
            grown_low, state_low
        )
        return carry

    lax.fori_loop(0, chunks, chunk, 0)
    factor = factor_ref[...]
    total = total_ref[...]
    for pair in range(pairs):
        first = slice(2 * pair * LANES, (2 * pair + 1) * LANES)
        second = slice((2 * pair + 1) * LANES, (2 * pair + 2) * LANES)
        own = slice(pair * LANES, (pair + 1) * LANES)
        taken = taken_buf[:, own]
        taps = conv_inner_ref[:, own]
        before = conv(taken, taps)
        before_sigmoid = sigmoid(before)
        grad = inner_grad_buf[:, own] * before_sigmoid * (1.0 + before * (1.0 - before_sigmoid))
        grad, tap_grads = conv_back(grad, taken, taps)
        for tap, tap_grad in enumerate(tap_grads):
            inner_taps_ref[tap : tap + 1, own] = tap_grad
        total = total + jnp.sum(grad * taken, axis=1, keepdims=True)
        grad = grad * factor
        low_a = mix_grad_ref[:, first].astype(f32)
        low_b = mix_grad_ref[:, second].astype(f32)
        mix_grad_ref[:, first] = jnp.where(low, low_a, pltpu.roll(grad, PM, 1)).astype(bf16)
        mix_grad_ref[:, second] = jnp.where(low, low_b, grad).astype(bf16)
    for block in range(shared_ref.shape[1] // LANES):
        own = slice(block * LANES, (block + 1) * LANES)
        taken = shared_ref[:, own]
        taps = conv_shared_ref[:, own]
        before = conv(taken, taps)
        before_sigmoid = sigmoid(before)
        grad = maps_grad_buf[:, own] * before_sigmoid * (1.0 + before * (1.0 - before_sigmoid))
        grad, tap_grads = conv_back(grad, taken, taps)
        for tap, tap_grad in enumerate(tap_grads):
            shared_taps_ref[tap : tap + 1, own] = tap_grad
        total = total + jnp.sum(grad * taken, axis=1, keepdims=True)
        shared_grad_ref[:, own] = (grad * factor).astype(bf16)
    total_ref[...] = total


def call(kernel, outs, scratch, flops, *operands):
    return pl.pallas_call(
        kernel,
        out_shape=outs,
        in_specs=[pl.BlockSpec(memory_space=pltpu.VMEM)] * len(operands),
        out_specs=[pl.BlockSpec(memory_space=pltpu.VMEM)] * len(outs),
        scratch_shapes=scratch,
        compiler_params=pltpu.CompilerParams(vmem_limit_bytes=VMEM_LIMIT),
        cost_estimate=pl.CostEstimate(flops=flops, bytes_accessed=10**6, transcendentals=0),
    )(*operands)


def shape(dims, dtype=f32):
    return jax.ShapeDtypeStruct(dims, dtype)


def mixer_forward(
    own, other, factor, shared, step, taps, shared_taps, heads, skip, gain, attended
):
    length, width = own.shape
    channels = width // 2
    chunks = length // CHUNK
    return call(
        mixer_forward_kernel,
        [
            shape((length, channels + attended.shape[1]), bf16),
            shape((length, 1)),
            shape((length, width)),
            shape((length, channels)),
            shape((chunks * NS, channels), bf16),
        ],
        [
            pltpu.VMEM((length, channels), f32),
            pltpu.VMEM((length, channels), f32),
            pltpu.VMEM((length, 2 * NS), bf16),
            pltpu.VMEM((length, LANES), f32),
            pltpu.VMEM((length, LANES), f32),
            pltpu.VMEM((CHUNK, channels), bf16),
            pltpu.VMEM((NS, channels), f32),
        ],
        10**8,
        own, other, factor, shared, step, taps, shared_taps, heads, skip, gain, attended,
    )


def mixer_backward(
    mix, ssm, states, shared, step, taps, shared_taps, heads, skip, gain, lanes, grad,
    group_factor, group_scale, factor, query_grad,
):
    length, width = mix.shape
    channels = width // 2
    return call(
        mixer_backward_kernel,
        [
            shape((length, width + query_grad.shape[1]), bf16),
            shape((length, 2 * NS), bf16),
            shape((length, LANES), bf16),
            shape((taps.shape[0], channels)),
            shape((taps.shape[0], 2 * NS)),
            shape((8, LANES)),
            shape((8, channels)),
            shape((length, 1)),
        ],
        [
            pltpu.VMEM((length, channels), f32),
            pltpu.VMEM((length, channels), f32),
            pltpu.VMEM((length, 2 * NS), bf16),
            pltpu.VMEM((length, LANES), f32),
            pltpu.VMEM((length, LANES), f32),
            pltpu.VMEM((CHUNK, channels), bf16),
            pltpu.VMEM((CHUNK, channels), bf16),
            pltpu.VMEM((length, channels), f32),
            pltpu.VMEM((length, 2 * NS), f32),
            pltpu.VMEM((3 * CHUNK, channels), bf16),
            pltpu.VMEM((NS, channels), f32),
        ],
        10**8,
        mix, ssm, states, shared, step, taps, shared_taps, heads, skip, gain, lanes, grad,
        group_factor, group_scale, factor, query_grad,
    )


def rotated(values_in, cosine, sine):
    return values_in * cosine + pltpu.roll(values_in, HD // 2, 1) * sine


def rotated_back(grad, cosine, sine):
    return grad * cosine + pltpu.roll(grad * sine, HD // 2, 1)


def attention_forward_kernel(query_ref, pair_ref, cosine_ref, sine_ref, out_ref):
    length = query_ref.shape[0]
    scale = 1.0 / math.sqrt(HD)
    block = min(256, length)
    keys = rotated(pair_ref[:, :HD], cosine_ref[...], sine_ref[...]).astype(bf16)
    vals = pair_ref[:, HD:].astype(bf16)
    for head in range(query_ref.shape[1] // HD):
        lanes = slice(head * HD, (head + 1) * HD)
        queries = rotated(query_ref[:, lanes], cosine_ref[...], sine_ref[...]).astype(bf16)
        for start in range(0, length, block):
            end = start + block
            scores = product_back(queries[start:end], keys[:end]) * scale
            rows = start + lax.broadcasted_iota(jnp.int32, (block, end), 0)
            columns = lax.broadcasted_iota(jnp.int32, (block, end), 1)
            scores = jnp.where(columns <= rows, scores, -1e30)
            exponent = jnp.exp(scores - jnp.max(scores, axis=1, keepdims=True))
            probs = exponent * (1.0 / jnp.sum(exponent, axis=1, keepdims=True))
            out_ref[start:end, lanes] = product(probs.astype(bf16), vals[:end]).astype(bf16)


def attention_backward_kernel(
    query_ref, pair_ref, cosine_ref, sine_ref, grad_ref, factor_ref,
    query_grad_ref, pair_grad_ref, total_ref, key_buf, val_buf,
):
    length = query_ref.shape[0]
    scale = 1.0 / math.sqrt(HD)
    block = min(256, length)
    cosine, sine = cosine_ref[...], sine_ref[...]
    keys = rotated(pair_ref[:, :HD], cosine, sine).astype(bf16)
    vals = pair_ref[:, HD:].astype(bf16)
    heads = query_ref.shape[1] // HD
    group = grad_ref.shape[1] // heads
    key_buf[...] = jnp.zeros_like(key_buf)
    val_buf[...] = jnp.zeros_like(val_buf)
    for head in range(heads):
        lanes = slice(head * HD, (head + 1) * HD)
        queries = rotated(query_ref[:, lanes], cosine, sine).astype(bf16)
        incoming = grad_ref[:, (head + 1) * group - HD : (head + 1) * group].astype(bf16)
        for start in range(0, length, block):
            end = start + block
            scores = product_back(queries[start:end], keys[:end]) * scale
            rows = start + lax.broadcasted_iota(jnp.int32, (block, end), 0)
            columns = lax.broadcasted_iota(jnp.int32, (block, end), 1)
            scores = jnp.where(columns <= rows, scores, -1e30)
            exponent = jnp.exp(scores - jnp.max(scores, axis=1, keepdims=True))
            probs = exponent * (1.0 / jnp.sum(exponent, axis=1, keepdims=True))
            grad_low = incoming[start:end]
            val_buf[:end, :] += outer_sum(probs.astype(bf16), grad_low)
            probs_grad = product_back(grad_low, vals[:end])
            inner = jnp.sum(probs * probs_grad, axis=1, keepdims=True)
            scores_grad = (probs * (probs_grad - inner) * scale).astype(bf16)
            query_grad = rotated_back(
                product(scores_grad, keys[:end]), cosine[start:end], sine[start:end]
            )
            key_buf[:end, :] += outer_sum(scores_grad, queries[start:end])
            taken = query_ref[start:end, lanes]
            part = jnp.sum(query_grad * taken, axis=1, keepdims=True)
            if head == 0:
                total_ref[start:end, :] = part
            else:
                total_ref[start:end, :] += part
            query_grad_ref[start:end, lanes] = (query_grad * factor_ref[start:end, :]).astype(bf16)
    key_grad = rotated_back(key_buf[...], cosine, sine)
    val_grad = val_buf[...]
    total_ref[...] += jnp.sum(
        key_grad * pair_ref[:, :HD] + val_grad * pair_ref[:, HD:], axis=1, keepdims=True
    )
    pair_grad_ref[:, :HD] = (key_grad * factor_ref[...]).astype(bf16)
    pair_grad_ref[:, HD:] = (val_grad * factor_ref[...]).astype(bf16)


def attention_forward(query, pair, cosine, sine):
    return call(
        attention_forward_kernel, [shape(query.shape, bf16)], [], 10**8,
        query, pair, cosine, sine,
    )[0]


def attention_backward(query, pair, cosine, sine, grad, factor):
    length = query.shape[0]
    return call(
        attention_backward_kernel,
        [shape(query.shape, bf16), shape(pair.shape, bf16), shape((length, 1))],
        [pltpu.VMEM((length, HD), f32), pltpu.VMEM((length, HD), f32)],
        10**8,
        query, pair, cosine, sine, grad, factor,
    )


def rope_tables(length):
    half = HD // 2
    inverse = rope_base ** (-jnp.arange(half, dtype=f32) * 2.0 / HD)
    angles = jnp.arange(length, dtype=f32)[:, None] * inverse[None, :]
    cosine, sine = jnp.cos(angles), jnp.sin(angles)
    return jnp.concatenate([cosine, cosine], axis=1), jnp.concatenate([-sine, sine], axis=1)


def to_lanes(values_in):
    return jnp.pad(values_in, ((0, 0), (0, LANES - values_in.shape[1])))


def local(
    tokens,
    norm_first,
    mixer_in,
    query_weight,
    bc_weight,
    step_weight,
    kv_weight,
    conv_inner,
    conv_shared,
    log_rate,
    step_bias,
    skip_gain,
    group_gain,
    out_weight,
    norm_second,
    gate_weight,
    up_weight,
    down_weight,
    cotangent,
):
    length = tokens.shape[0]
    row = lax.axis_index("row")
    col = lax.axis_index("col")
    me = lax.axis_index("dp")
    count = lax.axis_size("dp")
    near = me % 2
    quarter = col * 2 + row
    head_count = log_rate.shape[0]
    channels = group_gain.shape[0]
    kv_flat = kv_weight.reshape(kv_weight.shape[0], -1)
    residual = tokens.astype(f32)
    spine = Spine(jnp.zeros((1, LANES), f32))

    def column_share(weight):
        rows, columns = weight.shape[0] // count, weight.shape[1] // 2
        return lax.dynamic_slice(weight, (me * rows, (1 - row) * columns), (rows, columns))

    half_rows = out_weight.shape[0] // 2
    share_rows = half_rows // count
    out_own = part_of(out_weight, row, 0)
    gate_own, up_own = part_of(gate_weight, row, 1), part_of(up_weight, row, 1)
    out_share = lax.dynamic_slice_in_dim(
        out_weight, (1 - row) * half_rows + me * share_rows, share_rows, 0
    )
    ffn_share = jnp.concatenate([column_share(gate_weight), column_share(up_weight)], axis=1)
    out_share, ffn_share, residual = tie(out_share, ffn_share, residual)
    out_spread = Spread(swap(out_share, "row"))
    ffn_spread = Spread(swap(ffn_share, "row"))

    first_own = (residual * norm_first).astype(bf16)
    first_half = in_order(first_own, swap(first_own, "col"), col, 1)
    square_first = jnp.sum(residual * residual, axis=1)
    square_first = square_first + swap(square_first, "col")
    square_far = swap(square_first, "row")
    query_own = product(first_half, part_of(query_weight, row, 1))
    query_out = product(first_half, part_of(query_weight, 1 - row, 1)).astype(bf16)
    pair_own = product(first_half, kv_flat)
    shared_own = product(first_half, bc_weight)
    step_own = product(first_half, step_weight)
    query_width = query_own.shape[1]
    pair_width = pair_own.shape[1]
    shared_width = shared_own.shape[1]
    early = swap(
        jnp.concatenate(
            [
                query_out,
                pair_own.astype(bf16),
                part_of(shared_own, col, 1).astype(bf16),
                to_lanes(step_own).astype(bf16),
            ],
            axis=1,
        ),
        "row",
    )
    mix_out = product(first_half, part_of(mixer_in, 1 - row, 1)).astype(bf16)
    mix_own = product(first_half, part_of(mixer_in, row, 1))
    cot_near = swap_dp(cotangent, 1)
    cot_half = in_order(cotangent, swap(cotangent, "col"), col, 1)
    hidden_back = product_back(cot_half, part_of(down_weight, 1 - row, 0)).astype(bf16)
    hidden_back_own = product_back(cot_half, part_of(down_weight, row, 0))

    out_spread.wait(spine)
    out_spread.level()
    ffn_spread.wait(spine)
    ffn_spread.level()
    cot_near, early, square_far, mix_out = spine.wait(cot_near, early, square_far, mix_out)
    mix_other = swap(mix_out, "row")
    out_spread.wait(spine)
    out_spread.level()
    first_factor = lax.rsqrt((square_first + square_far) / D + norm_epsilon)
    first_column = first_factor[:, None]
    query_sum = (query_own + early[:, :query_width].astype(f32)) * first_column
    place = query_width
    pair_sum = (pair_own + early[:, place : place + pair_width].astype(f32)) * first_column
    place += pair_width
    shared_sum = (
        part_of(shared_own, col, 1) + early[:, place : place + shared_width // 2].astype(f32)
    ) * first_column
    shared_sum = in_order(
        shared_sum, swap(shared_sum.astype(bf16), "col").astype(f32), col, 1
    )
    place += shared_width // 2
    step_sum = (
        step_own + early[:, place : place + step_own.shape[1]].astype(f32)
    ) * first_column
    step_sum = to_lanes(lax.dynamic_slice_in_dim(step_sum, quarter * head_count, head_count, 1))
    ffn_spread.wait(spine)
    ffn_spread.level()
    cosine, sine = rope_tables(length)
    attended = attention_forward(query_sum, pair_sum, cosine, sine)
    heads = to_lanes(jnp.stack([log_rate, step_bias] + [jnp.zeros_like(log_rate)] * 6))
    skip_wide = jnp.repeat(skip_gain, PM)[None, :]
    gain_wide = group_gain[None, :]
    out_spread.wait(spine)
    out_spread.level()
    out_other = out_spread.finish(spine)
    mix_other, hidden_back, attended, shared_sum, step_sum = spine.wait(
        mix_other, hidden_back, attended, shared_sum, step_sum
    )
    hidden_back = swap(hidden_back, "row")
    mixed_raw, square, mix_sum, ssm, states = mixer_forward(
        mix_own, mix_other, first_column, shared_sum, step_sum, conv_inner, conv_shared,
        heads, skip_wide, gain_wide, attended,
    )
    square, hidden_back = spine.wait(square, hidden_back)
    square_total = square[:, 0] + swap(square[:, 0], "col")
    square_far = swap(square_total, "row")
    ffn_spread.wait(spine)
    ffn_spread.level()
    square_far = spine.wait(square_far)
    group_factor = lax.rsqrt((square_total + square_far) / (HM * PM) + norm_epsilon)
    groups = attended.shape[1] // HD
    group_width = mixed_raw.shape[1] // groups
    is_normed = jnp.arange(mixed_raw.shape[1])[None, :] % group_width < group_width - HD
    mixed = (
        mixed_raw.astype(f32) * jnp.where(is_normed, group_factor[:, None], 1.0)
    ).astype(bf16)

    out_far = sum_cols(product(mixed, out_other), col)
    out_far = swap(out_far.astype(bf16), "row")
    out_near = sum_cols(product(mixed, out_own), col)
    ffn_other = ffn_spread.finish(spine)
    out_far = spine.wait(out_far)
    second = residual + out_near + out_far.astype(f32)
    second_own = (second * norm_second).astype(bf16)
    second_far = swap(second_own, "row")
    second_half = in_order(second_own, swap(second_own, "col"), col, 1)
    second_near = swap_dp(second_own, 1)
    second_square = jnp.sum(second * second, axis=1)
    second_square = second_square + swap(second_square, "col")
    second_square_far = swap(second_square, "row")
    gate_width = gate_own.shape[1]
    gate_part, up_part = product(second_half, gate_own), product(second_half, up_own)
    second_far, second_near, first_send = spine.wait(second_far, second_near, first_own)
    second_far_near = swap_dp(second_far, 1)
    first_row = swap(first_send, "row")
    first_near = swap_dp(first_send, 1)
    second_far = in_order(second_far, swap(second_far, "col"), col, 1)
    second_near = in_order(second_near, swap(second_near, "col"), col, 1)
    second_factor = lax.rsqrt((second_square + second_square_far) / D + norm_epsilon)
    second_column = second_factor[:, None]
    gate_sum = (gate_part + product(second_far, ffn_other[:, :gate_width])) * second_column
    up_sum = (up_part + product(second_far, ffn_other[:, gate_width:])) * second_column
    gate_sigmoid = jax.nn.sigmoid(gate_sum)
    gate_act = gate_sum * gate_sigmoid
    hidden_grad = hidden_back_own + hidden_back.astype(f32)
    gate_grad = hidden_grad * up_sum * gate_sigmoid * (1.0 + gate_sum * (1.0 - gate_sigmoid))
    up_grad = hidden_grad * gate_act
    hidden = (gate_act * up_sum).astype(bf16)
    ffn_grad = jnp.concatenate(
        [(gate_grad * second_column).astype(bf16), (up_grad * second_column).astype(bf16)], axis=1
    )
    second_total = jnp.sum(gate_grad * gate_sum + up_grad * up_sum, axis=1)
    second_total = second_total + swap(second_total, "col")
    second_total_far = swap(second_total, "row")
    ffn_send = swap_dp(part_of(ffn_grad, 1 - near, 1), 1)
    back_far = sum_cols(product_back(ffn_grad, ffn_other), col).astype(bf16)
    second_far_near = spine.wait(second_far_near)
    second_far_near = in_order(second_far_near, swap(second_far_near, "col"), col, 1)
    second_total_far, back_far, first_row, first_near = spine.wait(
        second_total_far, back_far, first_row, first_near
    )
    back_far = swap(back_far, "row")
    back_near = sum_cols(
        product_back(ffn_grad[:, :gate_width], gate_own)
        + product_back(ffn_grad[:, gate_width:], up_own),
        col,
    )
    first_pair_col = swap(jnp.concatenate([first_row, first_near], axis=1), "col")
    size = first_row.shape[1]
    first_far = in_order(first_row, first_pair_col[:, :size], col, 1)
    first_near = in_order(first_near, first_pair_col[:, size:], col, 1)
    back_far, ffn_send, first_far, first_near = spine.wait(
        back_far, ffn_send, first_far, first_near
    )
    second_in_grad = back_near + back_far.astype(f32)
    second_grad = (
        cotangent.astype(f32)
        + norm_second * second_in_grad
        - second * (second_factor**2 * (second_total + second_total_far) / D)[:, None]
    )
    norm_second_grad = jnp.sum(second_in_grad * second, axis=0)
    branch = second_grad.astype(bf16)
    branch_far = swap(branch, "row")
    branch_half = in_order(branch, swap(branch, "col"), col, 1)

    def both_halves(scattered, sent):
        kept = lax.dynamic_index_in_dim(scattered, near, 0, keepdims=False)
        return jnp.where(near == 0, kept, sent), jnp.where(near == 0, sent, kept)

    def to_neighbour(scattered):
        return swap_dp(lax.dynamic_index_in_dim(scattered, 1 - near, 0, keepdims=False), 1)

    branch_half = spine.wait(branch_half)
    ffn_kept = part_of(ffn_grad, near, 1)
    blocks = count // 2
    ffn_sums = call(
        both_rows_kernel,
        [shape((blocks, 2, second_half.shape[1] // blocks, ffn_kept.shape[1]), bf16)],
        [pltpu.VMEM((second_half.shape[1], ffn_kept.shape[1]), f32)],
        10**6,
        second_half, second_far, second_near, second_far_near, ffn_kept, ffn_send,
    )[0]
    ffn_sums = spine.wait(ffn_sums)
    ffn_sums = far_sum(ffn_sums.reshape(-1, ffn_kept.shape[1]))
    mixed_send, hidden_send = spine.wait(mixed, hidden)
    near_pack = jnp.concatenate(
        [
            near_blocks(mixed_send, 1 - near),
            branch,
            near_blocks(hidden_send, 1 - near),
            first_row,
        ],
        axis=1,
    )
    near_pack = swap_dp(near_pack, 1)
    branch_far = spine.wait(branch_far)
    branch_far = in_order(branch_far, swap(branch_far, "col"), col, 1)
    mixed_grad = product_back(branch_half, out_own) + product_back(branch_far, out_other)

    group_total = jnp.sum(jnp.where(is_normed, mixed_grad * mixed.astype(f32), 0.0), axis=1)
    group_total = group_total + swap(group_total, "col")
    group_total_far = swap(group_total, "row")
    query_grad, pair_grad, attention_total = attention_backward(
        query_sum, pair_sum, cosine, sine, mixed_grad, first_column
    )
    group_total_far, attention_total = spine.wait(group_total_far, attention_total)
    group_scale = group_factor**2 * (group_total + group_total_far) / (HM * PM)

    def piece(pack, turn):
        return pack[:, turn * size : (turn + 1) * size]

    group_scale, mixed_kept = spine.wait(group_scale, near_blocks(mixed, near))
    mixed_kept_far = swap(mixed_kept, "row")
    lanes = (
        jnp.arange(channels)[:, None] // PM == jnp.arange(LANES)[None, :]
    ).astype(bf16)
    (
        own_grads,
        shared_grad,
        step_grad,
        conv_inner_grad,
        conv_shared_part,
        head_grads,
        wide_grads,
        mixer_total,
    ) = mixer_backward(
        mix_sum, ssm, states, shared_sum, step_sum, conv_inner, conv_shared, heads, skip_wide,
        gain_wide, lanes, mixed_grad, group_factor[:, None], group_scale[:, None], first_column,
        query_grad,
    )
    mixed_kept_far = spine.wait(mixed_kept_far)
    own_grads, shared_grad, near_pack = spine.wait(own_grads, shared_grad, near_pack)
    mix_width = mix_sum.shape[1]
    grads_send = swap_dp(part_of(own_grads, 1 - near, 1), 1)
    grads_kept = part_of(own_grads, near, 1)
    shared_low = (shared_grad.astype(f32) + swap(shared_grad, "col").astype(f32)).astype(bf16)
    late = jnp.concatenate([part_of(shared_low, col, 1), pair_grad, step_grad], axis=1)
    late_far = swap(late, "row")
    first_far_near = piece(near_pack, 3)
    first_far_near = in_order(first_far_near, swap(first_far_near, "col"), col, 1)
    grads_send, mixed_send, hidden_send = spine.wait(
        grads_send, piece(near_pack, 0), piece(near_pack, 2)
    )
    near_far = swap(jnp.concatenate([mixed_send, hidden_send], axis=1), "row")
    mixer_scatter_far = Scatter(
        spine,
        (outer_sum(first_far, grads_kept) + outer_sum(first_far_near, grads_send)).astype(bf16),
        True,
    )
    late_far, mixer_scatter_far.parts = spine.wait(late_far, mixer_scatter_far.parts)
    half = shared_width // 2
    late_sum = (
        late[:, : half + pair_width].astype(f32) + late_far[:, : half + pair_width].astype(f32)
    ).astype(bf16)
    shared_part, pair_low = late_sum[:, :half], late_sum[:, half:]
    step_two = in_order(
        late[:, half + pair_width :][:, :head_count],
        late_far[:, half + pair_width :][:, :head_count],
        row,
        1,
    )
    step_all = in_order(step_two, swap(step_two, "col"), col, 1)
    rest = jnp.concatenate(
        [pair_low, shared_part, to_lanes(step_all), jnp.zeros((length, LANES), bf16)], axis=1
    )
    rest_send = swap_dp(part_of(rest, 1 - near, 1), 1)
    rest_send = spine.wait(rest_send)
    mixer_scatter = Scatter(
        spine,
        (
            outer_sum(
                first_half, jnp.concatenate([grads_kept, part_of(rest, near, 1)], axis=1)
            )
            + outer_sum(first_near, jnp.concatenate([grads_send, rest_send], axis=1))
        ).astype(bf16),
        True,
    )
    near_far, mixer_scatter.parts, hidden_send, ffn_sums = spine.wait(
        near_far, mixer_scatter.parts, hidden, ffn_sums
    )
    hidden_far = swap(hidden_send, "row")
    mixed_kept = in_order(mixed_kept, mixed_kept_far, row, 1)
    mixed_near = in_order(piece(near_pack, 0), piece(near_far, 0), row, 1)
    branch_near = in_order(piece(near_pack, 1), swap(piece(near_pack, 1), "col"), col, 1)
    out_sums = far_sum(
        spine.wait(
            (
                outer_sum(mixed_kept, branch_half) + outer_sum(mixed_near, branch_near)
            ).astype(bf16)
        )
    )
    ffn_sums = ffn_sums.reshape(2, 2, -1, ffn_kept.shape[1])
    ffn_sent = swap_dp(lax.dynamic_index_in_dim(ffn_sums, 1 - near, 1, keepdims=False), 1)
    mixer_scatter_far.add()
    hidden_far, grads_again = spine.wait(hidden_far, own_grads)
    own_grads_far = swap(grads_again, "row")
    hidden_half = in_order(hidden, hidden_far, row, 1)
    hidden_near = in_order(piece(near_pack, 2), piece(near_far, 1), row, 1)
    cot_near = in_order(cot_near, swap(cot_near, "col"), col, 1)
    down_sums = far_sum(
        spine.wait(
            (
                outer_sum(near_blocks(hidden_half, near), cot_half)
                + outer_sum(hidden_near, cot_near)
            ).astype(bf16)
        )
    )
    ffn_sent, layer_half = spine.wait(ffn_sent, hidden_half)
    ffn_near = both_halves(ffn_sums[0], ffn_sent[0])
    ffn_far = swap(jnp.stack(both_halves(ffn_sums[1], ffn_sent[1])), "row")
    mixer_scatter.add()
    layer_out = (second + sum_cols(product(layer_half, down_weight), col)).astype(bf16)
    mixer_far = mixer_scatter_far.finish()
    mixer_far_sent = to_neighbour(mixer_far)
    first_total, conv_shared_part, own_grads_far = spine.wait(
        (attention_total + mixer_total)[:, 0], conv_shared_part, own_grads_far
    )
    first_total = first_total + swap(first_total, "col")
    first_total_far = swap(first_total, "row")
    conv_shared_sum = conv_shared_part + swap(conv_shared_part, "col")
    conv_shared_far = swap(conv_shared_sum, "row")
    mix_half = in_order(own_grads[:, :mix_width], own_grads_far[:, :mix_width], row, 1)
    query_half = in_order(own_grads[:, mix_width:], own_grads_far[:, mix_width:], row, 1)
    shared_low = in_order(shared_part, swap(shared_part, "col"), col, 1)
    first_in_partial = (
        product_back(mix_half, mixer_in)
        + product_back(query_half, query_weight)
        + product_back(pair_low, kv_flat)
        + 0.5 * (product_back(shared_low, bc_weight) + product_back(step_all, step_weight))
    )
    first_in_grad = sum_cols(first_in_partial, col)
    mixer_far_sent, first_total_far, conv_shared_far = spine.wait(
        mixer_far_sent, first_total_far, conv_shared_far
    )
    mixer_far = swap(jnp.concatenate(both_halves(mixer_far, mixer_far_sent), axis=1), "row")
    input_grad = (
        second_grad
        + norm_first * first_in_grad
        - residual * (first_factor**2 * (first_total + first_total_far) / D)[:, None]
    )
    norm_first_grad = jnp.sum(first_in_grad * residual, axis=0)
    conv_shared_sum = conv_shared_sum + conv_shared_far
    skip_grad = wide_grads[1].reshape(head_count, PM).sum(axis=1)
    pieces = [
        norm_first_grad,
        norm_second_grad,
        conv_inner_grad.reshape(-1),
        conv_shared_sum.reshape(-1),
        wide_grads[0],
        jnp.pad(head_grads[0, :head_count], (0, LANES - head_count)),
        jnp.pad(head_grads[1, :head_count], (0, LANES - head_count)),
        jnp.pad(skip_grad, (0, LANES - head_count)),
    ]
    small = jnp.concatenate(pieces).reshape(-1, LANES)
    bits = dp_bits()
    small_far = swap_dp(small, bits[0])
    ffn_far = spine.wait(ffn_far)
    gate_weight_grad = in_order(ffn_near[0], ffn_far[0], row, 1).astype(f32)
    up_weight_grad = in_order(ffn_near[1], ffn_far[1], row, 1).astype(f32)
    small = small + spine.wait(small_far)
    small_far = swap_dp(small, bits[1])
    out_weight_grad, down_weight_grad = spine.wait(out_sums, down_sums)
    mixer_near = mixer_scatter.finish()
    mixer_near_sent = to_neighbour(mixer_near)
    small_far, mixer_far = spine.wait(small_far, mixer_far)
    small = small + small_far
    small_far = swap_dp(small, bits[2])
    mixer_near_sent = spine.wait(mixer_near_sent)
    mixer_near = both_halves(mixer_near, mixer_near_sent)
    kept_width = grads_kept.shape[1]
    own_sums = jnp.concatenate([mixer_near[0][:, :kept_width], mixer_near[1][:, :kept_width]], axis=1)
    rest_sums = jnp.concatenate(
        [mixer_near[0][:, kept_width:], mixer_near[1][:, kept_width:]], axis=1
    ).astype(f32)
    mixer_in_grad = in_order(own_sums[:, :mix_width], mixer_far[:, :mix_width], row, 1).astype(f32)
    query_weight_grad = in_order(
        own_sums[:, mix_width:], mixer_far[:, mix_width:], row, 1
    ).astype(f32)
    kv_weight_grad = rest_sums[:, :pair_width].reshape((-1,) + kv_weight.shape[1:])
    place = pair_width
    bc_own = rest_sums[:, place : place + shared_width // 2].astype(bf16)
    bc_weight_grad = in_order(bc_own, swap(bc_own, "col"), col, 1).astype(f32)
    place += shared_width // 2
    step_weight_grad = rest_sums[:, place : place + step_weight.shape[1]]
    for bit in bits[3:]:
        small = small + spine.wait(small_far)
        small_far = swap_dp(small, bit)
    small = small + spine.wait(small_far)
    out_weight_grad, down_weight_grad = out_weight_grad.astype(f32), down_weight_grad.astype(f32)
    small = (small + spine.token).reshape(-1)
    sums, place = [], 0
    for piece in pieces:
        sums.append(small[place : place + piece.shape[0]])
        place += piece.shape[0]

    def own_block(values_in, axis):
        size = values_in.shape[axis] // count
        return lax.dynamic_slice_in_dim(values_in, me * size, size, axis)

    return (
        layer_out,
        input_grad,
        own_block(sums[0], 0),
        mixer_in_grad,
        query_weight_grad,
        bc_weight_grad,
        step_weight_grad,
        kv_weight_grad,
        own_block(sums[2].reshape(conv_inner.shape), 1),
        own_block(sums[3].reshape(conv_shared.shape), 1),
        sums[5][:head_count],
        sums[6][:head_count],
        sums[7][:head_count],
        own_block(sums[4], 0),
        out_weight_grad,
        own_block(sums[1], 0),
        gate_weight_grad,
        up_weight_grad,
        down_weight_grad,
    )


def solution(mesh):
    in_specs = (
        P("dp", ("row", "col")),
        P(("row", "col")),
        P("row", "col"),
        P("row", "col"),
        P("row", None),
        P("row", None),
        P("row", "col", None),
        P(None, ("col", "row")),
        P(),
        P(("col", "row")),
        P(("col", "row")),
        P(("col", "row")),
        P(("col", "row")),
        P("col", "row"),
        P(("row", "col")),
        P("row", "col"),
        P("row", "col"),
        P("col", "row"),
        P("dp", ("row", "col")),
    )
    out_specs = (
        P("dp", ("row", "col")),
        P("dp", ("row", "col")),
        P(("row", "col", "dp")),
        P(("row", "dp"), "col"),
        P(("row", "dp"), "col"),
        P(("row", "dp"), None),
        P(("row", "dp"), None),
        P(("row", "dp"), "col", None),
        P(None, ("col", "row", "dp")),
        P(None, "dp"),
        P(("col", "row")),
        P(("col", "row")),
        P(("col", "row")),
        P(("col", "row", "dp")),
        P(("col", "dp"), "row"),
        P(("row", "col", "dp")),
        P(("row", "dp"), "col"),
        P(("row", "dp"), "col"),
        P(("col", "dp"), "row"),
    )
    return jax.shard_map(local, mesh=mesh, in_specs=in_specs, out_specs=out_specs, check_vma=False)
```

```python
from functools import partial
import math

import jax
import jax.numpy as jnp
from jax import lax
from jax.experimental import pallas as pl
from jax.experimental.pallas import tpu as pltpu
from jax.sharding import PartitionSpec as P

D = 2048
HM = 48
PM = 64
NS = 256
HD = 128
MIX = 4096
LANES = 128
CHUNK = 128

norm_epsilon = 1e-05
rope_base = 10000.0
highest = lax.Precision.HIGHEST
f32 = jnp.float32
bf16 = jnp.bfloat16
VMEM_LIMIT = 56 * 1024 * 1024


def product(left_side, right_side):
    return jnp.dot(left_side, right_side, preferred_element_type=f32)


def product_back(left_side, right_side):
    return lax.dot_general(
        left_side, right_side, (((1,), (1,)), ((), ())), preferred_element_type=f32
    )


def outer_sum(left_side, right_side):
    return lax.dot_general(
        left_side, right_side, (((0,), (0,)), ((), ())), preferred_element_type=f32
    )


def swap(values_in, axis):
    return lax.ppermute(values_in, axis, [(0, 1), (1, 0)])


def in_order(own, other, place, axis):
    return jnp.concatenate(
        [jnp.where(place == 0, own, other), jnp.where(place == 0, other, own)], axis=axis
    )


def part_of(values_in, place, axis):
    size = values_in.shape[axis] // 2
    return lax.dynamic_slice_in_dim(values_in, place * size, size, axis)


def rows_total(values_in):
    values_in = values_in + swap(values_in, "col")
    return values_in + swap(values_in, "row")


def sum_cols(values_in, col):
    sent = swap(part_of(values_in, 1 - col, 1).astype(bf16), "col")
    return part_of(values_in, col, 1) + sent.astype(f32)


def near_blocks(values_in, near):
    size = MIX // 2 // lax.axis_size("dp")
    places = range(0, values_in.shape[1], 2 * size)
    return jnp.concatenate(
        [
            jnp.where(
                near == 0,
                values_in[:, place : place + size],
                values_in[:, place + size : place + 2 * size],
            )
            for place in places
        ],
        axis=1,
    )


def dp_bits():
    bits, bit = [], 1
    while bit < lax.axis_size("dp"):
        bits.append(bit)
        bit *= 2
    return bits


def swap_dp(values_in, bit):
    return lax.ppermute(values_in, "dp", [(i, i ^ bit) for i in range(lax.axis_size("dp"))])


def tie(*values_in):
    return lax.optimization_barrier(values_in)


class Spine:
    def __init__(self, token):
        self.token = token

    def wait(self, *values_in):
        tied = tie(self.token, *values_in)
        self.token = tied[0]
        return tied[1] if len(tied) == 2 else tied[1:]


class Scatter:
    def __init__(self, spine, grads, pairs, dtype=bf16):
        self.spine, self.dtype = spine, dtype
        self.bits = dp_bits()[1:]
        blocks = lax.axis_size("dp") // 2 * (2 if pairs else 1)
        rest = (blocks // 2 ** len(self.bits), grads.shape[0] // blocks) + grads.shape[1:]
        self.left = self.bits[::-1]
        self.parts = grads.reshape((2,) * len(self.bits) + rest)
        self.send()

    def send(self):
        bit = self.bits[len(self.bits) - len(self.left)]
        axis = self.left.index(bit)
        mine = (lax.axis_index("dp") // bit) % 2
        send = lax.dynamic_index_in_dim(self.parts, 1 - mine, axis, keepdims=False)
        self.parts = lax.dynamic_index_in_dim(self.parts, mine, axis, keepdims=False)
        self.arrived = swap_dp(send, bit)
        self.left.pop(axis)

    def add(self):
        arrived = self.spine.wait(self.arrived)
        total = self.parts.astype(f32) + arrived.astype(f32)
        self.parts = total.astype(bf16 if self.left else self.dtype)
        if self.left:
            self.send()

    def finish(self):
        while self.left:
            self.add()
        self.add()
        return self.parts


def far_sum(grads):
    count = lax.axis_size("dp")
    groups = [list(range(start, count, 2)) for start in range(2)]
    return lax.psum_scatter(
        grads, "dp", scatter_dimension=0, axis_index_groups=groups, tiled=True
    )


def both_rows_kernel(own_ref, far_ref, near_ref, far_near_ref, kept_ref, sent_ref, out_ref, sums):
    blocks, _, rows, _ = out_ref.shape
    for side, left_ref, right_ref in ((0, own_ref, near_ref), (1, far_ref, far_near_ref)):
        sums[...] = outer_sum(left_ref[...], kept_ref[...]) + outer_sum(
            right_ref[...], sent_ref[...]
        )
        for block in range(blocks):
            out_ref[block, side] = sums[block * rows : (block + 1) * rows, :].astype(bf16)


def place_kernel(count, owners, where_ref, *refs):
    pieces, out_ref = refs[:count], refs[count]
    rows = pieces[0].shape[0]
    for turn in range(count):
        start = pl.multiple_of((where_ref[0] ^ owners[turn]) * rows, rows)
        out_ref[pl.ds(start, rows), :] = pieces[turn][...]


def place_pieces(pieces, owners):
    count = len(pieces)
    rows, columns = pieces[0].shape
    return pl.pallas_call(
        partial(place_kernel, count, owners),
        out_shape=jax.ShapeDtypeStruct((count * rows, columns), pieces[0].dtype),
        in_specs=[pl.BlockSpec(memory_space=pltpu.SMEM)]
        + [pl.BlockSpec(memory_space=pltpu.VMEM)] * count,
        out_specs=pl.BlockSpec(memory_space=pltpu.VMEM),
        compiler_params=pltpu.CompilerParams(vmem_limit_bytes=VMEM_LIMIT),
        cost_estimate=pl.CostEstimate(
            flops=0, bytes_accessed=4 * count * rows * columns, transcendentals=0
        ),
    )(lax.axis_index("dp").astype(jnp.int32)[None], *pieces)


class Spread:
    def __init__(self, mine):
        self.pieces, self.owners = [mine], [0]
        self.bits = [dp_bits()[::-1]]
        self.first = 0

    def wait(self, spine):
        arrived = spine.wait(*self.pieces[self.first :])
        self.pieces[self.first :] = arrived if isinstance(arrived, (tuple, list)) else [arrived]

    def level(self):
        start, self.first = self.first, len(self.pieces)
        sends = [
            (-bit, turn) for turn in range(start, self.first) for bit in self.bits[turn]
        ]
        for bit, turn in sorted(sends):
            self.pieces.append(swap_dp(self.pieces[turn], -bit))
            self.owners.append(self.owners[turn] ^ -bit)
            self.bits.append([lower for lower in self.bits[turn] if lower < -bit])

    def finish(self, spine):
        self.wait(spine)
        while len(self.pieces) < lax.axis_size("dp"):
            self.level()
            self.wait(spine)
        return place_pieces(self.pieces, self.owners)


def sigmoid(values_in):
    return 1.0 / (1.0 + jnp.exp(-values_in))


def softplus(values_in):
    return jnp.maximum(values_in, 0.0) + jnp.log1p(jnp.exp(-jnp.abs(values_in)))


def low_lanes():
    return lax.broadcasted_iota(jnp.int32, (1, LANES), 1) < PM


def pair_columns(values_in, pair):
    return jnp.where(
        low_lanes(), values_in[:, 2 * pair : 2 * pair + 1], values_in[:, 2 * pair + 1 : 2 * pair + 2]
    )


def shift_down(values_in, count):
    if count == 0:
        return values_in
    rows = lax.broadcasted_iota(jnp.int32, values_in.shape, 0)
    return jnp.where(rows >= count, pltpu.roll(values_in, count, 0), 0.0)


def shift_up(values_in, count):
    if count == 0:
        return values_in
    length = values_in.shape[0]
    rows = lax.broadcasted_iota(jnp.int32, values_in.shape, 0)
    return jnp.where(rows < length - count, pltpu.roll(values_in, length - count, 0), 0.0)


def conv(values_in, taps):
    count = taps.shape[0]
    total = values_in * taps[count - 1 : count, :]
    for tap in range(count - 1):
        total = total + taps[tap : tap + 1, :] * shift_down(values_in, count - 1 - tap)
    return total


def conv_back(grad, values_in, taps):
    count = taps.shape[0]
    total = grad * taps[count - 1 : count, :]
    for tap in range(count - 1):
        total = total + taps[tap : tap + 1, :] * shift_up(grad, count - 1 - tap)
    tap_grads = [
        jnp.sum(grad * shift_down(values_in, count - 1 - tap), axis=0, keepdims=True)
        for tap in range(count)
    ]
    return total, tap_grads


def stacked_pair(values_in):
    low = low_lanes()
    return jnp.concatenate(
        [jnp.where(low, values_in, 0.0), jnp.where(low, 0.0, values_in)], axis=0
    ).astype(bf16)


def lower_mask():
    rows = lax.broadcasted_iota(jnp.int32, (CHUNK, CHUNK), 0)
    columns = lax.broadcasted_iota(jnp.int32, (CHUNK, CHUNK), 1)
    return (rows >= columns).astype(f32)


def mixer_forward_kernel(
    own_ref,
    other_ref,
    factor_ref,
    shared_ref,
    step_ref,
    conv_inner_ref,
    conv_shared_ref,
    head_ref,
    skip_ref,
    gain_ref,
    attended_ref,
    mixed_ref,
    square_ref,
    mix_ref,
    ssm_ref,
    states_ref,
    inner_buf,
    gate_buf,
    maps_buf,
    step_buf,
    decay_buf,
    weighted_buf,
    state_buf,
):
    pairs = ssm_ref.shape[1] // LANES
    length = own_ref.shape[0]
    groups = attended_ref.shape[1] // HD
    group_pairs = pairs // groups
    low = low_lanes()
    factor = factor_ref[...]
    for group in range(groups):
        place = ((group + 1) * group_pairs + group) * LANES
        mixed_ref[:, place : place + HD] = attended_ref[:, group * HD : (group + 1) * HD]
    for pair in range(pairs):
        first = slice(2 * pair * LANES, (2 * pair + 1) * LANES)
        second = slice((2 * pair + 1) * LANES, (2 * pair + 2) * LANES)
        own = slice(pair * LANES, (pair + 1) * LANES)
        head_a = (own_ref[:, first] + other_ref[:, first].astype(f32)) * factor
        head_b = (own_ref[:, second] + other_ref[:, second].astype(f32)) * factor
        mix_ref[:, first] = head_a
        mix_ref[:, second] = head_b
        taken = jnp.where(low, pltpu.roll(head_a, PM, 1), head_b)
        gate_buf[:, own] = jnp.where(low, head_a, pltpu.roll(head_b, PM, 1))
        taken = conv(taken, conv_inner_ref[:, own])
        inner_buf[:, own] = taken * sigmoid(taken)
    for block in range(shared_ref.shape[1] // LANES):
        own = slice(block * LANES, (block + 1) * LANES)
        taken = conv(shared_ref[:, own], conv_shared_ref[:, own])
        maps_buf[:, own] = (taken * sigmoid(taken)).astype(bf16)
    steps = softplus(step_ref[...] + head_ref[1:2, :])
    step_buf[...] = steps
    decay_buf[...] = -jnp.exp(head_ref[0:1, :]) * steps
    state_buf[...] = jnp.zeros_like(state_buf)
    mask = lower_mask()

    def chunk(index, carry):
        rows = pl.ds(pl.multiple_of(index * CHUNK, CHUNK), CHUNK)
        running = jnp.dot(mask, decay_buf[rows, :], precision=highest, preferred_element_type=f32)
        running_t = running.T
        step = step_buf[rows, :]
        step_t = step.T
        last = running[CHUNK - 1 : CHUNK, :]
        grown = jnp.exp(running)
        tail = jnp.exp(last - running) * step
        grown_last = jnp.exp(last)
        basis = maps_buf[rows, 0:NS]
        read = maps_buf[rows, NS : 2 * NS]
        gram = product_back(read, basis)
        state_low = state_buf[...].astype(bf16)
        states_ref[pl.ds(pl.multiple_of(index * NS, NS), NS), :] = state_low
        carried = product(read, state_low)
        square = jnp.zeros((CHUNK, 1), f32)
        for pair in range(pairs):
            own = slice(pair * LANES, (pair + 1) * LANES)
            inner = inner_buf[rows, own]
            mixing = []
            for head in (2 * pair, 2 * pair + 1):
                spread = jnp.exp(
                    jnp.minimum(running[:, head : head + 1] - running_t[head : head + 1, :], 0.0)
                )
                mixing.append(
                    (gram * spread * mask * step_t[head : head + 1, :]).astype(bf16)
                )
            ssm = product(jnp.concatenate(mixing, axis=1), stacked_pair(inner))
            ssm = ssm + pair_columns(grown, pair) * carried[:, own] + skip_ref[:, own] * inner
            ssm_ref[rows, own] = ssm
            weighted_buf[:, own] = (pair_columns(tail, pair) * inner).astype(bf16)
            gate = gate_buf[rows, own]
            gated = ssm * gate * sigmoid(gate)
            square = square + jnp.sum(gated * gated, axis=1, keepdims=True)
            place = pair * LANES + (pair // group_pairs) * HD
            mixed_ref[rows, place : place + LANES] = (gated * gain_ref[:, own]).astype(bf16)
        square_ref[rows, :] = square
        fresh = outer_sum(basis, weighted_buf[...])
        for pair in range(pairs):
            own = slice(pair * LANES, (pair + 1) * LANES)
            state_buf[:, own] = (
                pair_columns(grown_last, pair) * state_buf[:, own] + fresh[:, own]
            )
        return carry

    lax.fori_loop(0, length // CHUNK, chunk, 0)


def mixer_backward_kernel(
    mix_ref,
    ssm_ref,
    states_ref,
    shared_ref,
    step_ref,
    conv_inner_ref,
    conv_shared_ref,
    head_ref,
    skip_ref,
    gain_ref,
    lanes_ref,
    grad_ref,
    group_factor_ref,
    group_scale_ref,
    factor_ref,
    query_grad_ref,
    mix_grad_ref,
    shared_grad_ref,
    step_grad_ref,
    inner_taps_ref,
    shared_taps_ref,
    head_grad_ref,
    wide_grad_ref,
    total_ref,
    taken_buf,
    inner_buf,
    maps_buf,
    step_buf,
    decay_buf,
    weighted_buf,
    grown_buf,
    inner_grad_buf,
    maps_grad_buf,
    sums_buf,
    state_grad_buf,
):
    pairs = ssm_ref.shape[1] // LANES
    length = ssm_ref.shape[0]
    group_pairs = pairs // (grad_ref.shape[1] // (pairs * LANES // 2 + HD))
    low = low_lanes()
    mix_grad_ref[:, 2 * pairs * LANES :] = query_grad_ref[...]
    for pair in range(pairs):
        first = slice(2 * pair * LANES, (2 * pair + 1) * LANES)
        second = slice((2 * pair + 1) * LANES, (2 * pair + 2) * LANES)
        own = slice(pair * LANES, (pair + 1) * LANES)
        taken = jnp.where(low, pltpu.roll(mix_ref[:, first], PM, 1), mix_ref[:, second])
        taken_buf[:, own] = taken
        taken = conv(taken, conv_inner_ref[:, own])
        inner_buf[:, own] = taken * sigmoid(taken)
    for block in range(shared_ref.shape[1] // LANES):
        own = slice(block * LANES, (block + 1) * LANES)
        taken = conv(shared_ref[:, own], conv_shared_ref[:, own])
        maps_buf[:, own] = (taken * sigmoid(taken)).astype(bf16)
    shifted = step_ref[...] + head_ref[1:2, :]
    steps = softplus(shifted)
    rate = -jnp.exp(head_ref[0:1, :])
    step_buf[...] = steps
    decay_buf[...] = rate * steps
    state_grad_buf[...] = jnp.zeros_like(state_grad_buf)
    head_grad_ref[...] = jnp.zeros_like(head_grad_ref)
    wide_grad_ref[...] = jnp.zeros_like(wide_grad_ref)
    mask = lower_mask()
    chunks = length // CHUNK
    lane_index = lax.broadcasted_iota(jnp.int32, (1, LANES), 1)

    def chunk(turn, carry):
        index = chunks - 1 - turn
        rows = pl.ds(pl.multiple_of(index * CHUNK, CHUNK), CHUNK)
        running = jnp.dot(mask, decay_buf[rows, :], precision=highest, preferred_element_type=f32)
        running_t = running.T
        step = step_buf[rows, :]
        step_t = step.T
        last = running[CHUNK - 1 : CHUNK, :]
        grown = jnp.exp(running)
        fading = jnp.exp(last - running)
        grown_last = jnp.exp(last)
        basis = maps_buf[rows, 0:NS]
        read = maps_buf[rows, NS : 2 * NS]
        gram = product_back(read, basis)
        state_low = states_ref[pl.ds(pl.multiple_of(index * NS, NS), NS), :]
        carried = product(read, state_low)
        state_grad_low = state_grad_buf[...].astype(bf16)
        weighted_grad = product(basis, state_grad_low)
        gram_grad = jnp.zeros((CHUNK, CHUNK), f32)
        decay_grad = jnp.zeros((CHUNK, LANES), f32)
        column_grads = []
        total = jnp.zeros((CHUNK, 1), f32)
        group_factor = group_factor_ref[rows, :]
        group_scale = group_scale_ref[rows, :]
        factor = factor_ref[rows, :]
        for pair in range(pairs):
            first = slice(2 * pair * LANES, (2 * pair + 1) * LANES)
            second = slice((2 * pair + 1) * LANES, (2 * pair + 2) * LANES)
            own = slice(pair * LANES, (pair + 1) * LANES)
            place = pair * LANES + (pair // group_pairs) * HD
            incoming = grad_ref[rows, place : place + LANES]
            head_a = mix_ref[rows, first]
            head_b = mix_ref[rows, second]
            gate = jnp.where(low, head_a, pltpu.roll(head_b, PM, 1))
            gate_sigmoid = sigmoid(gate)
            gate_act = gate * gate_sigmoid
            ssm = ssm_ref[rows, own]
            gated = ssm * gate_act
            wide_grad_ref[0:1, own] += jnp.sum(
                incoming * gated * group_factor, axis=0, keepdims=True
            )
            gated_grad = group_factor * gain_ref[:, own] * incoming - gated * group_scale
            gate_grad = gated_grad * ssm * gate_sigmoid * (1.0 + gate * (1.0 - gate_sigmoid))
            ssm_grad = gated_grad * gate_act
            inner = inner_buf[rows, own]
            wide_grad_ref[1:2, own] += jnp.sum(ssm_grad * inner, axis=0, keepdims=True)
            gate_b = pltpu.roll(gate_grad, PM, 1)
            total = total + jnp.sum(gate_grad * gate, axis=1, keepdims=True)
            mix_grad_ref[rows, first] = jnp.where(low, gate_grad * factor, 0.0).astype(bf16)
            mix_grad_ref[rows, second] = jnp.where(low, gate_b * factor, 0.0).astype(bf16)
            grad_low = ssm_grad.astype(bf16)
            mixing_grad = product_back(grad_low, stacked_pair(inner))
            spreads = []
            for side, head in enumerate((2 * pair, 2 * pair + 1)):
                spread = mask * jnp.exp(
                    jnp.minimum(running[:, head : head + 1] - running_t[head : head + 1, :], 0.0)
                )
                step_row = step_t[head : head + 1, :]
                spread_gram = gram * spread
                spreads.append(spread_gram.astype(bf16))
                own_grad = mixing_grad[:, side * CHUNK : (side + 1) * CHUNK] * step_row
                gram_grad = gram_grad + own_grad * spread
                moved = own_grad * spread_gram
                decay_grad = decay_grad + jnp.where(
                    lane_index == head, jnp.sum(moved, axis=1, keepdims=True), 0.0
                )
                column_grads.append(jnp.sum(moved, axis=0, keepdims=True))
            within = outer_sum(jnp.concatenate(spreads, axis=0), stacked_pair(ssm_grad))
            fading_grad = pair_columns(fading, pair) * weighted_grad[:, own]
            spread_grad = within + fading_grad
            step_wide = pair_columns(step, pair)
            inner_grad_buf[rows, own] = step_wide * spread_grad + skip_ref[:, own] * ssm_grad
            grown_grad = pair_columns(grown, pair) * ssm_grad
            grown_buf[:, own] = grown_grad.astype(bf16)
            weighted_buf[:, own] = (pair_columns(fading, pair) * step_wide * inner).astype(bf16)
            sums_buf[0:CHUNK, own] = (inner * spread_grad).astype(bf16)
            sums_buf[CHUNK : 2 * CHUNK, own] = (inner * fading_grad * step_wide).astype(bf16)
            sums_buf[2 * CHUNK : 3 * CHUNK, own] = (grown_grad * carried[:, own]).astype(bf16)
        head_sums = product(sums_buf[...], lanes_ref[...])
        step_part = head_sums[0:CHUNK, :]
        fading_part = head_sums[CHUNK : 2 * CHUNK, :]
        grown_part = head_sums[2 * CHUNK : 3 * CHUNK, :]
        fill = jnp.zeros((CHUNK - len(column_grads), CHUNK), f32)
        column_grad = jnp.concatenate(column_grads + [fill], axis=0).T
        decay_grad = decay_grad - column_grad + grown_part - fading_part
        state_part = jnp.zeros((1, LANES), f32)
        grown_low = grown_buf[...]
        fresh = outer_sum(read, grown_low)
        for pair in range(pairs):
            own = slice(pair * LANES, (pair + 1) * LANES)
            state_grad = state_grad_buf[:, own]
            held = jnp.sum(state_grad * state_low[:, own].astype(f32), axis=0, keepdims=True)
            for side, head in enumerate((2 * pair, 2 * pair + 1)):
                kept = jnp.where(low if side == 0 else jnp.logical_not(low), held, 0.0)
                state_part = state_part + jnp.where(
                    lane_index == head, jnp.sum(kept, axis=1, keepdims=True), 0.0
                )
            state_grad_buf[:, own] = pair_columns(grown_last, pair) * state_grad + fresh[:, own]
        last_grad = jnp.sum(fading_part, axis=0, keepdims=True) + grown_last * state_part
        decay_sum = (
            lax.dot_general(
                mask,
                decay_grad,
                (((0,), (0,)), ((), ())),
                precision=highest,
                preferred_element_type=f32,
            )
            + last_grad
        )
        raw_shift = step_ref[rows, :] + head_ref[1:2, :]
        raw_grad = (step_part + decay_sum * rate) * sigmoid(raw_shift)
        head_grad_ref[0:1, :] += jnp.sum(decay_sum * decay_buf[rows, :], axis=0, keepdims=True)
        head_grad_ref[1:2, :] += jnp.sum(raw_grad, axis=0, keepdims=True)
        step_grad_ref[rows, :] = (raw_grad * factor).astype(bf16)
        total = total + jnp.sum(raw_grad * step_ref[rows, :], axis=1, keepdims=True)
        total_ref[rows, :] = total
        gram_low = gram_grad.astype(bf16)
        maps_grad_buf[rows, 0:NS] = outer_sum(gram_low, read) + product_back(
            weighted_buf[...], state_grad_low
        )
        maps_grad_buf[rows, NS : 2 * NS] = product(gram_low, basis) + product_back(
            grown_low, state_low
        )
        return carry

    lax.fori_loop(0, chunks, chunk, 0)
    factor = factor_ref[...]
    total = total_ref[...]
    for pair in range(pairs):
        first = slice(2 * pair * LANES, (2 * pair + 1) * LANES)
        second = slice((2 * pair + 1) * LANES, (2 * pair + 2) * LANES)
        own = slice(pair * LANES, (pair + 1) * LANES)
        taken = taken_buf[:, own]
        taps = conv_inner_ref[:, own]
        before = conv(taken, taps)
        before_sigmoid = sigmoid(before)
        grad = inner_grad_buf[:, own] * before_sigmoid * (1.0 + before * (1.0 - before_sigmoid))
        grad, tap_grads = conv_back(grad, taken, taps)
        for tap, tap_grad in enumerate(tap_grads):
            inner_taps_ref[tap : tap + 1, own] = tap_grad
        total = total + jnp.sum(grad * taken, axis=1, keepdims=True)
        grad = grad * factor
        low_a = mix_grad_ref[:, first].astype(f32)
        low_b = mix_grad_ref[:, second].astype(f32)
        mix_grad_ref[:, first] = jnp.where(low, low_a, pltpu.roll(grad, PM, 1)).astype(bf16)
        mix_grad_ref[:, second] = jnp.where(low, low_b, grad).astype(bf16)
    for block in range(shared_ref.shape[1] // LANES):
        own = slice(block * LANES, (block + 1) * LANES)
        taken = shared_ref[:, own]
        taps = conv_shared_ref[:, own]
        before = conv(taken, taps)
        before_sigmoid = sigmoid(before)
        grad = maps_grad_buf[:, own] * before_sigmoid * (1.0 + before * (1.0 - before_sigmoid))
        grad, tap_grads = conv_back(grad, taken, taps)
        for tap, tap_grad in enumerate(tap_grads):
            shared_taps_ref[tap : tap + 1, own] = tap_grad
        total = total + jnp.sum(grad * taken, axis=1, keepdims=True)
        shared_grad_ref[:, own] = (grad * factor).astype(bf16)
    total_ref[...] = total


def call(kernel, outs, scratch, flops, *operands):
    return pl.pallas_call(
        kernel,
        out_shape=outs,
        in_specs=[pl.BlockSpec(memory_space=pltpu.VMEM)] * len(operands),
        out_specs=[pl.BlockSpec(memory_space=pltpu.VMEM)] * len(outs),
        scratch_shapes=scratch,
        compiler_params=pltpu.CompilerParams(vmem_limit_bytes=VMEM_LIMIT),
        cost_estimate=pl.CostEstimate(flops=flops, bytes_accessed=10**6, transcendentals=0),
    )(*operands)


def shape(dims, dtype=f32):
    return jax.ShapeDtypeStruct(dims, dtype)


def mixer_forward(
    own, other, factor, shared, step, taps, shared_taps, heads, skip, gain, attended
):
    length, width = own.shape
    channels = width // 2
    chunks = length // CHUNK
    return call(
        mixer_forward_kernel,
        [
            shape((length, channels + attended.shape[1]), bf16),
            shape((length, 1)),
            shape((length, width)),
            shape((length, channels)),
            shape((chunks * NS, channels), bf16),
        ],
        [
            pltpu.VMEM((length, channels), f32),
            pltpu.VMEM((length, channels), f32),
            pltpu.VMEM((length, 2 * NS), bf16),
            pltpu.VMEM((length, LANES), f32),
            pltpu.VMEM((length, LANES), f32),
            pltpu.VMEM((CHUNK, channels), bf16),
            pltpu.VMEM((NS, channels), f32),
        ],
        10**8,
        own, other, factor, shared, step, taps, shared_taps, heads, skip, gain, attended,
    )


def mixer_backward(
    mix, ssm, states, shared, step, taps, shared_taps, heads, skip, gain, lanes, grad,
    group_factor, group_scale, factor, query_grad,
):
    length, width = mix.shape
    channels = width // 2
    return call(
        mixer_backward_kernel,
        [
            shape((length, width + query_grad.shape[1]), bf16),
            shape((length, 2 * NS), bf16),
            shape((length, LANES), bf16),
            shape((taps.shape[0], channels)),
            shape((taps.shape[0], 2 * NS)),
            shape((8, LANES)),
            shape((8, channels)),
            shape((length, 1)),
        ],
        [
            pltpu.VMEM((length, channels), f32),
            pltpu.VMEM((length, channels), f32),
            pltpu.VMEM((length, 2 * NS), bf16),
            pltpu.VMEM((length, LANES), f32),
            pltpu.VMEM((length, LANES), f32),
            pltpu.VMEM((CHUNK, channels), bf16),
            pltpu.VMEM((CHUNK, channels), bf16),
            pltpu.VMEM((length, channels), f32),
            pltpu.VMEM((length, 2 * NS), f32),
            pltpu.VMEM((3 * CHUNK, channels), bf16),
            pltpu.VMEM((NS, channels), f32),
        ],
        10**8,
        mix, ssm, states, shared, step, taps, shared_taps, heads, skip, gain, lanes, grad,
        group_factor, group_scale, factor, query_grad,
    )


def rotated(values_in, cosine, sine):
    return values_in * cosine + pltpu.roll(values_in, HD // 2, 1) * sine


def rotated_back(grad, cosine, sine):
    return grad * cosine + pltpu.roll(grad * sine, HD // 2, 1)


def attention_forward_kernel(query_ref, pair_ref, cosine_ref, sine_ref, out_ref):
    length = query_ref.shape[0]
    scale = 1.0 / math.sqrt(HD)
    block = min(256, length)
    keys = rotated(pair_ref[:, :HD], cosine_ref[...], sine_ref[...]).astype(bf16)
    vals = pair_ref[:, HD:].astype(bf16)
    for head in range(query_ref.shape[1] // HD):
        lanes = slice(head * HD, (head + 1) * HD)
        queries = rotated(query_ref[:, lanes], cosine_ref[...], sine_ref[...]).astype(bf16)
        for start in range(0, length, block):
            end = start + block
            scores = product_back(queries[start:end], keys[:end]) * scale
            rows = start + lax.broadcasted_iota(jnp.int32, (block, end), 0)
            columns = lax.broadcasted_iota(jnp.int32, (block, end), 1)
            scores = jnp.where(columns <= rows, scores, -1e30)
            exponent = jnp.exp(scores - jnp.max(scores, axis=1, keepdims=True))
            probs = exponent * (1.0 / jnp.sum(exponent, axis=1, keepdims=True))
            out_ref[start:end, lanes] = product(probs.astype(bf16), vals[:end]).astype(bf16)


def attention_backward_kernel(
    query_ref, pair_ref, cosine_ref, sine_ref, grad_ref, factor_ref,
    query_grad_ref, pair_grad_ref, total_ref, key_buf, val_buf,
):
    length = query_ref.shape[0]
    scale = 1.0 / math.sqrt(HD)
    block = min(256, length)
    cosine, sine = cosine_ref[...], sine_ref[...]
    keys = rotated(pair_ref[:, :HD], cosine, sine).astype(bf16)
    vals = pair_ref[:, HD:].astype(bf16)
    heads = query_ref.shape[1] // HD
    group = grad_ref.shape[1] // heads
    key_buf[...] = jnp.zeros_like(key_buf)
    val_buf[...] = jnp.zeros_like(val_buf)
    for head in range(heads):
        lanes = slice(head * HD, (head + 1) * HD)
        queries = rotated(query_ref[:, lanes], cosine, sine).astype(bf16)
        incoming = grad_ref[:, (head + 1) * group - HD : (head + 1) * group].astype(bf16)
        for start in range(0, length, block):
            end = start + block
            scores = product_back(queries[start:end], keys[:end]) * scale
            rows = start + lax.broadcasted_iota(jnp.int32, (block, end), 0)
            columns = lax.broadcasted_iota(jnp.int32, (block, end), 1)
            scores = jnp.where(columns <= rows, scores, -1e30)
            exponent = jnp.exp(scores - jnp.max(scores, axis=1, keepdims=True))
            probs = exponent * (1.0 / jnp.sum(exponent, axis=1, keepdims=True))
            grad_low = incoming[start:end]
            val_buf[:end, :] += outer_sum(probs.astype(bf16), grad_low)
            probs_grad = product_back(grad_low, vals[:end])
            inner = jnp.sum(probs * probs_grad, axis=1, keepdims=True)
            scores_grad = (probs * (probs_grad - inner) * scale).astype(bf16)
            query_grad = rotated_back(
                product(scores_grad, keys[:end]), cosine[start:end], sine[start:end]
            )
            key_buf[:end, :] += outer_sum(scores_grad, queries[start:end])
            taken = query_ref[start:end, lanes]
            part = jnp.sum(query_grad * taken, axis=1, keepdims=True)
            if head == 0:
                total_ref[start:end, :] = part
            else:
                total_ref[start:end, :] += part
            query_grad_ref[start:end, lanes] = (query_grad * factor_ref[start:end, :]).astype(bf16)
    key_grad = rotated_back(key_buf[...], cosine, sine)
    val_grad = val_buf[...]
    total_ref[...] += jnp.sum(
        key_grad * pair_ref[:, :HD] + val_grad * pair_ref[:, HD:], axis=1, keepdims=True
    )
    pair_grad_ref[:, :HD] = (key_grad * factor_ref[...]).astype(bf16)
    pair_grad_ref[:, HD:] = (val_grad * factor_ref[...]).astype(bf16)


def attention_forward(query, pair, cosine, sine):
    return call(
        attention_forward_kernel, [shape(query.shape, bf16)], [], 10**8,
        query, pair, cosine, sine,
    )[0]


def attention_backward(query, pair, cosine, sine, grad, factor):
    length = query.shape[0]
    return call(
        attention_backward_kernel,
        [shape(query.shape, bf16), shape(pair.shape, bf16), shape((length, 1))],
        [pltpu.VMEM((length, HD), f32), pltpu.VMEM((length, HD), f32)],
        10**8,
        query, pair, cosine, sine, grad, factor,
    )


def rope_tables(length):
    half = HD // 2
    inverse = rope_base ** (-jnp.arange(half, dtype=f32) * 2.0 / HD)
    angles = jnp.arange(length, dtype=f32)[:, None] * inverse[None, :]
    cosine, sine = jnp.cos(angles), jnp.sin(angles)
    return jnp.concatenate([cosine, cosine], axis=1), jnp.concatenate([-sine, sine], axis=1)


def to_lanes(values_in):
    return jnp.pad(values_in, ((0, 0), (0, LANES - values_in.shape[1])))


def local(
    tokens,
    norm_first,
    mixer_in,
    query_weight,
    bc_weight,
    step_weight,
    kv_weight,
    conv_inner,
    conv_shared,
    log_rate,
    step_bias,
    skip_gain,
    group_gain,
    out_weight,
    norm_second,
    gate_weight,
    up_weight,
    down_weight,
    cotangent,
):
    length = tokens.shape[0]
    row = lax.axis_index("row")
    col = lax.axis_index("col")
    me = lax.axis_index("dp")
    count = lax.axis_size("dp")
    near = me % 2
    quarter = col * 2 + row
    head_count = log_rate.shape[0]
    channels = group_gain.shape[0]
    kv_flat = kv_weight.reshape(kv_weight.shape[0], -1)
    residual = tokens.astype(f32)
    spine = Spine(jnp.zeros((1, LANES), f32))

    def column_share(weight):
        rows, columns = weight.shape[0] // count, weight.shape[1] // 2
        return lax.dynamic_slice(weight, (me * rows, (1 - row) * columns), (rows, columns))

    half_rows = out_weight.shape[0] // 2
    share_rows = half_rows // count
    out_own = part_of(out_weight, row, 0)
    gate_own, up_own = part_of(gate_weight, row, 1), part_of(up_weight, row, 1)
    out_share = lax.dynamic_slice_in_dim(
        out_weight, (1 - row) * half_rows + me * share_rows, share_rows, 0
    )
    ffn_share = jnp.concatenate([column_share(gate_weight), column_share(up_weight)], axis=1)
    out_share, ffn_share, residual = tie(out_share, ffn_share, residual)
    out_spread = Spread(swap(out_share, "row"))
    ffn_spread = Spread(swap(ffn_share, "row"))

    first_own = (residual * norm_first).astype(bf16)
    first_half = in_order(first_own, swap(first_own, "col"), col, 1)
    square_first = jnp.sum(residual * residual, axis=1)
    square_first = square_first + swap(square_first, "col")
    square_far = swap(square_first, "row")
    query_own = product(first_half, part_of(query_weight, row, 1))
    query_out = product(first_half, part_of(query_weight, 1 - row, 1)).astype(bf16)
    pair_own = product(first_half, kv_flat)
    shared_own = product(first_half, bc_weight)
    step_own = product(first_half, step_weight)
    query_width = query_own.shape[1]
    pair_width = pair_own.shape[1]
    shared_width = shared_own.shape[1]
    early = swap(
        jnp.concatenate(
            [
                query_out,
                pair_own.astype(bf16),
                part_of(shared_own, col, 1).astype(bf16),
                to_lanes(step_own).astype(bf16),
            ],
            axis=1,
        ),
        "row",
    )
    mix_out = product(first_half, part_of(mixer_in, 1 - row, 1)).astype(bf16)
    mix_own = product(first_half, part_of(mixer_in, row, 1))
    cot_near = swap_dp(cotangent, 1)
    cot_half = in_order(cotangent, swap(cotangent, "col"), col, 1)
    hidden_back = product_back(cot_half, part_of(down_weight, 1 - row, 0)).astype(bf16)
    hidden_back_own = product_back(cot_half, part_of(down_weight, row, 0))

    out_spread.wait(spine)
    out_spread.level()
    ffn_spread.wait(spine)
    ffn_spread.level()
    cot_near, early, square_far, mix_out = spine.wait(cot_near, early, square_far, mix_out)
    mix_other = swap(mix_out, "row")
    out_spread.wait(spine)
    out_spread.level()
    first_factor = lax.rsqrt((square_first + square_far) / D + norm_epsilon)
    first_column = first_factor[:, None]
    query_sum = (query_own + early[:, :query_width].astype(f32)) * first_column
    place = query_width
    pair_sum = (pair_own + early[:, place : place + pair_width].astype(f32)) * first_column
    place += pair_width
    shared_sum = (
        part_of(shared_own, col, 1) + early[:, place : place + shared_width // 2].astype(f32)
    ) * first_column
    shared_sum = in_order(
        shared_sum, swap(shared_sum.astype(bf16), "col").astype(f32), col, 1
    )
    place += shared_width // 2
    step_sum = (
        step_own + early[:, place : place + step_own.shape[1]].astype(f32)
    ) * first_column
    step_sum = to_lanes(lax.dynamic_slice_in_dim(step_sum, quarter * head_count, head_count, 1))
    ffn_spread.wait(spine)
    ffn_spread.level()
    cosine, sine = rope_tables(length)
    attended = attention_forward(query_sum, pair_sum, cosine, sine)
    heads = to_lanes(jnp.stack([log_rate, step_bias] + [jnp.zeros_like(log_rate)] * 6))
    skip_wide = jnp.repeat(skip_gain, PM)[None, :]
    gain_wide = group_gain[None, :]
    out_spread.wait(spine)
    out_spread.level()
    out_other = out_spread.finish(spine)
    mix_other, hidden_back, attended, shared_sum, step_sum = spine.wait(
        mix_other, hidden_back, attended, shared_sum, step_sum
    )
    hidden_back = swap(hidden_back, "row")
    mixed_raw, square, mix_sum, ssm, states = mixer_forward(
        mix_own, mix_other, first_column, shared_sum, step_sum, conv_inner, conv_shared,
        heads, skip_wide, gain_wide, attended,
    )
    square, hidden_back = spine.wait(square, hidden_back)
    square_total = square[:, 0] + swap(square[:, 0], "col")
    square_far = swap(square_total, "row")
    ffn_spread.wait(spine)
    ffn_spread.level()
    square_far = spine.wait(square_far)
    group_factor = lax.rsqrt((square_total + square_far) / (HM * PM) + norm_epsilon)
    groups = attended.shape[1] // HD
    group_width = mixed_raw.shape[1] // groups
    is_normed = jnp.arange(mixed_raw.shape[1])[None, :] % group_width < group_width - HD
    mixed = (
        mixed_raw.astype(f32) * jnp.where(is_normed, group_factor[:, None], 1.0)
    ).astype(bf16)

    out_far = sum_cols(product(mixed, out_other), col)
    out_far = swap(out_far.astype(bf16), "row")
    out_near = sum_cols(product(mixed, out_own), col)
    ffn_other = ffn_spread.finish(spine)
    out_far = spine.wait(out_far)
    second = residual + out_near + out_far.astype(f32)
    second_own = (second * norm_second).astype(bf16)
    second_far = swap(second_own, "row")
    second_half = in_order(second_own, swap(second_own, "col"), col, 1)
    second_near = swap_dp(second_own, 1)
    second_square = jnp.sum(second * second, axis=1)
    second_square = second_square + swap(second_square, "col")
    second_square_far = swap(second_square, "row")
    gate_width = gate_own.shape[1]
    gate_part, up_part = product(second_half, gate_own), product(second_half, up_own)
    second_far, second_near, first_send = spine.wait(second_far, second_near, first_own)
    second_far_near = swap_dp(second_far, 1)
    first_row = swap(first_send, "row")
    first_near = swap_dp(first_send, 1)
    second_far = in_order(second_far, swap(second_far, "col"), col, 1)
    second_near = in_order(second_near, swap(second_near, "col"), col, 1)
    second_factor = lax.rsqrt((second_square + second_square_far) / D + norm_epsilon)
    second_column = second_factor[:, None]
    gate_sum = (gate_part + product(second_far, ffn_other[:, :gate_width])) * second_column
    up_sum = (up_part + product(second_far, ffn_other[:, gate_width:])) * second_column
    gate_sigmoid = jax.nn.sigmoid(gate_sum)
    gate_act = gate_sum * gate_sigmoid
    hidden_grad = hidden_back_own + hidden_back.astype(f32)
    gate_grad = hidden_grad * up_sum * gate_sigmoid * (1.0 + gate_sum * (1.0 - gate_sigmoid))
    up_grad = hidden_grad * gate_act
    hidden = (gate_act * up_sum).astype(bf16)
    ffn_grad = jnp.concatenate(
        [(gate_grad * second_column).astype(bf16), (up_grad * second_column).astype(bf16)], axis=1
    )
    second_total = jnp.sum(gate_grad * gate_sum + up_grad * up_sum, axis=1)
    second_total = second_total + swap(second_total, "col")
    second_total_far = swap(second_total, "row")
    ffn_send = swap_dp(part_of(ffn_grad, 1 - near, 1), 1)
    back_far = sum_cols(product_back(ffn_grad, ffn_other), col).astype(bf16)
    second_far_near = spine.wait(second_far_near)
    second_far_near = in_order(second_far_near, swap(second_far_near, "col"), col, 1)
    second_total_far, back_far, first_row, first_near = spine.wait(
        second_total_far, back_far, first_row, first_near
    )
    back_far = swap(back_far, "row")
    back_near = sum_cols(
        product_back(ffn_grad[:, :gate_width], gate_own)
        + product_back(ffn_grad[:, gate_width:], up_own),
        col,
    )
    first_pair_col = swap(jnp.concatenate([first_row, first_near], axis=1), "col")
    size = first_row.shape[1]
    first_far = in_order(first_row, first_pair_col[:, :size], col, 1)
    first_near = in_order(first_near, first_pair_col[:, size:], col, 1)
    back_far, ffn_send, first_far, first_near = spine.wait(
        back_far, ffn_send, first_far, first_near
    )
    second_in_grad = back_near + back_far.astype(f32)
    second_grad = (
        cotangent.astype(f32)
        + norm_second * second_in_grad
        - second * (second_factor**2 * (second_total + second_total_far) / D)[:, None]
    )
    norm_second_grad = jnp.sum(second_in_grad * second, axis=0)
    branch = second_grad.astype(bf16)
    branch_far = swap(branch, "row")
    branch_half = in_order(branch, swap(branch, "col"), col, 1)

    def both_halves(scattered, sent):
        kept = lax.dynamic_index_in_dim(scattered, near, 0, keepdims=False)
        return jnp.where(near == 0, kept, sent), jnp.where(near == 0, sent, kept)

    def to_neighbour(scattered):
        return swap_dp(lax.dynamic_index_in_dim(scattered, 1 - near, 0, keepdims=False), 1)

    branch_half = spine.wait(branch_half)
    ffn_kept = part_of(ffn_grad, near, 1)
    blocks = count // 2
    ffn_sums = call(
        both_rows_kernel,
        [shape((blocks, 2, second_half.shape[1] // blocks, ffn_kept.shape[1]), bf16)],
        [pltpu.VMEM((second_half.shape[1], ffn_kept.shape[1]), f32)],
        10**6,
        second_half, second_far, second_near, second_far_near, ffn_kept, ffn_send,
    )[0]
    ffn_sums = spine.wait(ffn_sums)
    ffn_sums = far_sum(ffn_sums.reshape(-1, ffn_kept.shape[1]))
    mixed_send, hidden_send = spine.wait(mixed, hidden)
    near_pack = jnp.concatenate(
        [
            near_blocks(mixed_send, 1 - near),
            branch,
            near_blocks(hidden_send, 1 - near),
            first_row,
        ],
        axis=1,
    )
    near_pack = swap_dp(near_pack, 1)
    branch_far = spine.wait(branch_far)
    branch_far = in_order(branch_far, swap(branch_far, "col"), col, 1)
    mixed_grad = product_back(branch_half, out_own) + product_back(branch_far, out_other)

    group_total = jnp.sum(jnp.where(is_normed, mixed_grad * mixed.astype(f32), 0.0), axis=1)
    group_total = group_total + swap(group_total, "col")
    group_total_far = swap(group_total, "row")
    query_grad, pair_grad, attention_total = attention_backward(
        query_sum, pair_sum, cosine, sine, mixed_grad, first_column
    )
    group_total_far, attention_total = spine.wait(group_total_far, attention_total)
    group_scale = group_factor**2 * (group_total + group_total_far) / (HM * PM)

    def piece(pack, turn):
        return pack[:, turn * size : (turn + 1) * size]

    group_scale, mixed_kept = spine.wait(group_scale, near_blocks(mixed, near))
    mixed_kept_far = swap(mixed_kept, "row")
    lanes = (
        jnp.arange(channels)[:, None] // PM == jnp.arange(LANES)[None, :]
    ).astype(bf16)
    (
        own_grads,
        shared_grad,
        step_grad,
        conv_inner_grad,
        conv_shared_part,
        head_grads,
        wide_grads,
        mixer_total,
    ) = mixer_backward(
        mix_sum, ssm, states, shared_sum, step_sum, conv_inner, conv_shared, heads, skip_wide,
        gain_wide, lanes, mixed_grad, group_factor[:, None], group_scale[:, None], first_column,
        query_grad,
    )
    mixed_kept_far = spine.wait(mixed_kept_far)
    own_grads, shared_grad, near_pack = spine.wait(own_grads, shared_grad, near_pack)
    mix_width = mix_sum.shape[1]
    grads_send = swap_dp(part_of(own_grads, 1 - near, 1), 1)
    grads_kept = part_of(own_grads, near, 1)
    shared_low = (shared_grad.astype(f32) + swap(shared_grad, "col").astype(f32)).astype(bf16)
    late = jnp.concatenate([part_of(shared_low, col, 1), pair_grad, step_grad], axis=1)
    late_far = swap(late, "row")
    first_far_near = piece(near_pack, 3)
    first_far_near = in_order(first_far_near, swap(first_far_near, "col"), col, 1)
    grads_send, mixed_send, hidden_send = spine.wait(
        grads_send, piece(near_pack, 0), piece(near_pack, 2)
    )
    near_far = swap(jnp.concatenate([mixed_send, hidden_send], axis=1), "row")
    mixer_scatter_far = Scatter(
        spine,
        (outer_sum(first_far, grads_kept) + outer_sum(first_far_near, grads_send)).astype(bf16),
        True,
    )
    late_far = spine.wait(late_far)
    half = shared_width // 2
    late_sum = (
        late[:, : half + pair_width].astype(f32) + late_far[:, : half + pair_width].astype(f32)
    ).astype(bf16)
    shared_part, pair_low = late_sum[:, :half], late_sum[:, half:]
    step_two = in_order(
        late[:, half + pair_width :][:, :head_count],
        late_far[:, half + pair_width :][:, :head_count],
        row,
        1,
    )
    step_all = in_order(step_two, swap(step_two, "col"), col, 1)
    rest = jnp.concatenate(
        [pair_low, shared_part, to_lanes(step_all), jnp.zeros((length, LANES), bf16)], axis=1
    )
    rest_send = swap_dp(part_of(rest, 1 - near, 1), 1)
    rest_send = spine.wait(rest_send)
    mixer_scatter = Scatter(
        spine,
        (
            outer_sum(
                first_half, jnp.concatenate([grads_kept, part_of(rest, near, 1)], axis=1)
            )
            + outer_sum(first_near, jnp.concatenate([grads_send, rest_send], axis=1))
        ).astype(bf16),
        True,
    )
    near_far, mixer_scatter.parts, hidden_send, ffn_sums = spine.wait(
        near_far, mixer_scatter.parts, hidden, ffn_sums
    )
    hidden_far = swap(hidden_send, "row")
    mixed_kept = in_order(mixed_kept, mixed_kept_far, row, 1)
    mixed_near = in_order(piece(near_pack, 0), piece(near_far, 0), row, 1)
    branch_near = in_order(piece(near_pack, 1), swap(piece(near_pack, 1), "col"), col, 1)
    out_sums = far_sum(
        spine.wait(
            (
                outer_sum(mixed_kept, branch_half) + outer_sum(mixed_near, branch_near)
            ).astype(bf16)
        )
    )
    ffn_sums = ffn_sums.reshape(2, 2, -1, ffn_kept.shape[1])
    ffn_sent = swap_dp(lax.dynamic_index_in_dim(ffn_sums, 1 - near, 1, keepdims=False), 1)
    mixer_scatter_far.add()
    hidden_far, grads_again = spine.wait(hidden_far, own_grads)
    own_grads_far = swap(grads_again, "row")
    hidden_half = in_order(hidden, hidden_far, row, 1)
    hidden_near = in_order(piece(near_pack, 2), piece(near_far, 1), row, 1)
    cot_near = in_order(cot_near, swap(cot_near, "col"), col, 1)
    down_sums = far_sum(
        spine.wait(
            (
                outer_sum(near_blocks(hidden_half, near), cot_half)
                + outer_sum(hidden_near, cot_near)
            ).astype(bf16)
        )
    )
    ffn_sent, layer_half = spine.wait(ffn_sent, hidden_half)
    ffn_near = both_halves(ffn_sums[0], ffn_sent[0])
    ffn_far = swap(jnp.stack(both_halves(ffn_sums[1], ffn_sent[1])), "row")
    mixer_scatter.add()
    layer_out = (second + sum_cols(product(layer_half, down_weight), col)).astype(bf16)
    mixer_far = mixer_scatter_far.finish()
    mixer_far_sent = to_neighbour(mixer_far)
    first_total, conv_shared_part, own_grads_far = spine.wait(
        (attention_total + mixer_total)[:, 0], conv_shared_part, own_grads_far
    )
    first_total = first_total + swap(first_total, "col")
    first_total_far = swap(first_total, "row")
    conv_shared_sum = conv_shared_part + swap(conv_shared_part, "col")
    conv_shared_far = swap(conv_shared_sum, "row")
    mix_half = in_order(own_grads[:, :mix_width], own_grads_far[:, :mix_width], row, 1)
    query_half = in_order(own_grads[:, mix_width:], own_grads_far[:, mix_width:], row, 1)
    shared_low = in_order(shared_part, swap(shared_part, "col"), col, 1)
    first_in_partial = (
        product_back(mix_half, mixer_in)
        + product_back(query_half, query_weight)
        + product_back(pair_low, kv_flat)
        + 0.5 * (product_back(shared_low, bc_weight) + product_back(step_all, step_weight))
    )
    first_in_grad = sum_cols(first_in_partial, col)
    mixer_far_sent, first_total_far, conv_shared_far = spine.wait(
        mixer_far_sent, first_total_far, conv_shared_far
    )
    mixer_far = swap(jnp.concatenate(both_halves(mixer_far, mixer_far_sent), axis=1), "row")
    input_grad = (
        second_grad
        + norm_first * first_in_grad
        - residual * (first_factor**2 * (first_total + first_total_far) / D)[:, None]
    )
    norm_first_grad = jnp.sum(first_in_grad * residual, axis=0)
    conv_shared_sum = conv_shared_sum + conv_shared_far
    skip_grad = wide_grads[1].reshape(head_count, PM).sum(axis=1)
    pieces = [
        norm_first_grad,
        norm_second_grad,
        conv_inner_grad.reshape(-1),
        conv_shared_sum.reshape(-1),
        wide_grads[0],
        jnp.pad(head_grads[0, :head_count], (0, LANES - head_count)),
        jnp.pad(head_grads[1, :head_count], (0, LANES - head_count)),
        jnp.pad(skip_grad, (0, LANES - head_count)),
    ]
    small = jnp.concatenate(pieces).reshape(-1, LANES)
    bits = dp_bits()
    small_far = swap_dp(small, bits[0])
    ffn_far = spine.wait(ffn_far)
    gate_weight_grad = in_order(ffn_near[0], ffn_far[0], row, 1).astype(f32)
    up_weight_grad = in_order(ffn_near[1], ffn_far[1], row, 1).astype(f32)
    small = small + spine.wait(small_far)
    small_far = swap_dp(small, bits[1])
    out_weight_grad, down_weight_grad = spine.wait(out_sums, down_sums)
    mixer_near = mixer_scatter.finish()
    mixer_near_sent = to_neighbour(mixer_near)
    small_far, mixer_far = spine.wait(small_far, mixer_far)
    small = small + small_far
    small_far = swap_dp(small, bits[2])
    mixer_near_sent = spine.wait(mixer_near_sent)
    mixer_near = both_halves(mixer_near, mixer_near_sent)
    kept_width = grads_kept.shape[1]
    own_sums = jnp.concatenate([mixer_near[0][:, :kept_width], mixer_near[1][:, :kept_width]], axis=1)
    rest_sums = jnp.concatenate(
        [mixer_near[0][:, kept_width:], mixer_near[1][:, kept_width:]], axis=1
    ).astype(f32)
    mixer_in_grad = in_order(own_sums[:, :mix_width], mixer_far[:, :mix_width], row, 1).astype(f32)
    query_weight_grad = in_order(
        own_sums[:, mix_width:], mixer_far[:, mix_width:], row, 1
    ).astype(f32)
    kv_weight_grad = rest_sums[:, :pair_width].reshape((-1,) + kv_weight.shape[1:])
    place = pair_width
    bc_own = rest_sums[:, place : place + shared_width // 2].astype(bf16)
    bc_weight_grad = in_order(bc_own, swap(bc_own, "col"), col, 1).astype(f32)
    place += shared_width // 2
    step_weight_grad = rest_sums[:, place : place + step_weight.shape[1]]
    for bit in bits[3:]:
        small = small + spine.wait(small_far)
        small_far = swap_dp(small, bit)
    small = small + spine.wait(small_far)
    out_weight_grad, down_weight_grad = out_weight_grad.astype(f32), down_weight_grad.astype(f32)
    small = (small + spine.token).reshape(-1)
    sums, place = [], 0
    for piece in pieces:
        sums.append(small[place : place + piece.shape[0]])
        place += piece.shape[0]

    def own_block(values_in, axis):
        size = values_in.shape[axis] // count
        return lax.dynamic_slice_in_dim(values_in, me * size, size, axis)

    return (
        layer_out,
        input_grad,
        own_block(sums[0], 0),
        mixer_in_grad,
        query_weight_grad,
        bc_weight_grad,
        step_weight_grad,
        kv_weight_grad,
        own_block(sums[2].reshape(conv_inner.shape), 1),
        own_block(sums[3].reshape(conv_shared.shape), 1),
        sums[5][:head_count],
        sums[6][:head_count],
        sums[7][:head_count],
        own_block(sums[4], 0),
        out_weight_grad,
        own_block(sums[1], 0),
        gate_weight_grad,
        up_weight_grad,
        down_weight_grad,
    )


def solution(mesh):
    in_specs = (
        P("dp", ("row", "col")),
        P(("row", "col")),
        P("row", "col"),
        P("row", "col"),
        P("row", None),
        P("row", None),
        P("row", "col", None),
        P(None, ("col", "row")),
        P(),
        P(("col", "row")),
        P(("col", "row")),
        P(("col", "row")),
        P(("col", "row")),
        P("col", "row"),
        P(("row", "col")),
        P("row", "col"),
        P("row", "col"),
        P("col", "row"),
        P("dp", ("row", "col")),
    )
    out_specs = (
        P("dp", ("row", "col")),
        P("dp", ("row", "col")),
        P(("row", "col", "dp")),
        P(("row", "dp"), "col"),
        P(("row", "dp"), "col"),
        P(("row", "dp"), None),
        P(("row", "dp"), None),
        P(("row", "dp"), "col", None),
        P(None, ("col", "row", "dp")),
        P(None, "dp"),
        P(("col", "row")),
        P(("col", "row")),
        P(("col", "row")),
        P(("col", "row", "dp")),
        P(("col", "dp"), "row"),
        P(("row", "col", "dp")),
        P(("row", "dp"), "col"),
        P(("row", "dp"), "col"),
        P(("col", "dp"), "row"),
    )
    return jax.shard_map(local, mesh=mesh, in_specs=in_specs, out_specs=out_specs, check_vma=False)
```
